32 devices in a mesh: dp: 8 (over y, x, core), section: 4 (over z).
Axes of the slice: x: 2, y: 2, z: 4, core: 2. Of those that a mesh axis runs over, the one named last changes fastest.
Arguments:
- tokens: bfloat16 [3584, 768], P('dp'), may hold values from -6 to 6
- lengths: int32 [32, 4], P('dp'), may hold values from 1 to 84, 112 in all within a row
- section_weights: bfloat16 [4, 768, 9216], P('section'), may hold values from -2 to 2
- norm_gains: float32 [4, 2, 768], P('section'), may hold values from 0.5 to 1.5
- cotangent: bfloat16 [3584, 768], P('dp'), may hold values from -6 to 6
Outputs:
- section_out: bfloat16 [4, 3584, 768], P('section', 'dp')
- grad_weights: float32 [4, 768, 9216], P('section', 'dp')
- grad_gains: float32 [4, 2, 768], P('section', None, 'dp')
The draws below stay inside these ranges and needn't reach their ends.
Inputs may be any that keep to these rules, and one draw needn't show every extreme that they name: The lengths of each bucket sum to 112, and the largest of each bucket is exactly 84.
All inputs are finite; a program needn't handle non-finite values.
Results may differ from the reference program's by a relative error of at most 0.018.
Values may be sent and summed in bfloat16 or wider, within the bound.
No kernel may reach another device: no remote copies, remote signals or barrier semaphores. Data moves between devices by JAX's collectives and lax.ppermute only.
A program may use at most 256 MiB of HBM per device.

```python
import math
import jax
import jax.numpy as jnp
import numpy as np
from jax import lax

D = 768
H = 12
HD = 64
FF = 3072
SHARED = 6
ROWS = 112
SEQS = 4
LONGEST = 84
BUCKETS = 32
TOKENS = 3584


def draw_section_weights(key, part):
    key = jax.random.fold_in(key, 11)
    columns = jnp.arange(4 * D + 2 * FF)
    inner = D ** (-0.5)
    down_scale = 2.0 * FF ** (-0.5)
    fresh_width = D - SHARED * HD
    first_cols = jnp.where(columns < 3 * D, inner, jnp.where(columns < 4 * D, 5.0 * inner, jnp.where(columns < 4 * D + FF, inner, down_scale)))
    second_cols = jnp.where(columns < 2 * D + fresh_width, inner, jnp.where(columns < 3 * D + fresh_width, 5.0 * inner, inner))
    third_cols = jnp.where(columns < FF, inner, inner)
    fourth_cols = jnp.where(columns < FF, down_scale, inner)
    scales = jnp.stack([first_cols, second_cols, third_cols, fourth_cols]).astype(jnp.float32)
    base = jnp.clip(jax.random.normal(key, (4, D, 4 * D + 2 * FF), jnp.float32), -3.0, 3.0)
    return (base * scales[:, None, :]).astype(jnp.bfloat16)


def block_levels(rng, extent, split, least, high):
    def one(axis_at, blocks):
        steps = jax.random.uniform(jax.random.fold_in(jax.random.fold_in(rng, 6), axis_at), (blocks,), jnp.float32, least / len(split), high / len(split))
        return jnp.repeat(jnp.exp(steps), extent[axis_at] // blocks).reshape((-1,) + (1,) * (len(extent) - axis_at - 1))

    factor_of = one(*split[0])
    for cut in split[1:]:
        factor_of = factor_of * one(*cut)
    return factor_of


def profile(number_of, total, reach, lean):
    weights = [(1 << 20) // math.isqrt(rank ** lean) + 1 for rank in range(2, number_of + 1)]
    surplus, given = total - reach - (number_of - 1), [1] * (number_of - 1)
    while surplus > 0:
        free = [i for i in range(number_of - 1) if given[i] < reach]
        pool, remaining = sum([weights[i] for i in free]), surplus
        for i in free:
            addition = min(reach - given[i], max(1, remaining * weights[i] // pool), surplus)
            given[i] = given[i] + addition
            surplus = surplus - addition
    return np.array([reach] + given)


def ragged_sizes(own_key, count, total, most, slope):
    if count == 2:
        one = jax.random.randint(own_key, (), max(1, total - most), min(most, total - 1) + 1)
        return jnp.stack([one, total - one])
    sizes = jnp.asarray(profile(count, total, most, slope), jnp.int32)
    twos = (count - 1) // 2
    source_of, receiver = sizes[1:1 + 2 * twos:2], sizes[2:2 + 2 * twos:2]
    room = jnp.minimum(source_of - 1, most - receiver)
    moved = jax.random.randint(jax.random.fold_in(own_key, 1), (twos,), 0, 1 << 20) % (room + 1)
    sizes = sizes.at[1:1 + 2 * twos:2].set(source_of - moved).at[2:2 + 2 * twos:2].set(receiver + moved)
    return sizes[jax.random.permutation(jax.random.fold_in(own_key, 2), count)]


def centred(own_key, shape, scale, bound, shards=(), held_as=jnp.bfloat16):
    values = scale * jax.random.normal(own_key, shape, jnp.float32)
    if shards:
        values = values * block_levels(own_key, shape, shards, -0.22, 0.18)
    return jnp.clip(values, -bound, bound).astype(held_as)


def setup_inputs(seed: int = 0) -> dict:
    keys = jax.random.split(jax.random.key(seed), 6)
    return {
        "tokens": centred(keys[0], (TOKENS, D), 1.0, 6.0, ((0, 8),)),
        "lengths": jax.vmap(lambda own: ragged_sizes(own, SEQS, ROWS, LONGEST, 2))(jax.random.split(keys[1], BUCKETS)).reshape((BUCKETS, SEQS)).astype(jnp.int32),
        "section_weights": draw_section_weights(jax.random.fold_in(keys[5], 71), 0),
        "norm_gains": jnp.clip(1.0 + 0.1 * jax.random.normal(keys[3], (4, 2, D), jnp.float32), 0.5, 1.5),
        "cotangent": centred(keys[4], (TOKENS, D), 1.0, 6.0, ((0, 8),)),
    }


EPS = 1e-05
HIGH = lax.Precision.HIGHEST

@jax.custom_vjp
def low(v):
    return lax.optimization_barrier(v.astype(jnp.bfloat16)).astype(jnp.float32)

@jax.custom_vjp
def low_back(v):
    return v

def low_keep(v):
    return (low(v), None)

def low_pass(kept, grad):
    return (grad,)

def back_keep(v):
    return (v, None)

def back_low(kept, grad):
    return (low(grad),)
low.defvjp(low_keep, low_pass)
low_back.defvjp(back_keep, back_low)

def wire(values):
    return low(low_back(values))

def layer_norm(inputs, gain_vec):
    centre = lax.optimization_barrier(jnp.mean(inputs, axis=-1, keepdims=True))
    centered = inputs - centre
    spread = lax.rsqrt(lax.optimization_barrier(jnp.mean(centered * centered, axis=-1, keepdims=True)) + EPS)
    return centered * spread * gain_vec

def doc_mask(lengths, row_count):
    doc_ends = jnp.cumsum(lengths)
    places = jnp.arange(row_count, dtype=jnp.int32)
    doc_ids = lax.optimization_barrier(jnp.sum((places[:, None] >= doc_ends[None, :]).astype(jnp.int32), axis=1))
    return (doc_ids[:, None] == doc_ids[None, :]) & (places[None, :] <= places[:, None])

def product(left_op, right_op):
    return jnp.dot(left_op, right_op, precision=HIGH)

def attention(queries, key_rows, value_rows, allowed):
    row_count = queries.shape[0]
    query_heads = queries.reshape(row_count, H, HD)
    key_heads = key_rows.reshape(row_count, H, HD)
    value_heads = value_rows.reshape(row_count, H, HD)
    raw_scores = jnp.einsum('qhd,khd->hqk', query_heads, key_heads, precision=HIGH)
    scores = low_back(raw_scores * HD ** (-0.5))
    scores = jnp.where(allowed[None], scores, -1e+30)
    probabilities = low(jax.nn.softmax(scores, axis=-1))
    mixture = jnp.einsum('hqk,khd->qhd', probabilities, value_heads, precision=HIGH)
    return mixture.reshape(row_count, D)

def two_layers(weights, gain_table, inputs, lengths, probe_zero):
    allowed = doc_mask(lengths, ROWS)
    shared_width = SHARED * HD
    fresh_width = D - shared_width
    first_block = weights[0]
    second_block = weights[1]
    third_block = weights[2]
    fourth_block = weights[3]
    norm_in = low(layer_norm(inputs, gain_table[0, 0]))
    projected = wire(product(norm_in, first_block[:, :3 * D]))
    cached = low_back(projected[:, 2 * D:2 * D + shared_width])
    attended = wire(attention(projected[:, :D], projected[:, D:2 * D], projected[:, 2 * D:3 * D], allowed))
    middle = inputs + low_back(product(attended, first_block[:, 3 * D:4 * D]))
    norm_mid = low(layer_norm(middle, gain_table[0, 1]))
    lifted = low_back(product(norm_mid, first_block[:, 4 * D:4 * D + FF]))
    active = low(jax.nn.gelu(lifted, approximate=True))
    layer_one = wire(middle + low_back(product(active, first_block[:, 4 * D + FF:4 * D + 2 * FF].T)))
    norm_two = low(layer_norm(layer_one, gain_table[1, 0]))
    projected_two = wire(product(norm_two, second_block[:, :2 * D + fresh_width]))
    values_two = jnp.concatenate([cached, projected_two[:, 2 * D:]], axis=1)
    attended_two = wire(attention(projected_two[:, :D], projected_two[:, D:2 * D], values_two, allowed))
    out_cols = second_block[:, 2 * D + fresh_width:3 * D + fresh_width]
    mid_two = wire(layer_one + low_back(product(attended_two, out_cols))) + probe_zero
    norm_three = low(layer_norm(mid_two, gain_table[2, 0]))
    lifted_two = low_back(product(norm_three, third_block[:, :FF]))
    active_two = wire(jax.nn.gelu(lifted_two, approximate=True))
    layer_two = mid_two + low_back(product(active_two, fourth_block[:, :FF].T))
    return (layer_one, layer_two)

def reference(tokens, lengths, section_weights, norm_gains, cotangent):
    inputs = tokens.astype(jnp.float32).reshape(BUCKETS, ROWS, D)
    upstream = cotangent.astype(jnp.float32).reshape(BUCKETS, ROWS, D)
    weights = section_weights.astype(jnp.float32)
    gain_args = norm_gains.astype(jnp.float32)
    probe_zero = jnp.zeros((BUCKETS, ROWS, D), jnp.float32)
    layer_pair = jax.checkpoint(two_layers)

    def forward(weight_arg, gain_arg, input_arg, probe_arg):
        return lax.map(lambda bucket_item: layer_pair(weight_arg, gain_arg, bucket_item[0], bucket_item[1], bucket_item[2]), (input_arg, lengths, probe_arg))
    outputs, pullback = jax.vjp(forward, weights, gain_args, inputs, probe_zero)
    grad_weights, grad_gains, grad_inputs, grad_probe = pullback((jnp.zeros_like(outputs[0]), upstream))
    stacked = jnp.stack([grad_inputs, outputs[0], grad_probe, outputs[1]])
    section_out = stacked.reshape(4, TOKENS, D).astype(jnp.bfloat16)
    return (section_out, grad_weights, grad_gains)
```

```python
import functools

import jax
import jax.numpy as jnp
from jax import lax
from jax.experimental import pallas as pl
from jax.experimental.pallas import tpu as pltpu
from jax.sharding import PartitionSpec as P

D = 768
HD = 64
FF = 3072
SV = 384
ROWS = 112
PAIRS = 6
EPS = 1e-05
BF = jnp.bfloat16
F32 = jnp.float32
MICRO = 2

L0, L1, L2, L3 = 0, D, 2 * D, 3 * D
R0 = 4 * D
R1 = R0 + 3 * D
R2 = R1 + D
R3 = R2 + FF
E0 = R3 + FF
E1 = E0 + 3 * D
STORE = E1 + FF

QKV, OUT, UP, DOWN = 0, 3 * D, 4 * D, 4 * D + FF
FRESH = 2 * D + D - SV
CHUNK = 1024
CHUNKS = FF // CHUNK

VM = pl.BlockSpec(memory_space=pltpu.VMEM)
SM = pl.BlockSpec(memory_space=pltpu.SMEM)
HB = pl.BlockSpec(memory_space=pl.ANY)


def dot(left, right):
    return jnp.dot(left, right, preferred_element_type=F32)


def dot_nt(left, right):
    return lax.dot_general(left, right, (((1,), (1,)), ((), ())), preferred_element_type=F32)


def dot_tn(left, right):
    return lax.dot_general(left, right, (((0,), (0,)), ((), ())), preferred_element_type=F32)


def normalized(rows):
    centered = rows - jnp.mean(rows, axis=-1, keepdims=True)
    spread = lax.rsqrt(jnp.mean(centered * centered, axis=-1, keepdims=True) + EPS)
    return centered * spread, spread


def norm_back(hat, spread, gain, grad):
    scaled = grad * gain
    inner = jnp.mean(scaled, axis=-1, keepdims=True)
    along = jnp.mean(scaled * hat, axis=-1, keepdims=True)
    return spread * (scaled - inner - hat * along)


def gelu_pair(u):
    k = 0.7978845608028654
    square = u * u
    t = jnp.tanh(k * u * (1.0 + 0.044715 * square))
    half = 0.5 * (1.0 + t)
    slope = half + 0.5 * u * (1.0 - t * t) * (k * (1.0 + 3 * 0.044715 * square))
    return u * half, slope


def bias_of(lengths, bucket):
    i = lax.broadcasted_iota(jnp.int32, (ROWS, ROWS), 0)
    j = lax.broadcasted_iota(jnp.int32, (ROWS, ROWS), 1)
    e0 = lengths[bucket, 0]
    e1 = e0 + lengths[bucket, 1]
    e2 = e1 + lengths[bucket, 2]
    first = jnp.where(i >= e2, e2, jnp.where(i >= e1, e1, jnp.where(i >= e0, e0, 0)))
    bias = jnp.where((j <= i) & (j >= first), 0.0, -1e30)
    return jnp.concatenate([bias, bias], axis=0)


def lane_masks(scale):
    low = lax.broadcasted_iota(jnp.int32, (ROWS, 2 * HD), 1) < HD
    return jnp.where(low, scale, 0.0).astype(BF), jnp.where(low, 0.0, scale).astype(BF)


def two_heads(block, masks):
    return jnp.concatenate([block * masks[0], block * masks[1]], axis=0)


def joined(stacked):
    low = lax.broadcasted_iota(jnp.int32, (ROWS, 2 * HD), 1) < HD
    return jnp.where(low, stacked[:ROWS], stacked[ROWS:])


def softmax(scores):
    top = jnp.max(scores, axis=-1, keepdims=True)
    powers = jnp.exp(scores - top)
    return powers * (1.0 / jnp.sum(powers, axis=-1, keepdims=True))


def attention(qkv, mixed, row, bias):
    masks = lane_masks(HD ** (-0.5))
    rows = slice(row, row + ROWS)
    for pair in range(PAIRS):
        cols = 2 * HD * pair
        q = qkv[rows, cols : cols + 2 * HD]
        k = qkv[rows, D + cols : D + cols + 2 * HD]
        v = qkv[rows, 2 * D + cols : 2 * D + cols + 2 * HD]
        probs = softmax(dot_nt(two_heads(q, masks), k) + bias)
        mixed[rows, cols : cols + 2 * HD] = joined(dot(probs.astype(BF), v)).astype(BF)


def attention_back(qkv, grad, row, bias, put):
    scaled = lane_masks(HD ** (-0.5))
    plain = lane_masks(1.0)
    rows = slice(row, row + ROWS)
    for pair in range(PAIRS):
        cols = 2 * HD * pair
        q = qkv[rows, cols : cols + 2 * HD]
        k = qkv[rows, D + cols : D + cols + 2 * HD]
        v = qkv[rows, 2 * D + cols : 2 * D + cols + 2 * HD]
        qs = two_heads(q, scaled)
        gs = two_heads(grad[rows, cols : cols + 2 * HD], plain)
        probs = softmax(dot_nt(qs, k) + bias)
        grad_probs = dot_nt(gs, v)
        inner = jnp.sum(grad_probs * probs, axis=-1, keepdims=True)
        grad_scores = (probs * (grad_probs - inner)).astype(BF)
        grad_q = joined(dot(grad_scores, k)) * HD ** (-0.5)
        grad_k = dot_tn(grad_scores, qs)
        grad_v = dot_tn(probs.astype(BF), gs)
        put(rows, cols, grad_q, grad_k, grad_v)


class Moves:
    def __init__(self, sems):
        self.sems = sems
        self.used = 0
        self.open = []

    def load(self, src, dst):
        copy = pltpu.make_async_copy(src, dst, self.sems.at[self.used])
        self.used += 1
        copy.start()
        return copy

    def save(self, src, dst):
        self.open.append(self.load(src, dst))

    def finish(self):
        for copy in self.open:
            copy.wait()


def first_forward(mb, rb, fresh, sec, lengths, gains, slab, tokens, *rest):
    if not fresh:
        rest = rest[3:]
    message, store, mid, outs, w, x, n1, qkv, o1, n2, a1, g1, m1, sems = rest

    @pl.when(sec[0] == 0)
    def _():
        moves = Moves(sems)
        mine = pl.ds(mb * rb, rb)
        get_x = moves.load(tokens.at[mine, :], x)
        pieces = [(QKV, 3 * D), (OUT, D)]
        for c in range(CHUNKS):
            pieces += [(UP + c * CHUNK, CHUNK), (DOWN + c * CHUNK, CHUNK)]
        gets = [
            moves.load(slab.at[:, pl.ds(at, wide)], w.at[:, pl.ds(at, wide)])
            for at, wide in pieces
        ]
        get_x.wait()
        rows = x[...].astype(F32)
        n1[...] = (normalized(rows)[0] * gains[0:1, :]).astype(BF)
        moves.save(n1, store.at[mine, pl.ds(L0, D)])
        gets[0].wait()
        qkv[...] = dot(n1[...], w[:, : 3 * D]).astype(BF)
        moves.save(qkv, store.at[mine, pl.ds(E0, 3 * D)])
        for b in range(rb // ROWS):
            attention(qkv, o1, b * ROWS, bias_of(lengths, mb * (rb // ROWS) + b))
        moves.save(o1, store.at[mine, pl.ds(L1, D)])
        gets[1].wait()
        middle = rows + dot(o1[...], w[:, OUT : OUT + D])
        m1[...] = middle
        moves.save(m1, mid.at[mine, :])
        n2[...] = (normalized(middle)[0] * gains[1:2, :]).astype(BF)
        moves.save(n2, store.at[mine, pl.ds(L2, D)])
        total = middle
        for c in range(CHUNKS):
            cols = slice(c * CHUNK, (c + 1) * CHUNK)
            gets[2 + 2 * c].wait()
            act, slope = gelu_pair(dot(n2[...], w[:, UP + c * CHUNK : UP + (c + 1) * CHUNK]))
            act = act.astype(BF)
            a1[:, cols] = act
            g1[:, cols] = slope.astype(BF)
            gets[3 + 2 * c].wait()
            total = total + dot_nt(act, w[:, DOWN + c * CHUNK : DOWN + (c + 1) * CHUNK])
        moves.save(a1, store.at[mine, pl.ds(R3, FF)])
        moves.save(g1, store.at[mine, pl.ds(E1, FF)])
        message[:, :D] = total.astype(BF)
        message[:, D:] = qkv[:, 2 * D : 2 * D + SV]
        moves.finish()


def second_forward(mb, rb, sec, lengths, gains, slab, arrived, _s, _o, message, store, outs, *rest):
    w, n3, qkv, o2, sems = rest

    @pl.when(sec[0] == 1)
    def _():
        moves = Moves(sems)
        mine = pl.ds(mb * rb, rb)
        get_in = moves.load(slab.at[:, pl.ds(0, FRESH)], w.at[:, pl.ds(0, FRESH)])
        get_out = moves.load(slab.at[:, pl.ds(FRESH, D)], w.at[:, pl.ds(FRESH, D)])
        moves.save(arrived.at[:, pl.ds(0, D)], outs.at[mine, :])
        rows = arrived[:, :D].astype(F32)
        n3[...] = (normalized(rows)[0] * gains[0:1, :]).astype(BF)
        moves.save(n3, store.at[mine, pl.ds(L0, D)])
        qkv[:, 2 * D : 2 * D + SV] = arrived[:, D:]
        get_in.wait()
        mixed = dot(n3[...], w[:, :FRESH]).astype(BF)
        qkv[:, : 2 * D] = mixed[:, : 2 * D]
        qkv[:, 2 * D + SV :] = mixed[:, 2 * D :]
        moves.save(qkv, store.at[mine, pl.ds(E0, 3 * D)])
        for b in range(rb // ROWS):
            attention(qkv, o2, b * ROWS, bias_of(lengths, mb * (rb // ROWS) + b))
        moves.save(o2, store.at[mine, pl.ds(L1, D)])
        get_out.wait()
        message[...] = (rows + dot(o2[...], w[:, FRESH : FRESH + D])).astype(BF)
        moves.finish()


def third_both(mb, rb, sec, gains, slab, other, cot, arrived, _s, _o, message, gg, store, outs, *rest):
    w2, w3, c, n4, a2, du, sems = rest
    gg[...] = jnp.zeros_like(gg)

    @pl.when(sec[0] == 2)
    def _():
        moves = Moves(sems)
        mine = pl.ds(mb * rb, rb)
        get_2, get_3 = [], []
        for k in range(CHUNKS):
            cols = pl.ds(k * CHUNK, CHUNK)
            get_2.append(moves.load(slab.at[:, cols], w2.at[:, cols]))
            get_3.append(moves.load(other.at[:, cols], w3.at[:, cols]))
        get_c = moves.load(cot.at[mine, :], c)
        hat, spread = normalized(arrived[...].astype(F32))
        n4[...] = (hat * gains[0:1, :]).astype(BF)
        moves.save(n4, store.at[mine, pl.ds(L2, D)])
        get_c.wait()
        moves.save(c, store.at[mine, pl.ds(L3, D)])
        back = jnp.zeros((rb, D), F32)
        for k in range(CHUNKS):
            cols = slice(k * CHUNK, (k + 1) * CHUNK)
            get_2[k].wait()
            act, slope = gelu_pair(dot(n4[...], w2[:, cols]))
            a2[:, cols] = act.astype(BF)
            get_3[k].wait()
            grad = dot(c[...], w3[:, cols]).astype(BF).astype(F32)
            lifted = (slope * grad).astype(BF)
            du[:, cols] = lifted
            back = back + dot_nt(lifted, w2[:, cols])
        moves.save(a2, store.at[mine, pl.ds(R3, FF)])
        moves.save(du, store.at[mine, pl.ds(R2, FF)])
        gg[0:1, :] = jnp.sum(back * hat, axis=0, keepdims=True)
        resid = c[...].astype(F32) + norm_back(hat, spread, gains[0:1, :], back)
        message[...] = resid.astype(BF)
        moves.save(message, outs.at[mine, :])
        moves.finish()


def second_back(mb, rb, sec, lengths, gains, slab, arrived, outs, _s, message, gg, store, *rest):
    w, y, qkv, do, dp, sems = rest
    gg[...] = jnp.zeros_like(gg)

    @pl.when(sec[0] == 1)
    def _():
        moves = Moves(sems)
        mine = pl.ds(mb * rb, rb)
        get_out = moves.load(slab.at[:, pl.ds(FRESH, D)], w.at[:, pl.ds(FRESH, D)])
        get_q = moves.load(store.at[mine, pl.ds(E0, 3 * D)], qkv)
        get_y = moves.load(outs.at[mine, :], y)
        get_in = moves.load(slab.at[:, pl.ds(0, FRESH)], w.at[:, pl.ds(0, FRESH)])
        moves.save(arrived, store.at[mine, pl.ds(R1, D)])
        get_out.wait()
        do[...] = dot_nt(arrived[...], w[:, FRESH : FRESH + D]).astype(BF)
        get_q.wait()

        def put(rows, cols, grad_q, grad_k, grad_v):
            wide = 2 * HD
            dp[rows, cols : cols + wide] = grad_q.astype(BF)
            dp[rows, D + cols : D + cols + wide] = grad_k.astype(BF)
            if cols < SV:
                message[rows, D + cols : D + cols + wide] = grad_v.astype(BF)
            else:
                dp[rows, 2 * D + cols - SV : 2 * D + cols - SV + wide] = grad_v.astype(BF)

        for b in range(rb // ROWS):
            bias = bias_of(lengths, mb * (rb // ROWS) + b)
            attention_back(qkv, do, b * ROWS, bias, put)
        moves.save(dp, store.at[mine, pl.ds(R0, FRESH)])
        get_in.wait()
        back = dot_nt(dp[...], w[:, :FRESH])
        get_y.wait()
        hat, spread = normalized(y[...].astype(F32))
        gg[0:1, :] = jnp.sum(back * hat, axis=0, keepdims=True)
        resid = arrived[...].astype(F32) + norm_back(hat, spread, gains[0:1, :], back)
        message[:, :D] = resid.astype(BF)
        moves.finish()


def first_back_wide(mb, rb, sec, gains, slab, arrived, _s, _m, gg, store, mid, *rest):
    w_up, w_down, m1, g1, du, low, sems = rest
    gg[...] = jnp.zeros_like(gg)

    @pl.when(sec[0] == 0)
    def _():
        moves = Moves(sems)
        mine = pl.ds(mb * rb, rb)
        get_d, get_u, get_g = [], [], []
        for k in range(CHUNKS):
            cols = pl.ds(k * CHUNK, CHUNK)
            get_d.append(moves.load(slab.at[:, pl.ds(DOWN + k * CHUNK, CHUNK)], w_down.at[:, cols]))
            get_g.append(moves.load(store.at[mine, pl.ds(E1 + k * CHUNK, CHUNK)], g1.at[:, cols]))
            get_u.append(moves.load(slab.at[:, pl.ds(UP + k * CHUNK, CHUNK)], w_up.at[:, cols]))
        get_m = moves.load(mid.at[mine, :], m1)
        moves.save(arrived.at[:, pl.ds(0, D)], store.at[mine, pl.ds(L3, D)])
        grad = arrived[:, :D]
        back = jnp.zeros((rb, D), F32)
        for k in range(CHUNKS):
            cols = slice(k * CHUNK, (k + 1) * CHUNK)
            get_d[k].wait()
            pulled = dot(grad, w_down[:, cols])
            get_g[k].wait()
            lifted = (g1[:, cols].astype(F32) * pulled).astype(BF)
            du[:, cols] = lifted
            get_u[k].wait()
            back = back + dot_nt(lifted, w_up[:, cols])
        moves.save(du, store.at[mine, pl.ds(R2, FF)])
        get_m.wait()
        hat, spread = normalized(m1[...])
        gg[1:2, :] = jnp.sum(back * hat, axis=0, keepdims=True)
        resid = grad.astype(F32) + norm_back(hat, spread, gains[1:2, :], back)
        low[...] = resid.astype(BF)
        moves.save(low, store.at[mine, pl.ds(R1, D)])
        m1[...] = resid
        moves.save(m1, mid.at[mine, :])
        moves.finish()


def first_back_attend(micro, rb, sec, lengths, gains, slab, tokens, *rest):
    arrived, rest = rest[:micro], rest[micro:]
    mid, _s, _o, gg, store, outs, w, x, qkv, low, do, dq, dm, dx, sems = rest
    gg[...] = jnp.zeros_like(gg)

    @pl.when(sec[0] == 0)
    def _():
        moves = Moves(sems)
        get_l = moves.load(store.at[:, pl.ds(R1, D)], low)
        get_out = moves.load(slab.at[:, pl.ds(OUT, D)], w.at[:, pl.ds(OUT, D)])
        get_q = moves.load(store.at[:, pl.ds(E0, 3 * D)], qkv)
        get_in = moves.load(slab.at[:, pl.ds(QKV, 3 * D)], w.at[:, pl.ds(QKV, 3 * D)])
        get_x = moves.load(tokens, x)
        get_m = moves.load(mid, dm)
        get_l.wait()
        get_out.wait()
        do[...] = dot_nt(low[...], w[:, OUT : OUT + D]).astype(BF)
        get_q.wait()

        def put(rows, cols, grad_q, grad_k, grad_v):
            wide = 2 * HD
            dq[rows, cols : cols + wide] = grad_q.astype(BF)
            dq[rows, D + cols : D + cols + wide] = grad_k.astype(BF)
            if cols < SV:
                part, local = rows.start // rb, rows.start % rb
                cached = arrived[part][local : local + ROWS, D + cols : D + cols + wide]
                grad_v = grad_v + cached.astype(F32)
            dq[rows, 2 * D + cols : 2 * D + cols + wide] = grad_v.astype(BF)

        for b in range(micro * rb // ROWS):
            attention_back(qkv, do, b * ROWS, bias_of(lengths, b), put)
        moves.save(dq, store.at[:, pl.ds(R0, 3 * D)])
        get_in.wait()
        back = dot_nt(dq[...], w[:, QKV : QKV + 3 * D])
        get_x.wait()
        hat, spread = normalized(x[...].astype(F32))
        gg[0:1, :] = jnp.sum(back * hat, axis=0, keepdims=True)
        get_m.wait()
        dx[...] = (dm[...] + norm_back(hat, spread, gains[0:1, :], back)).astype(BF)
        moves.save(dx, outs)
        moves.finish()


def last_forward(micro, rb, sec, other, store, *rest):
    arrived, (result, w3, a2, sems) = rest[:micro], rest[micro:]

    @pl.when(sec[0] == 2)
    def _():
        moves = Moves(sems)
        get_w = moves.load(other, w3)
        get_a = moves.load(store.at[:, pl.ds(R3, FF)], a2)
        get_w.wait()
        get_a.wait()
        total = dot_nt(a2[...], w3[...])
        for part in range(micro):
            rows = slice(part * rb, (part + 1) * rb)
            result[rows, :] = (arrived[part][...].astype(F32) + total[rows]).astype(BF)


def weight_grads(split, core, left, right, *rest):
    total = dot_tn(left[...], right[...]).astype(BF)
    if not split:
        rest[0][...] = total
        return
    keep, send, whole = rest
    whole[...] = total
    wide = whole.shape[0] // 8
    for k in range(4):
        at = pl.multiple_of((2 * k + core[0]) * wide, wide)
        keep[k * wide : (k + 1) * wide, :] = whole[pl.ds(at, wide), :]
        at = pl.multiple_of((2 * k + 1 - core[0]) * wide, wide)
        send[k * wide : (k + 1) * wide, :] = whole[pl.ds(at, wide), :]


def shape(rows, cols, dtype=BF):
    return jax.ShapeDtypeStruct((rows, cols), dtype)


def call(kernel, name, operands, specs, outs, out_specs, scratch, sems, aliases=None, flops=0):
    return pl.pallas_call(
        kernel,
        name=name,
        out_shape=outs,
        in_specs=specs,
        out_specs=out_specs,
        scratch_shapes=scratch + [pltpu.SemaphoreType.DMA((sems,))],
        input_output_aliases=aliases or {},
        compiler_params=pltpu.CompilerParams(vmem_limit_bytes=40 << 20),
        cost_estimate=pl.CostEstimate(flops=flops, bytes_accessed=4 << 20, transcendentals=0),
    )(*operands)


def sum_products(name, store, core, first, lefts, split):
    count = len(lefts)
    rows = store.shape[0]
    table = jnp.asarray(lefts, jnp.int32)
    half = shape(D // 2, count * D)
    if split:
        outs = [half, half]
        out_specs = [pl.BlockSpec((D // 2, D), lambda j, c, t: (0, j))] * 2
        scratch = [pltpu.VMEM((D, D), BF)]
    else:
        outs = [shape(D, count * D)]
        out_specs = [pl.BlockSpec((D, D), lambda j, c, t: (0, j))]
        scratch = []

    def kernel(core_ref, table_ref, left, right, *rest):
        weight_grads(split, core_ref, left, right, *rest)

    return pl.pallas_call(
        kernel,
        name=name,
        out_shape=outs,
        grid_spec=pltpu.PrefetchScalarGridSpec(
            num_scalar_prefetch=2,
            grid=(count,),
            in_specs=[
                pl.BlockSpec((rows, D), lambda j, c, t: (0, t[j])),
                pl.BlockSpec((rows, D), lambda j, c, t: (0, first + j)),
            ],
            out_specs=out_specs,
            scratch_shapes=scratch,
        ),
        compiler_params=pltpu.CompilerParams(vmem_limit_bytes=40 << 20),
        cost_estimate=pl.CostEstimate(
            flops=2 * rows * D * D * count, bytes_accessed=4 << 20, transcendentals=0
        ),
    )(core, table, store, store)


def exchange(block, bit, axis="dp"):
    count = lax.axis_size(axis)
    return lax.ppermute(block, axis, [(i, i ^ bit) for i in range(count)])


def shift(block, pairs):
    return lax.ppermute(block, "section", pairs)


def scatter_sum(keep, send):
    index = lax.axis_index("dp")
    x = (index // 2) % 2
    y = index // 4
    got = exchange(send, 1)
    rows, cols = keep.shape
    part = rows // 4
    half = cols // 2
    keep = keep.reshape(2, 2, part, cols)
    got = got.reshape(2, 2, part, cols)

    def pick(block, where, axis, lo):
        block = block[..., lo : lo + half]
        return lax.dynamic_index_in_dim(block, where, axis, keepdims=False).astype(F32)

    def summed(where, axis, lo):
        return (pick(keep, where, axis, lo) + pick(got, where, axis, lo)).astype(BF)

    send_a, send_b = summed(1 - x, 1, 0), summed(1 - y, 0, half)
    got_a, got_b = exchange(send_a, 2), exchange(send_b, 4)
    mine_a, mine_b = summed(x, 1, 0), summed(y, 0, half)

    def second(mine, got, where):
        def one(block):
            return lax.dynamic_index_in_dim(block, where, 0, keepdims=False).astype(F32)

        return one(mine) + one(got)

    last_a = exchange(second(mine_a, got_a, 1 - y).astype(BF), 4)
    last_b = exchange(second(mine_b, got_b, 1 - x).astype(BF), 2)
    return jnp.concatenate(
        [
            second(mine_a, got_a, y) + last_a.astype(F32),
            second(mine_b, got_b, x) + last_b.astype(F32),
        ],
        axis=1,
    )


def body(tokens, lengths, section_weights, norm_gains, cotangent):
    slab = section_weights[0]
    gains = norm_gains[0]
    section = lax.axis_index("section")
    dp = lax.axis_size("dp")
    place = lax.axis_index("dp")
    sec = section.astype(jnp.int32).reshape(1)
    core = (place % 2).astype(jnp.int32).reshape(1)
    total_rows = tokens.shape[0]
    rb = total_rows // MICRO
    shard = D // dp

    piece = lax.dynamic_slice(slab, (place * shard, 0), (shard, FF))
    piece = shift(piece, [(3, 2)])
    other = lax.all_gather(piece, "dp", axis=0, tiled=True)

    def act(cols, dtype=BF, rows=rb):
        return pltpu.VMEM((rows, cols), dtype)

    store = mid = outs = None
    sent = []
    for mb in range(MICRO):
        fresh = mb == 0
        operands = [sec, lengths, gains, slab, tokens]
        specs = [SM, SM, VM, HB, HB]
        aliases = {}
        if not fresh:
            operands += [store, mid, outs]
            specs += [HB, HB, HB]
            aliases = {5: 1, 6: 2, 7: 3}
        message, store, mid, outs = call(
            functools.partial(first_forward, mb, rb, fresh),
            "first_forward",
            operands,
            specs,
            [shape(rb, D + SV), shape(total_rows, STORE), shape(total_rows, D, F32), shape(total_rows, D)],
            [VM, HB, HB, HB],
            [pltpu.VMEM((D, 4 * D + 2 * FF), BF), act(D), act(D), act(3 * D), act(D), act(D)]
            + [act(FF), act(FF), act(D, F32)],
            20,
            aliases,
            flops=2 * rb * D * (4 * D + 2 * FF),
        )
        sent.append(shift(message, [(0, 1)]))

    sent_2 = []
    for mb in range(MICRO):
        message, store, outs = call(
            functools.partial(second_forward, mb, rb),
            "second_forward",
            [sec, lengths, gains, slab, sent[mb], store, outs],
            [SM, SM, VM, HB, VM, HB, HB],
            [shape(rb, D), shape(total_rows, STORE), shape(total_rows, D)],
            [VM, HB, HB],
            [pltpu.VMEM((D, FRESH + D), BF), act(D), act(3 * D), act(D)],
            10,
            {5: 1, 6: 2},
            flops=2 * rb * D * (FRESH + D),
        )
        sent_2.append(shift(message, [(1, 2)]))

    gain_parts = []
    back_2 = []
    for mb in range(MICRO):
        message, gg, store, outs = call(
            functools.partial(third_both, mb, rb),
            "third_both",
            [sec, gains, slab, other, cotangent, sent_2[mb], store, outs],
            [SM, VM, HB, HB, HB, VM, HB, HB],
            [shape(rb, D), shape(8, D, F32), shape(total_rows, STORE), shape(total_rows, D)],
            [VM, VM, HB, HB],
            [pltpu.VMEM((D, FF), BF), pltpu.VMEM((D, FF), BF), act(D), act(D), act(FF), act(FF)],
            20,
            {6: 2, 7: 3},
            flops=6 * rb * D * FF,
        )
        gain_parts.append(gg)
        back_2.append(shift(message, [(2, 1)]))

    back_1 = []
    for mb in range(MICRO):
        message, gg, store = call(
            functools.partial(second_back, mb, rb),
            "second_back",
            [sec, lengths, gains, slab, back_2[mb], outs, store],
            [SM, SM, VM, HB, VM, HB, HB],
            [shape(rb, D + SV), shape(8, D, F32), shape(total_rows, STORE)],
            [VM, VM, HB],
            [pltpu.VMEM((D, FRESH + D), BF), act(D), act(3 * D), act(D), act(FRESH)],
            10,
            {6: 2},
            flops=2 * rb * D * (FRESH + D),
        )
        gain_parts.append(gg)
        back_1.append(shift(message, [(1, 0)]))

    for mb in range(MICRO):
        gg, store, mid = call(
            functools.partial(first_back_wide, mb, rb),
            "first_back_wide",
            [sec, gains, slab, back_1[mb], store, mid],
            [SM, VM, HB, VM, HB, HB],
            [shape(8, D, F32), shape(total_rows, STORE), shape(total_rows, D, F32)],
            [VM, HB, HB],
            [pltpu.VMEM((D, FF), BF), pltpu.VMEM((D, FF), BF), act(D, F32), act(FF), act(FF), act(D)],
            20,
            {4: 1, 5: 2},
            flops=4 * rb * D * FF,
        )
        gain_parts.append(gg)

    split = dp == 8
    wide = sum_products("wide_grads", store, core, R2 // D, [2] * 4 + [3] * 4, split)

    gg, store, outs = call(
        functools.partial(first_back_attend, MICRO, rb),
        "first_back_attend",
        [sec, lengths, gains, slab, tokens] + back_1 + [mid, store, outs],
        [SM, SM, VM, HB, HB] + [VM] * MICRO + [HB, HB, HB],
        [shape(8, D, F32), shape(total_rows, STORE), shape(total_rows, D)],
        [VM, HB, HB],
        [pltpu.VMEM((D, 4 * D), BF), act(D, BF, total_rows), act(3 * D, BF, total_rows)]
        + [act(D, BF, total_rows), act(D, BF, total_rows), act(3 * D, BF, total_rows)]
        + [act(D, F32, total_rows), act(D, BF, total_rows)],
        12,
        {6 + MICRO: 1, 7 + MICRO: 2},
        flops=2 * total_rows * D * 4 * D,
    )
    gain_parts.append(gg)
    narrow = sum_products("narrow_grads", store, core, R0 // D, [0] * 3 + [1], split)

    result = call(
        functools.partial(last_forward, MICRO, rb),
        "last_forward",
        [sec, other, store] + sent_2,
        [SM, HB, HB] + [VM] * MICRO,
        [shape(total_rows, D)],
        [VM],
        [pltpu.VMEM((D, FF), BF), act(FF, BF, total_rows)],
        4,
        flops=2 * total_rows * D * FF,
    )[0]
    result = shift(result, [(2, 3)])

    if split:
        wide_sum = scatter_sum(*wide)
        narrow_sum = scatter_sum(*narrow)
    else:
        wide_sum, narrow_sum = [
            lax.psum_scatter(part[0], "dp", scatter_dimension=0, tiled=True).astype(F32)
            for part in (wide, narrow)
        ]
    moved = shift(wide_sum[:, FF:].astype(BF), [(2, 3)]).astype(F32)

    gain_total = functools.reduce(jnp.add, gain_parts)[:2]
    gain_cols = lax.psum_scatter(gain_total.T, "dp", scatter_dimension=0, tiled=True)

    blank = functools.partial(jnp.zeros, dtype=F32)
    width = slab.shape[1]
    choices = [
        jnp.concatenate([narrow_sum, wide_sum], axis=1),
        jnp.concatenate(
            [narrow_sum[:, :FRESH], narrow_sum[:, 3 * D :], blank((shard, width - FRESH - D))], axis=1
        ),
        jnp.concatenate([wide_sum[:, :FF], blank((shard, width - FF))], axis=1),
        jnp.concatenate([moved, blank((shard, width - FF))], axis=1),
    ]
    slab_grad = jnp.where(
        section == 0,
        choices[0],
        jnp.where(section == 1, choices[1], jnp.where(section == 2, choices[2], choices[3])),
    )
    outs = jnp.where(section == 3, result, outs)
    return (outs[None], slab_grad[None], gain_cols.T[None])


def solution(mesh):
    placed = (
        P("dp", None),
        P("dp", None),
        P("section", None, None),
        P("section", None, None),
        P("dp", None),
    )
    return jax.shard_map(
        body,
        mesh=mesh,
        in_specs=placed,
        out_specs=(P("section", "dp", None), P("section", "dp", None), P("section", None, "dp")),
        check_vma=False,
    )
```

```python
import functools

import jax
import jax.numpy as jnp
from jax import lax
from jax.experimental import pallas as pl
from jax.experimental.pallas import tpu as pltpu
from jax.sharding import PartitionSpec as P

D = 768
HD = 64
FF = 3072
SV = 384
ROWS = 112
PAIRS = 6
WIDE = 2 * HD
EPS = 1e-05
BF = jnp.bfloat16
F32 = jnp.float32

SPLIT = (1, 1, 1, 1)

L0, L1, L2, L3 = 0, D, 2 * D, 3 * D
R0, R1, R2, R3 = 0, 3 * D, 4 * D, 4 * D + FF
ALL = 4 * D + 2 * FF

QKV, OUT, UP, DOWN = 0, 3 * D, 4 * D, 4 * D + FF
FRESH = 2 * D + D - SV
HALF = FF // 2

VM = pl.BlockSpec(memory_space=pltpu.VMEM)
SM = pl.BlockSpec(memory_space=pltpu.SMEM)
HB = pl.BlockSpec(memory_space=pltpu.HBM)
ANY = pl.BlockSpec(memory_space=pl.ANY)


def dot(left, right):
    return jnp.dot(left, right, preferred_element_type=F32)


def dot_nt(left, right):
    return lax.dot_general(left, right, (((1,), (1,)), ((), ())), preferred_element_type=F32)


def normalized(rows):
    centered = rows - jnp.mean(rows, axis=-1, keepdims=True)
    spread = lax.rsqrt(jnp.mean(centered * centered, axis=-1, keepdims=True) + EPS)
    return centered * spread, spread


def norm_back(hat, spread, gain, grad):
    scaled = grad * gain
    inner = jnp.mean(scaled, axis=-1, keepdims=True)
    along = jnp.mean(scaled * hat, axis=-1, keepdims=True)
    return spread * (scaled - inner - hat * along)


def gelu_pair(u):
    c0 = 0.7978845608028654
    c1 = c0 * 0.044715
    square = u * u
    half = 0.5 + 0.5 * jnp.tanh(u * (c0 + c1 * square))
    act = u * half
    return act, half + act * ((1.0 - half) * (2.0 * c0 + (6.0 * c1) * square))


def sequence_start(lengths, bucket, i):
    e0 = lengths[bucket, 0]
    e1 = e0 + lengths[bucket, 1]
    e2 = e1 + lengths[bucket, 2]
    return jnp.where(i >= e2, e2, jnp.where(i >= e1, e1, jnp.where(i >= e0, e0, 0)))


def bias_rows(lengths, bucket):
    i = lax.broadcasted_iota(jnp.int32, (ROWS, ROWS), 0)
    j = lax.broadcasted_iota(jnp.int32, (ROWS, ROWS), 1)
    bias = jnp.where((j <= i) & (j >= sequence_start(lengths, bucket, i)), 0.0, -1e30)
    return jnp.concatenate([bias, bias], axis=0)


def bias_columns(lengths, bucket):
    j = lax.broadcasted_iota(jnp.int32, (ROWS, 2 * ROWS), 0)
    i = lax.broadcasted_iota(jnp.int32, (ROWS, 2 * ROWS), 1)
    i = jnp.where(i >= ROWS, i - ROWS, i)
    return jnp.where((j <= i) & (j >= sequence_start(lengths, bucket, i)), 0.0, -1e30)


def lane_masks(scale):
    low = lax.broadcasted_iota(jnp.int32, (ROWS, WIDE), 1) < HD
    return jnp.where(low, scale, 0.0).astype(BF), jnp.where(low, 0.0, scale).astype(BF)


def two_heads(block, masks):
    return jnp.concatenate([block * masks[0], block * masks[1]], axis=0)


def joined(stacked):
    low = lax.broadcasted_iota(jnp.int32, (ROWS, WIDE), 1) < HD
    return jnp.where(low, stacked[:ROWS], stacked[ROWS:])


def softmax(scores, axis):
    top = jnp.max(scores, axis=axis, keepdims=True)
    powers = jnp.exp(scores - top)
    return powers * (1.0 / jnp.sum(powers, axis=axis, keepdims=True))


def attention(qkv, rows, bias, put):
    masks = lane_masks(HD ** (-0.5))
    at = [WIDE * p for p in range(PAIRS)]
    scores = [
        dot_nt(two_heads(qkv[rows, c : c + WIDE], masks), qkv[rows, D + c : D + c + WIDE]) + bias
        for c in at
    ]
    probs = [softmax(s, -1).astype(BF) for s in scores]
    for c, p in zip(at, probs):
        put(c, joined(dot(p, qkv[rows, 2 * D + c : 2 * D + c + WIDE])))


def attention_back(qkv, rows, grad, bias, put):
    scaled = lane_masks(HD ** (-0.5))
    plain = lane_masks(1.0)
    at = [WIDE * p for p in range(PAIRS)]
    qs = [two_heads(qkv[rows, c : c + WIDE], scaled) for c in at]
    ks = [qkv[rows, D + c : D + c + WIDE] for c in at]
    vs = [qkv[rows, 2 * D + c : 2 * D + c + WIDE] for c in at]
    gs = [two_heads(grad[:, c : c + WIDE], plain) for c in at]
    scores = [dot_nt(k, q) + bias for k, q in zip(ks, qs)]
    grad_probs = [dot_nt(v, g) for v, g in zip(vs, gs)]
    probs = [softmax(s, 0) for s in scores]
    inner = [jnp.sum(d * p, axis=0, keepdims=True) for d, p in zip(grad_probs, probs)]
    grad_scores = [(p * (d - i)).astype(BF) for p, d, i in zip(probs, grad_probs, inner)]
    grad_v = [dot(p.astype(BF), g) for p, g in zip(probs, gs)]
    grad_k = [dot(s, q) for s, q in zip(grad_scores, qs)]
    turned = [s.T for s in grad_scores]
    grad_q = [joined(dot(t, k)) * HD ** (-0.5) for t, k in zip(turned, ks)]
    for c, dq, dk, dv in zip(at, grad_q, grad_k, grad_v):
        put(c, dq, dk, dv)


def buckets_of(start, stop):
    return [(b // ROWS, slice(b, b + ROWS)) for b in range(start, stop, ROWS)]


class Loads:
    def __init__(self, sems):
        self.sems = sems
        self.used = 0

    def start(self, src, dst):
        copy = pltpu.make_async_copy(src, dst, self.sems.at[self.used])
        self.used += 1
        copy.start()
        return copy


def forward_wide(left, right, slope, rows, rb, w, up, down, chunk, waits=None):
    count = FF // chunk

    def lift(c):
        if waits:
            waits[0][c].wait()
        return dot(left[rows, L2 : L2 + D], w[:, up + c * chunk : up + (c + 1) * chunk])

    total = None
    here = lift(0)
    for c in range(count):
        ahead = lift(c + 1) if c + 1 < count else None
        act, gradient = gelu_pair(here)
        act = act.astype(BF)
        right[rows, R3 + c * chunk : R3 + (c + 1) * chunk] = act
        slope[rows, c * chunk : (c + 1) * chunk] = gradient.astype(BF)
        if down is not None:
            if waits:
                waits[1][c].wait()
            part = dot_nt(act, w[:, down + c * chunk : down + (c + 1) * chunk])
            total = part if total is None else total + part
        here = ahead
    return total


CHUNK = 512
COST = 1000


def first_forward(start, stop, fresh, sec, lengths, gains, tokens, *refs):
    if fresh:
        slab, refs = refs[0], refs[1:]
        w, left, right, qkv, slope, mid, outs, gg, message, sems = refs
        gg[...] = jnp.zeros_like(gg)
    else:
        w, refs = refs[0], refs[1:]
        left, right, qkv, slope, mid, message, sems = refs[5:]
    rows = slice(start, stop)
    rb = stop - start
    if fresh:

        @pl.when((sec[0] == 1) | (sec[0] == 2))
        def _():
            loads = Loads(sems)
            both = [
                loads.start(slab.at[:, pl.ds(at, HALF)], w.at[:, pl.ds(at, HALF)])
                for at in (0, HALF)
            ]
            for load in both:
                load.wait()

    @pl.when(sec[0] == 0)
    def _():
        loads = Loads(sems)
        first = second = waits = None
        if fresh:

            def get(at, wide):
                return loads.start(slab.at[:, pl.ds(at, wide)], w.at[:, pl.ds(at, wide)])

            first = [get(QKV + c * D, D) for c in range(3)]
            second = get(OUT, D)
            waits = ([], [])
            for c in range(FF // CHUNK):
                waits[0].append(get(UP + c * CHUNK, CHUNK))
                waits[1].append(get(DOWN + c * CHUNK, CHUNK))
        x = tokens[rows, :].astype(F32)
        low = (normalized(x)[0] * gains[0:1, :]).astype(BF)
        left[rows, L0 : L0 + D] = low
        for c in range(3):
            if fresh:
                first[c].wait()
            qkv[rows, c * D : (c + 1) * D] = dot(low, w[:, QKV + c * D : QKV + (c + 1) * D]).astype(BF)
        message[:, D:] = qkv[rows, 2 * D : 2 * D + SV]
        for bucket, here in buckets_of(start, stop):

            def put(c, value):
                left[here, L1 + c : L1 + c + WIDE] = value.astype(BF)

            attention(qkv, here, bias_rows(lengths, bucket), put)
        if fresh:
            second.wait()
        middle = x + dot(left[rows, L1 : L1 + D], w[:, OUT : OUT + D])
        mid[rows, :] = middle
        left[rows, L2 : L2 + D] = (normalized(middle)[0] * gains[1:2, :]).astype(BF)
        total = forward_wide(left, right, slope, rows, rb, w, UP, DOWN, CHUNK, waits)
        message[:, :D] = (middle + total).astype(BF)


def second_forward(start, stop, sec, lengths, gains, w, arrived, *refs):
    left, qkv, outs, message, sems = refs[3:]
    rows = slice(start, stop)

    @pl.when(sec[0] == 1)
    def _():
        outs[rows, :] = arrived[:, :D]
        x = arrived[:, :D].astype(F32)
        low = (normalized(x)[0] * gains[0:1, :]).astype(BF)
        left[rows, L0 : L0 + D] = low
        mixed = dot(low, w[:, :FRESH]).astype(BF)
        qkv[rows, : 2 * D] = mixed[:, : 2 * D]
        qkv[rows, 2 * D : 2 * D + SV] = arrived[:, D:]
        qkv[rows, 2 * D + SV :] = mixed[:, 2 * D :]
        for bucket, here in buckets_of(start, stop):

            def put(c, value):
                left[here, L1 + c : L1 + c + WIDE] = value.astype(BF)

            attention(qkv, here, bias_rows(lengths, bucket), put)
        message[...] = (x + dot(left[rows, L1 : L1 + D], w[:, FRESH : FRESH + D])).astype(BF)


def third_forward(start, stop, sec, gains, w, cot, arrived, *refs):
    left, right, slope, token, sems = refs[3:]
    rows = slice(start, stop)
    token[...] = jnp.zeros_like(token)

    @pl.when(sec[0] == 2)
    def _():
        left[rows, L1 : L1 + D] = arrived[...]
        left[rows, L3 : L3 + D] = cot[rows, :]
        hat = normalized(arrived[...].astype(F32))[0]
        left[rows, L2 : L2 + D] = (hat * gains[0:1, :]).astype(BF)
        forward_wide(left, right, slope, rows, stop - start, w, 0, None, CHUNK)


def third_back(start, stop, sec, core, gains, w, mine, got, slope, left, *refs):
    right, outs, gg, message, sems = refs[3:]
    rows = slice(start, stop)

    @pl.when(sec[0] == 2)
    def _():
        c = left[rows, L3 : L3 + D]
        back = None
        for other, which in ((mine, core[0]), (got, 1 - core[0])):
            for k in range(0, HALF, D):
                at = pl.multiple_of(which * HALF + k, 128)
                grad = dot(c, other[:, k : k + D]).astype(BF).astype(F32)
                lifted = (slope[rows, pl.ds(at, D)].astype(F32) * grad).astype(BF)
                right[rows, pl.ds(pl.multiple_of(R2 + at, 128), D)] = lifted
                part = dot_nt(lifted, w[:, pl.ds(at, D)])
                back = part if back is None else back + part
        hat, spread = normalized(left[rows, L1 : L1 + D].astype(F32))
        gg[0:1, :] += jnp.sum(back * hat, axis=0, keepdims=True)
        resid = c.astype(F32) + norm_back(hat, spread, gains[0:1, :], back)
        message[...] = resid.astype(BF)
        outs[rows, :] = resid.astype(BF)


def second_back(start, stop, sec, lengths, gains, w, qkv, outs, arrived, *refs):
    right, gg, message, sems = refs[2:]
    rows = slice(start, stop)

    @pl.when(sec[0] == 1)
    def _():
        right[rows, R1 : R1 + D] = arrived[...]
        grad = dot_nt(arrived[...], w[:, FRESH : FRESH + D]).astype(BF)
        for bucket, here in buckets_of(start, stop):
            local = slice(here.start - start, here.stop - start)

            def put(c, dq, dk, dv):
                right[here, R0 + c : R0 + c + WIDE] = dq.astype(BF)
                right[here, R0 + D + c : R0 + D + c + WIDE] = dk.astype(BF)
                if c < SV:
                    message[local, D + c : D + c + WIDE] = dv.astype(BF)
                else:
                    right[here, R0 + 2 * D + c - SV : R0 + 2 * D + c - SV + WIDE] = dv.astype(BF)

            attention_back(qkv, here, grad[local], bias_columns(lengths, bucket), put)
        back = dot_nt(right[rows, R0 : R0 + FRESH], w[:, :FRESH])
        hat, spread = normalized(outs[rows, :].astype(F32))
        gg[0:1, :] += jnp.sum(back * hat, axis=0, keepdims=True)
        resid = arrived[...].astype(F32) + norm_back(hat, spread, gains[0:1, :], back)
        message[:, :D] = resid.astype(BF)


def first_back_wide(start, stop, sec, gains, w, slope, arrived, *refs):
    left, right, mid, gg, sems = refs[4:]
    rows = slice(start, stop)

    @pl.when(sec[0] == 0)
    def _():
        left[rows, L3 : L3 + D] = arrived[:, :D]
        grad = arrived[:, :D]
        back = None
        pulled = dot(grad, w[:, DOWN : DOWN + CHUNK])
        for c in range(FF // CHUNK):
            k = c * CHUNK
            ahead = None
            if k + CHUNK < FF:
                ahead = dot(grad, w[:, DOWN + k + CHUNK : DOWN + k + 2 * CHUNK])
            lifted = (slope[rows, k : k + CHUNK].astype(F32) * pulled).astype(BF)
            right[rows, R2 + k : R2 + k + CHUNK] = lifted
            part = dot_nt(lifted, w[:, UP + k : UP + k + CHUNK])
            back = part if back is None else back + part
            pulled = ahead
        hat, spread = normalized(mid[rows, :])
        gg[1:2, :] += jnp.sum(back * hat, axis=0, keepdims=True)
        resid = grad.astype(F32) + norm_back(hat, spread, gains[1:2, :], back)
        right[rows, R1 : R1 + D] = resid.astype(BF)
        mid[rows, :] = resid


def first_back_attend(start, stop, sec, lengths, gains, tokens, w, qkv, mid, arrived, *refs):
    right, outs, gg, sems = refs[3:]
    rows = slice(start, stop)

    @pl.when(sec[0] == 0)
    def _():
        grad = dot_nt(right[rows, R1 : R1 + D], w[:, OUT : OUT + D]).astype(BF)
        for bucket, here in buckets_of(start, stop):
            local = slice(here.start - start, here.stop - start)

            def put(c, dq, dk, dv):
                right[here, R0 + c : R0 + c + WIDE] = dq.astype(BF)
                right[here, R0 + D + c : R0 + D + c + WIDE] = dk.astype(BF)
                if c < SV:
                    dv = dv + arrived[local, D + c : D + c + WIDE].astype(F32)
                right[here, R0 + 2 * D + c : R0 + 2 * D + c + WIDE] = dv.astype(BF)

            attention_back(qkv, here, grad[local], bias_columns(lengths, bucket), put)
        back = dot_nt(right[rows, R0 : R0 + 3 * D], w[:, QKV : QKV + 3 * D])
        hat, spread = normalized(tokens[rows, :].astype(F32))
        gg[0:1, :] += jnp.sum(back * hat, axis=0, keepdims=True)
        outs[rows, :] = (mid[rows, :] + norm_back(hat, spread, gains[0:1, :], back)).astype(BF)


def last_forward(sec, core, left, right, mine, got, result, sems):
    @pl.when(sec[0] == 2)
    def _():
        total = left[:, L1 : L1 + D].astype(F32)
        for other, which in ((mine, core[0]), (got, 1 - core[0])):
            at = pl.multiple_of(R3 + which * HALF, 128)
            total = total + dot_nt(right[:, pl.ds(at, HALF)], other[...])
        result[...] = total.astype(BF)


def take_columns(sec, order, slab, piece, sems):
    @pl.when(sec[0] == 3)
    def _():
        wide = piece.shape[1]
        at = pl.multiple_of(order[0] * wide, 128)
        Loads(sems).start(slab.at[:, pl.ds(at, wide)], piece).wait()


def halve_rows(sec, piece, upper, lower):
    @pl.when(sec[0] == 2)
    def _():
        upper[...] = piece[: D // 2]
        lower[...] = piece[D // 2 :]


def gather_columns(sec, spot, piece, from_x, from_y, merged):
    @pl.when(sec[0] == 2)
    def _():
        wide = piece.shape[1]
        odd = (spot[0] + spot[1]) % 2
        merged[:, pl.ds(pl.multiple_of(odd * wide, 128), wide)] = piece[...]
        other = pl.ds(pl.multiple_of((1 - odd) * wide, 128), wide)
        merged[: D // 2, other] = from_x[...]
        merged[D // 2 :, other] = from_y[...]


def weight_grads(first, groups, split, core, left, right, *refs):
    turned, refs = refs[-1], refs[:-1]
    step = pl.program_id(0)
    before = None
    for j, group in enumerate(groups):
        if group != before:

            @pl.when(step == j)
            def _(group=group):
                turned[...] = left[:, group * D : (group + 1) * D].T

        before = group
    cols = pl.ds(pl.multiple_of(first + step * D, 128), D)
    total = dot(turned[...], right[:, cols]).astype(BF)
    if not split:
        refs[0][...] = total
        return
    keep, send, whole = refs
    whole[...] = total
    wide = D // 8
    for k in range(4):
        at = pl.multiple_of((2 * k + core[0]) * wide, wide)
        keep[k * wide : (k + 1) * wide, :] = whole[pl.ds(at, wide), :]
        at = pl.multiple_of((2 * k + 1 - core[0]) * wide, wide)
        send[k * wide : (k + 1) * wide, :] = whole[pl.ds(at, wide), :]


def sum_first(spot, keep, got, send_a, send_b, mine_a, mine_b):
    part, half = send_a.shape[0] // 2, send_a.shape[1]
    x, y = spot[0], spot[1]

    def both(where, lo):
        rows = pl.ds(pl.multiple_of(where * part, part), part)
        cols = slice(lo, lo + half)
        return (keep[rows, cols].astype(F32) + got[rows, cols].astype(F32)).astype(BF)

    for k in range(2):
        here = slice(k * part, (k + 1) * part)
        send_a[here, :] = both(2 * k + 1 - x, 0)
        send_b[here, :] = both(2 * (1 - y) + k, half)
        mine_a[here, :] = both(2 * k + x, 0)
        mine_b[here, :] = both(2 * y + k, half)


def sum_second(spot, mine_a, mine_b, got_a, got_b, send_a, send_b, last_a, last_b):
    part = send_a.shape[0]
    x, y = spot[0], spot[1]

    def both(mine, got, where):
        rows = pl.ds(pl.multiple_of(where * part, part), part)
        return mine[rows, :].astype(F32) + got[rows, :].astype(F32)

    send_a[...] = both(mine_a, got_a, 1 - y).astype(BF)
    send_b[...] = both(mine_b, got_b, 1 - x).astype(BF)
    last_a[...] = both(mine_a, got_a, y)
    last_b[...] = both(mine_b, got_b, x)


def finish(sec, wide, narrow, moved, outs, result, grads, rows):
    count = grads.shape[0]

    def total(pair, at, lo, hi):
        return pair[2 * at][:, lo:hi] + pair[2 * at + 1][:, lo:hi].astype(F32)

    @pl.when(sec[0] == 0)
    def _():
        half = 2 * D
        grads[:, :half] = total(narrow, 0, 0, half)
        grads[:, half : 2 * half] = total(narrow, 1, 0, half)
        grads[:, 2 * half : 2 * half + FF] = total(wide, 0, 0, FF)
        grads[:, 2 * half + FF :] = total(wide, 1, 0, FF)

    @pl.when(sec[0] == 1)
    def _():
        half = 2 * D
        grads[:, :half] = total(narrow, 0, 0, half)
        grads[:, half:FRESH] = total(narrow, 1, 0, FRESH - half)
        grads[:, FRESH : FRESH + D] = total(narrow, 1, D, 2 * D)
        grads[:, FRESH + D :] = jnp.zeros((count, ALL - FRESH - D), F32)

    @pl.when(sec[0] == 2)
    def _():
        grads[:, :FF] = total(wide, 0, 0, FF)
        grads[:, FF:] = jnp.zeros((count, ALL - FF), F32)

    @pl.when(sec[0] == 3)
    def _():
        grads[:, :FF] = moved[...].astype(F32)
        grads[:, FF:] = jnp.zeros((count, ALL - FF), F32)
        rows[...] = result[...]

    @pl.when(sec[0] != 3)
    def _():
        rows[...] = outs[...]


def shape(rows, cols, dtype=BF):
    return jax.ShapeDtypeStruct((rows, cols), dtype)


def held(rows, cols, dtype=BF):
    return pltpu.VMEM((rows, cols), dtype)


def keep_in_vmem(array):
    return pltpu.with_memory_space_constraint(array, pltpu.VMEM)


def call(kernel, name, ins, states, outs, sems=1, scratch=(), after=()):
    operands = [a for a, _ in ins] + [keep_in_vmem(s) for s in states]
    aliases = {len(ins) + i: i for i in range(len(states))}
    out_shape = [held(*s.shape, s.dtype) for s in states] + list(outs)
    return pl.pallas_call(
        behind(kernel, len(operands), after),
        name=name,
        out_shape=out_shape,
        in_specs=[s for _, s in ins] + [VM] * len(states) + [ANY] * len(after),
        out_specs=[VM] * len(out_shape),
        scratch_shapes=[pltpu.SemaphoreType.DMA((sems,))] + list(scratch),
        input_output_aliases=aliases,
        compiler_params=pltpu.CompilerParams(vmem_limit_bytes=8 << 20),
        cost_estimate=pl.CostEstimate(flops=COST, bytes_accessed=1024, transcendentals=0),
    )(*operands, *after)


def products(name, left, right, core, first, groups, split):
    count = len(groups)
    rows = left.shape[0]
    if split:
        outs = [shape(D // 2, count * D)] * 2
        out_specs = [pl.BlockSpec((D // 2, D), lambda j: (0, j))] * 2
        scratch = [pltpu.VMEM((D, D), BF)]
    else:
        outs = [shape(D, count * D)]
        out_specs = [pl.BlockSpec((D, D), lambda j: (0, j))]
        scratch = []
    return pl.pallas_call(
        functools.partial(weight_grads, first, groups, split),
        name=name,
        out_shape=outs,
        grid=(count,),
        in_specs=[SM, VM, VM],
        out_specs=out_specs,
        scratch_shapes=scratch + [pltpu.VMEM((D, rows), BF)],
        compiler_params=pltpu.CompilerParams(vmem_limit_bytes=8 << 20),
        cost_estimate=pl.CostEstimate(flops=COST, bytes_accessed=1024, transcendentals=0),
    )(core, keep_in_vmem(left), keep_in_vmem(right))


def behind(kernel, count, after):
    def ordered(*refs):
        kernel(*refs[:count], *refs[count + len(after) :])

    return ordered


def plain(kernel, name, operands, specs, outs, limit=8, scratch=(), after=()):
    return pl.pallas_call(
        behind(kernel, len(operands), after),
        name=name,
        out_shape=outs,
        in_specs=specs + [ANY] * len(after),
        out_specs=[VM] * len(outs),
        scratch_shapes=list(scratch),
        compiler_params=pltpu.CompilerParams(vmem_limit_bytes=limit << 20),
        cost_estimate=pl.CostEstimate(flops=COST, bytes_accessed=1024, transcendentals=0),
    )(*operands, *after)


def exchange(block, bit):
    count = lax.axis_size("dp")
    return lax.ppermute(block, "dp", [(i, i ^ bit) for i in range(count)])


def exchange_on(part, block, bit):
    count, parts = lax.axis_size("dp"), lax.axis_size("section")
    pairs = [(i * parts + part, (i ^ bit) * parts + part) for i in range(count)]
    return lax.ppermute(block, ("dp", "section"), pairs)


def shift(block, pairs):
    return lax.ppermute(block, "section", pairs)


def scatter_sum(name, keep, send, spot):
    got = exchange(send, 1)
    part, half = keep.shape[0] // 4, keep.shape[1] // 2
    send_a, send_b, mine_a, mine_b = plain(
        sum_first, name + "_first", [spot, keep, got], [SM, VM, VM], [shape(2 * part, half)] * 4
    )
    got_a, got_b = exchange(send_a, 2), exchange(send_b, 4)
    send_a, send_b, last_a, last_b = plain(
        sum_second,
        name + "_second",
        [spot, mine_a, mine_b, got_a, got_b],
        [SM, VM, VM, VM, VM],
        [shape(part, half)] * 2 + [held(part, half, F32)] * 2,
    )
    return last_a, exchange(send_a, 4), last_b, exchange(send_b, 2)


def body(tokens, lengths, section_weights, norm_gains, cotangent):
    slab = pltpu.with_memory_space_constraint(section_weights[0], pltpu.HBM)
    gains = norm_gains[0]
    section = lax.axis_index("section")
    dp = lax.axis_size("dp")
    place = lax.axis_index("dp")
    split = dp == 8
    sec = section.astype(jnp.int32).reshape(1)
    core = (place % 2).astype(jnp.int32).reshape(1)
    spot = jnp.stack([(place // 2) % 2, (place // 4) % 2]).astype(jnp.int32)
    order = ((place % 2) * 2 + (place // 2 + place // 4) % 2).astype(jnp.int32).reshape(1)
    sec, core, spot, order, tokens = lax.optimization_barrier((sec, core, spot, order, tokens))
    total = tokens.shape[0]
    shard = D // dp
    sizes = SPLIT if sum(SPLIT) * ROWS == total else (1,) * (total // ROWS)
    bounds = []
    for size in sizes:
        first = bounds[-1][1] if bounds else 0
        bounds.append((first, first + size * ROWS))

    if split:
        piece = plain(
            take_columns,
            "take_columns",
            [sec, order, slab],
            [SM, SM, HB],
            [shape(D, FF // 4)],
            scratch=[pltpu.SemaphoreType.DMA((1,))],
        )[0]
    else:
        piece = lax.dynamic_slice(section_weights[0], (place * shard, 0), (shard, FF))
    piece = shift(piece, [(3, 2)])

    state = {}
    sent, sent_2, notes = [], [], []

    def run_first(mb, after=()):
        start, stop = bounds[mb]
        fresh = mb == 0
        kernel = functools.partial(first_forward, start, stop, fresh)
        message = shape(stop - start, D + SV)
        ins = [(sec, SM), (lengths, SM), (gains, VM), (tokens, VM)]
        if fresh:
            names = ["w", "left", "right", "qkv", "slope", "mid", "outs", "gg"]
            arrays = [
                held(D, ALL),
                held(total, 4 * D),
                held(total, ALL),
                held(total, 3 * D),
                held(total, FF),
                held(total, D, F32),
                held(total, D),
                held(8, D, F32),
            ]
            results = call(kernel, "first_forward", ins + [(slab, HB)], [], arrays + [message], 16)
        else:
            names = ["left", "right", "qkv", "slope", "mid"]
            ins += [(keep_in_vmem(state["w"]), VM)]
            results = call(
                kernel, "first_forward", ins, [state[n] for n in names], [message], after=after
            )
        state.update(zip(names, results))
        sent.append(shift(results[-1], [(0, 1)]))

    def run_second(mb, after=()):
        start, stop = bounds[mb]
        names = ["left", "qkv", "outs"]
        results = call(
            functools.partial(second_forward, start, stop),
            "second_forward",
            [(sec, SM), (lengths, SM), (gains, VM), (keep_in_vmem(state["w"]), VM), (sent[mb], VM)],
            [state[n] for n in names],
            [shape(stop - start, D)],
            after=after,
        )
        state.update(zip(names, results))
        sent_2.append(shift(results[-1], [(1, 2)]))

    def run_third(mb, after=()):
        start, stop = bounds[mb]
        names = ["left", "right", "slope"]
        results = call(
            functools.partial(third_forward, start, stop),
            "third_forward",
            [(sec, SM), (gains, VM), (keep_in_vmem(state["w"]), VM), (cotangent, VM), (sent_2[mb], VM)],
            [state[n] for n in names],
            [shape(8, 128, F32)],
            after=after,
        )
        state.update(zip(names, results))
        notes.append(results[-1])

    def halves():
        parts = plain(
            halve_rows,
            "halve_rows",
            [sec, piece],
            [SM, VM],
            [shape(D // 2, FF // 4)] * 2,
            after=[notes[0], sent[-1]],
        )
        return exchange_on(2, parts[0], 2), exchange_on(2, parts[1], 4)

    def gathered(from_x, from_y):
        mine = plain(
            gather_columns,
            "gather_columns",
            [sec, spot, piece, from_x, from_y],
            [SM, SM] + [VM] * 3,
            [shape(D, HALF)],
            after=[notes[-1]],
        )[0]
        return mine, exchange_on(2, mine, 1)

    if len(bounds) == 4 and split:
        run_first(0)
        run_first(1)
        run_first(2)
        run_second(0)
        run_first(3, after=[sent[1]])
        run_second(1, after=[sent[2]])
        run_second(2)
        run_third(0)
        sides = halves()
        run_second(3)
        run_third(1)
        run_third(2)
        run_third(3)
        mine, got = gathered(*sides)
    else:
        for run in (run_first, run_second, run_third):
            for mb in range(len(bounds)):
                run(mb)
        if split:
            mine, got = gathered(*halves())
        else:
            whole = lax.all_gather(piece, "dp", axis=0, tiled=True)
            parts = [whole[:, :HALF], whole[:, HALF:]]
            odd = place % 2 == 1
            mine = jnp.where(odd, parts[1], parts[0])
            got = jnp.where(odd, parts[0], parts[1])
    w = keep_in_vmem(state["w"])
    left, right, qkv, slope, mid, outs, gg = [
        state[n] for n in ("left", "right", "qkv", "slope", "mid", "outs", "gg")
    ]

    back_2 = []
    for start, stop in bounds:
        right, outs, gg, message = call(
            functools.partial(third_back, start, stop),
            "third_back",
            [(sec, SM), (core, SM), (gains, VM), (w, VM), (mine, VM), (got, VM)]
            + [(keep_in_vmem(slope), VM), (keep_in_vmem(left), VM)],
            [right, outs, gg],
            [shape(stop - start, D)],
        )
        back_2.append(shift(message, [(2, 1)]))

    back_1 = []
    for (start, stop), arrived in zip(bounds, back_2):
        right, gg, message = call(
            functools.partial(second_back, start, stop),
            "second_back",
            [(sec, SM), (lengths, SM), (gains, VM), (w, VM)]
            + [(keep_in_vmem(qkv), VM), (keep_in_vmem(outs), VM), (arrived, VM)],
            [right, gg],
            [shape(stop - start, D + SV)],
        )
        back_1.append(shift(message, [(1, 0)]))

    wide = None
    for (start, stop), arrived in zip(bounds, back_1):
        left, right, mid, gg = call(
            functools.partial(first_back_wide, start, stop),
            "first_back_wide",
            [(sec, SM), (gains, VM), (w, VM), (keep_in_vmem(slope), VM), (arrived, VM)],
            [left, right, mid, gg],
            [],
        )
        if stop == total:
            wide = products("wide_grads", left, right, core, R2, [2] * 4 + [3] * 4, split)
        right, outs, gg = call(
            functools.partial(first_back_attend, start, stop),
            "first_back_attend",
            [(sec, SM), (lengths, SM), (gains, VM), (tokens, VM), (w, VM)]
            + [(keep_in_vmem(qkv), VM), (keep_in_vmem(mid), VM), (arrived, VM)],
            [right, outs, gg],
            [],
        )
    narrow = products("narrow_grads", left, right, core, R0, [0] * 3 + [1], split)

    result = call(
        last_forward,
        "last_forward",
        [(sec, SM), (core, SM), (keep_in_vmem(left), VM), (keep_in_vmem(right), VM)]
        + [(mine, VM), (got, VM)],
        [],
        [shape(total, D)],
    )[0]
    result = shift(result, [(2, 3)])

    if split:
        wide_sum = scatter_sum("wide_sum", *wide, spot)
        narrow_sum = scatter_sum("narrow_sum", *narrow, spot)
        gain_total = gg[:2]
        for bit in (1, 2, 4):
            gain_total = gain_total + exchange(gain_total, bit)
        gain_out = lax.dynamic_slice(gain_total, (0, place * shard), (2, shard))
    else:
        wide_sum, narrow_sum = [
            lax.psum_scatter(part[0], "dp", scatter_dimension=0, tiled=True).astype(F32)
            for part in (wide, narrow)
        ]
        wide_sum, narrow_sum = [
            (s[:, : s.shape[1] // 2], blank, s[:, s.shape[1] // 2 :], blank)
            for s, blank in (
                (s, jnp.zeros((shard, s.shape[1] // 2), BF)) for s in (wide_sum, narrow_sum)
            )
        ]
        gain_out = lax.psum_scatter(gg[:2].T, "dp", scatter_dimension=0, tiled=True).T
    moved = shift((wide_sum[2] + wide_sum[3].astype(F32)).astype(BF), [(2, 3)])

    def kept(array):
        return keep_in_vmem(array) if array.dtype == F32 else array

    def last(*refs):
        finish(refs[0], refs[1:5], refs[5:9], *refs[9:])

    grads, rows = plain(
        last,
        "finish",
        [sec, *map(kept, wide_sum), *map(kept, narrow_sum), moved, outs, result],
        [SM] + [VM] * 11,
        [shape(shard, ALL, F32), shape(total, D)],
        16,
    )
    return (rows[None], grads[None], gain_out[None])


def solution(mesh):
    placed = (
        P("dp", None),
        P("dp", None),
        P("section", None, None),
        P("section", None, None),
        P("dp", None),
    )
    return jax.shard_map(
        body,
        mesh=mesh,
        in_specs=placed,
        out_specs=(P("section", "dp", None), P("section", "dp", None), P("section", None, "dp")),
        check_vma=False,
    )
```

```python
import functools

import jax
import jax.numpy as jnp
from jax import lax
from jax.experimental import pallas as pl
from jax.experimental.pallas import tpu as pltpu
from jax.sharding import PartitionSpec as P

D = 768
HD = 64
FF = 3072
SV = 384
ROWS = 112
PAIRS = 6
WIDE = 2 * HD
EPS = 1e-05
BF = jnp.bfloat16
F32 = jnp.float32

SPLIT = (1, 1, 1, 1)

L0, L1, L2, L3 = 0, D, 2 * D, 3 * D
R0, R1, R2 = 0, 3 * D, 4 * D
ALL = 4 * D + 2 * FF

QKV, OUT, UP, DOWN = 0, 3 * D, 4 * D, 4 * D + FF
FRESH = 2 * D + D - SV
HALF = FF // 2

VM = pl.BlockSpec(memory_space=pltpu.VMEM)
SM = pl.BlockSpec(memory_space=pltpu.SMEM)
HB = pl.BlockSpec(memory_space=pltpu.HBM)
ANY = pl.BlockSpec(memory_space=pl.ANY)


def dot(left, right):
    return jnp.dot(left, right, preferred_element_type=F32)


def dot_nt(left, right):
    return lax.dot_general(left, right, (((1,), (1,)), ((), ())), preferred_element_type=F32)


def normalized(rows):
    centered = rows - jnp.mean(rows, axis=-1, keepdims=True)
    spread = lax.rsqrt(jnp.mean(centered * centered, axis=-1, keepdims=True) + EPS)
    return centered * spread, spread


def norm_back(hat, spread, gain, grad):
    scaled = grad * gain
    inner = jnp.mean(scaled, axis=-1, keepdims=True)
    along = jnp.mean(scaled * hat, axis=-1, keepdims=True)
    return spread * (scaled - inner - hat * along)


def gelu_pair(u):
    c0 = 0.7978845608028654
    c1 = c0 * 0.044715
    square = u * u
    half = 0.5 + 0.5 * jnp.tanh(u * (c0 + c1 * square))
    act = u * half
    return act, half + act * ((1.0 - half) * (2.0 * c0 + (6.0 * c1) * square))


def sequence_start(lengths, bucket, i):
    e0 = lengths[bucket, 0]
    e1 = e0 + lengths[bucket, 1]
    e2 = e1 + lengths[bucket, 2]
    return jnp.where(i >= e2, e2, jnp.where(i >= e1, e1, jnp.where(i >= e0, e0, 0)))


def bias_rows(lengths, bucket):
    i = lax.broadcasted_iota(jnp.int32, (ROWS, ROWS), 0)
    j = lax.broadcasted_iota(jnp.int32, (ROWS, ROWS), 1)
    bias = jnp.where((j <= i) & (j >= sequence_start(lengths, bucket, i)), 0.0, -1e30)
    return jnp.concatenate([bias, bias], axis=0)


def bias_columns(lengths, bucket):
    j = lax.broadcasted_iota(jnp.int32, (ROWS, 2 * ROWS), 0)
    i = lax.broadcasted_iota(jnp.int32, (ROWS, 2 * ROWS), 1)
    i = jnp.where(i >= ROWS, i - ROWS, i)
    return jnp.where((j <= i) & (j >= sequence_start(lengths, bucket, i)), 0.0, -1e30)


def lane_masks(scale):
    low = lax.broadcasted_iota(jnp.int32, (ROWS, WIDE), 1) < HD
    return jnp.where(low, scale, 0.0).astype(BF), jnp.where(low, 0.0, scale).astype(BF)


def two_heads(block, masks):
    return jnp.concatenate([block * masks[0], block * masks[1]], axis=0)


def joined(stacked):
    low = lax.broadcasted_iota(jnp.int32, (ROWS, WIDE), 1) < HD
    return jnp.where(low, stacked[:ROWS], stacked[ROWS:])


def softmax(scores, axis):
    top = jnp.max(scores, axis=axis, keepdims=True)
    powers = jnp.exp(scores - top)
    return powers * (1.0 / jnp.sum(powers, axis=axis, keepdims=True))


def attention(qkv, rows, bias, put):
    masks = lane_masks(HD ** (-0.5))
    at = [WIDE * p for p in range(PAIRS)]
    scores = [
        dot_nt(two_heads(qkv[rows, c : c + WIDE], masks), qkv[rows, D + c : D + c + WIDE]) + bias
        for c in at
    ]
    probs = [softmax(s, -1).astype(BF) for s in scores]
    for c, p in zip(at, probs):
        put(c, joined(dot(p, qkv[rows, 2 * D + c : 2 * D + c + WIDE])))


def attention_back(qkv, rows, grad, bias, put):
    scaled = lane_masks(HD ** (-0.5))
    plain = lane_masks(1.0)
    at = [WIDE * p for p in range(PAIRS)]
    qs = [two_heads(qkv[rows, c : c + WIDE], scaled) for c in at]
    ks = [qkv[rows, D + c : D + c + WIDE] for c in at]
    vs = [qkv[rows, 2 * D + c : 2 * D + c + WIDE] for c in at]
    gs = [two_heads(grad[:, c : c + WIDE], plain) for c in at]
    scores = [dot_nt(k, q) + bias for k, q in zip(ks, qs)]
    grad_probs = [dot_nt(v, g) for v, g in zip(vs, gs)]
    probs = [softmax(s, 0) for s in scores]
    inner = [jnp.sum(d * p, axis=0, keepdims=True) for d, p in zip(grad_probs, probs)]
    grad_scores = [(p * (d - i)).astype(BF) for p, d, i in zip(probs, grad_probs, inner)]
    grad_v = [dot(p.astype(BF), g) for p, g in zip(probs, gs)]
    grad_k = [dot(s, q) for s, q in zip(grad_scores, qs)]
    turned = [s.T for s in grad_scores]
    grad_q = [joined(dot(t, k)) * HD ** (-0.5) for t, k in zip(turned, ks)]
    for c, dq, dk, dv in zip(at, grad_q, grad_k, grad_v):
        put(c, dq, dk, dv)


def buckets_of(start, stop):
    return [(b // ROWS, slice(b, b + ROWS)) for b in range(start, stop, ROWS)]


class Loads:
    def __init__(self, sems):
        self.sems = sems
        self.used = 0

    def start(self, src, dst):
        copy = pltpu.make_async_copy(src, dst, self.sems.at[self.used])
        self.used += 1
        copy.start()
        return copy


def forward_wide(left, store, slope, rows, w, up, down, chunk, waits=None):
    count = FF // chunk

    def lift(c):
        if waits:
            waits[0][c].wait()
        return dot(left[rows, L2 : L2 + D], w[:, up + c * chunk : up + (c + 1) * chunk])

    total = None
    here = lift(0)
    for c in range(count):
        ahead = lift(c + 1) if c + 1 < count else None
        act, gradient = gelu_pair(here)
        act = act.astype(BF)
        store[rows, c * chunk : (c + 1) * chunk] = act
        slope[rows, c * chunk : (c + 1) * chunk] = gradient.astype(BF)
        if down is not None:
            if waits:
                waits[1][c].wait()
            part = dot_nt(act, w[:, down + c * chunk : down + (c + 1) * chunk])
            total = part if total is None else total + part
        here = ahead
    return total


CHUNK = 512
COST = 1000


def first_forward(start, stop, fresh, sec, lengths, gains, tokens, *refs):
    if fresh:
        slab, refs = refs[0], refs[1:]
        w, left, acts, qkv, slope, mid, right, outs, gg, message, sems = refs
        gg[...] = jnp.zeros_like(gg)
    else:
        w, refs = refs[0], refs[1:]
        left, acts, qkv, slope, mid, message, sems = refs[5:]
    rows = slice(start, stop)
    if fresh:

        @pl.when((sec[0] == 1) | (sec[0] == 2))
        def _():
            loads = Loads(sems)
            both = [
                loads.start(slab.at[:, pl.ds(at, HALF)], w.at[:, pl.ds(at, HALF)])
                for at in (0, HALF)
            ]
            for load in both:
                load.wait()

    @pl.when(sec[0] == 0)
    def _():
        loads = Loads(sems)
        first = second = waits = None
        if fresh:

            def get(at, wide):
                return loads.start(slab.at[:, pl.ds(at, wide)], w.at[:, pl.ds(at, wide)])

            first = [get(QKV + c * D, D) for c in range(3)]
            second = get(OUT, D)
            waits = ([], [])
            for c in range(FF // CHUNK):
                waits[0].append(get(UP + c * CHUNK, CHUNK))
                waits[1].append(get(DOWN + c * CHUNK, CHUNK))
        x = tokens[rows, :].astype(F32)
        low = (normalized(x)[0] * gains[0:1, :]).astype(BF)
        left[rows, L0 : L0 + D] = low
        for c in range(3):
            if fresh:
                first[c].wait()
            qkv[rows, c * D : (c + 1) * D] = dot(low, w[:, QKV + c * D : QKV + (c + 1) * D]).astype(BF)
        message[:, D:] = qkv[rows, 2 * D : 2 * D + SV]
        for bucket, here in buckets_of(start, stop):

            def put(c, value):
                left[here, L1 + c : L1 + c + WIDE] = value.astype(BF)

            attention(qkv, here, bias_rows(lengths, bucket), put)
        if fresh:
            second.wait()
        middle = x + dot(left[rows, L1 : L1 + D], w[:, OUT : OUT + D])
        mid[rows, :] = middle
        left[rows, L2 : L2 + D] = (normalized(middle)[0] * gains[1:2, :]).astype(BF)
        total = forward_wide(left, acts, slope, rows, w, UP, DOWN, CHUNK, waits)
        message[:, :D] = (middle + total).astype(BF)


def second_forward(start, stop, sec, lengths, gains, w, arrived, *refs):
    left, qkv, outs, message, sems = refs[3:]
    rows = slice(start, stop)

    @pl.when(sec[0] == 1)
    def _():
        outs[rows, :] = arrived[:, :D]
        x = arrived[:, :D].astype(F32)
        low = (normalized(x)[0] * gains[0:1, :]).astype(BF)
        left[rows, L0 : L0 + D] = low
        mixed = dot(low, w[:, :FRESH]).astype(BF)
        qkv[rows, : 2 * D] = mixed[:, : 2 * D]
        qkv[rows, 2 * D : 2 * D + SV] = arrived[:, D:]
        qkv[rows, 2 * D + SV :] = mixed[:, 2 * D :]
        for bucket, here in buckets_of(start, stop):

            def put(c, value):
                left[here, L1 + c : L1 + c + WIDE] = value.astype(BF)

            attention(qkv, here, bias_rows(lengths, bucket), put)
        message[...] = (x + dot(left[rows, L1 : L1 + D], w[:, FRESH : FRESH + D])).astype(BF)


def third_forward(start, stop, sec, gains, w, cot, arrived, *refs):
    left, right, slope, token, sems = refs[3:]
    rows = slice(start, stop)
    token[...] = jnp.zeros_like(token)

    @pl.when(sec[0] == 2)
    def _():
        left[rows, L1 : L1 + D] = arrived[...]
        left[rows, L3 : L3 + D] = cot[rows, :]
        hat = normalized(arrived[...].astype(F32))[0]
        left[rows, L2 : L2 + D] = (hat * gains[0:1, :]).astype(BF)
        forward_wide(left, right, slope, rows, w, 0, None, CHUNK)


def third_back_half(left, right, slope, w, other, which, rows):
    back = None
    for k in range(0, HALF, D):
        at = pl.multiple_of(which * HALF + k, 128)
        grad = dot(left[rows, L3 : L3 + D], other[:, k : k + D]).astype(BF).astype(F32)
        lifted = (slope[rows, pl.ds(at, D)].astype(F32) * grad).astype(BF)
        right[rows, pl.ds(pl.multiple_of(R2 + at, 128), D)] = lifted
        part = dot_nt(lifted, w[:, pl.ds(at, D)])
        back = part if back is None else back + part
    return back


def third_back_first(sec, core, w, mine, slope, left, *refs):
    right, mid, sems = refs[2:]

    @pl.when(sec[0] == 2)
    def _():
        for start in range(0, left.shape[0], 2 * ROWS):
            rows = slice(start, start + 2 * ROWS)
            mid[rows, :] = third_back_half(left, right, slope, w, mine, core[0], rows)


def third_back(start, stop, sec, core, gains, w, got, slope, left, mid, *refs):
    right, outs, gg, message, sems = refs[3:]
    rows = slice(start, stop)

    @pl.when(sec[0] == 2)
    def _():
        back = mid[rows, :] + third_back_half(left, right, slope, w, got, 1 - core[0], rows)
        hat, spread = normalized(left[rows, L1 : L1 + D].astype(F32))
        gg[0:1, :] += jnp.sum(back * hat, axis=0, keepdims=True)
        c = left[rows, L3 : L3 + D].astype(F32)
        resid = (c + norm_back(hat, spread, gains[0:1, :], back)).astype(BF)
        message[...] = resid
        outs[rows, :] = resid


def second_back(start, stop, sec, lengths, gains, w, qkv, outs, arrived, *refs):
    left, right, gg, message, sems = refs[3:]
    rows = slice(start, stop)

    @pl.when(sec[0] == 1)
    def _():
        right[rows, R1 : R1 + D] = arrived[...]
        grad = dot_nt(arrived[...], w[:, FRESH : FRESH + D]).astype(BF)
        for bucket, here in buckets_of(start, stop):
            local = slice(here.start - start, here.stop - start)

            def put(c, dq, dk, dv):
                right[here, R0 + c : R0 + c + WIDE] = dq.astype(BF)
                right[here, R0 + D + c : R0 + D + c + WIDE] = dk.astype(BF)
                if c < SV:
                    message[local, D + c : D + c + WIDE] = dv.astype(BF)
                else:
                    right[here, R0 + 2 * D + c - SV : R0 + 2 * D + c - SV + WIDE] = dv.astype(BF)

            attention_back(qkv, here, grad[local], bias_columns(lengths, bucket), put)
        back = dot_nt(right[rows, R0 : R0 + FRESH], w[:, :FRESH])
        hat, spread = normalized(outs[rows, :].astype(F32))
        gg[0:1, :] += jnp.sum(back * hat, axis=0, keepdims=True)
        resid = arrived[...].astype(F32) + norm_back(hat, spread, gains[0:1, :], back)
        message[:, :D] = resid.astype(BF)
        left[rows, L3 : L3 + D] = resid.astype(BF)


def first_back_wide(start, stop, sec, gains, w, slope, arrived, *refs):
    right, mid, gg, sems = refs[3:]
    rows = slice(start, stop)

    @pl.when(sec[0] == 0)
    def _():
        grad = arrived[:, :D]
        back = None
        pulled = dot(grad, w[:, DOWN : DOWN + CHUNK])
        for c in range(FF // CHUNK):
            k = c * CHUNK
            ahead = None
            if k + CHUNK < FF:
                ahead = dot(grad, w[:, DOWN + k + CHUNK : DOWN + k + 2 * CHUNK])
            lifted = (slope[rows, k : k + CHUNK].astype(F32) * pulled).astype(BF)
            right[rows, R2 + k : R2 + k + CHUNK] = lifted
            part = dot_nt(lifted, w[:, UP + k : UP + k + CHUNK])
            back = part if back is None else back + part
            pulled = ahead
        hat, spread = normalized(mid[rows, :])
        gg[1:2, :] += jnp.sum(back * hat, axis=0, keepdims=True)
        resid = grad.astype(F32) + norm_back(hat, spread, gains[1:2, :], back)
        right[rows, R1 : R1 + D] = resid.astype(BF)
        mid[rows, :] = resid


def first_back_attend(start, stop, sec, lengths, gains, tokens, w, qkv, mid, arrived, *refs):
    right, outs, gg, sems = refs[3:]
    rows = slice(start, stop)

    @pl.when(sec[0] == 0)
    def _():
        grad = dot_nt(right[rows, R1 : R1 + D], w[:, OUT : OUT + D]).astype(BF)
        for bucket, here in buckets_of(start, stop):
            local = slice(here.start - start, here.stop - start)

            def put(c, dq, dk, dv):
                right[here, R0 + c : R0 + c + WIDE] = dq.astype(BF)
                right[here, R0 + D + c : R0 + D + c + WIDE] = dk.astype(BF)
                if c < SV:
                    dv = dv + arrived[local, D + c : D + c + WIDE].astype(F32)
                right[here, R0 + 2 * D + c : R0 + 2 * D + c + WIDE] = dv.astype(BF)

            attention_back(qkv, here, grad[local], bias_columns(lengths, bucket), put)
        back = dot_nt(right[rows, R0 : R0 + 3 * D], w[:, QKV : QKV + 3 * D])
        hat, spread = normalized(tokens[rows, :].astype(F32))
        gg[0:1, :] += jnp.sum(back * hat, axis=0, keepdims=True)
        outs[rows, :] = (mid[rows, :] + norm_back(hat, spread, gains[0:1, :], back)).astype(BF)


def last_forward(sec, core, mine, got, _l, _r, left, right, result, sems):
    @pl.when(sec[0] == 2)
    def _():
        total = left[:, L1 : L1 + D].astype(F32)
        for other, which in ((mine, core[0]), (got, 1 - core[0])):
            at = pl.multiple_of(which * HALF, 128)
            total = total + dot_nt(right[:, pl.ds(at, HALF)], other[...])
        result[...] = total.astype(BF)


def take_acts(sec, arrived, _r, right, sems):
    @pl.when(sec[0] == 1)
    def _():
        right[:, R2:] = arrived[...]


def same_acts(sec, _a, acts, sems):
    pass


def take_columns(sec, order, slab, piece, sems):
    @pl.when(sec[0] == 3)
    def _():
        wide = piece.shape[1]
        at = pl.multiple_of(order[0] * wide, 128)
        Loads(sems).start(slab.at[:, pl.ds(at, wide)], piece).wait()


def halve_rows(sec, piece, upper, lower):
    @pl.when(sec[0] == 2)
    def _():
        upper[...] = piece[: D // 2]
        lower[...] = piece[D // 2 :]


def gather_columns(sec, spot, piece, from_x, from_y, merged):
    @pl.when(sec[0] == 2)
    def _():
        wide = piece.shape[1]
        odd = (spot[0] + spot[1]) % 2
        merged[:, pl.ds(pl.multiple_of(odd * wide, 128), wide)] = piece[...]
        other = pl.ds(pl.multiple_of((1 - odd) * wide, 128), wide)
        merged[: D // 2, other] = from_x[...]
        merged[D // 2 :, other] = from_y[...]


def by_core(core, whole, keep, send):
    wide = whole.shape[0] // 8
    for k in range(4):
        here = slice(k * wide, (k + 1) * wide)
        keep[here, :] = whole[pl.ds(pl.multiple_of((2 * k + core) * wide, wide), wide), :]
        send[here, :] = whole[pl.ds(pl.multiple_of((2 * k + 1 - core) * wide, wide), wide), :]


def shares(roles, extra, again, sec, core, gg, *refs):
    left, right, keep, send, sems, turned, whole = refs[3 if again else 2 :]

    def run(first, groups):
        before = None
        for j, group in enumerate(groups):
            if group != before:
                turned[...] = left[:, group * D : (group + 1) * D].T
            before = group
            whole[...] = dot(turned[...], right[:, first + j * D : first + (j + 1) * D]).astype(BF)
            cols = pl.ds(j * D, D)
            by_core(core[0], whole, keep.at[:, cols], send.at[:, cols])
        if extra:
            block = whole.at[:, pl.ds(0, 256)]
            block[...] = jnp.zeros((D, 256), BF)
            block[:, :8] = gg[...].T.astype(BF)
            cols = pl.ds(len(groups) * D, 256)
            by_core(core[0], block, keep.at[:, cols], send.at[:, cols])

    for part, (first, groups) in roles.items():
        pl.when(sec[0] == part)(functools.partial(run, first, groups))


def sum_first(spot, keep, got, send_a, send_b, mine_a, mine_b):
    part, half = send_a.shape[0] // 2, send_a.shape[1]
    x, y = spot[0], spot[1]

    def both(where, lo):
        rows = pl.ds(pl.multiple_of(where * part, part), part)
        cols = slice(lo, lo + half)
        return (keep[rows, cols].astype(F32) + got[rows, cols].astype(F32)).astype(BF)

    for k in range(2):
        here = slice(k * part, (k + 1) * part)
        send_a[here, :] = both(2 * k + 1 - x, 0)
        send_b[here, :] = both(2 * (1 - y) + k, half)
        mine_a[here, :] = both(2 * k + x, 0)
        mine_b[here, :] = both(2 * y + k, half)


def sum_second(spot, mine_a, mine_b, got_a, got_b, send_a, send_b, last_a, last_b):
    part = send_a.shape[0]
    x, y = spot[0], spot[1]

    def both(mine, got, where):
        rows = pl.ds(pl.multiple_of(where * part, part), part)
        return mine[rows, :].astype(F32) + got[rows, :].astype(F32)

    send_a[...] = both(mine_a, got_a, 1 - y).astype(BF)
    send_b[...] = both(mine_b, got_b, 1 - x).astype(BF)
    last_a[...] = both(mine_a, got_a, y).astype(BF)
    last_b[...] = both(mine_b, got_b, x).astype(BF)


def sum_last(last_a, got_a, last_b, got_b, total):
    half = last_a.shape[1]
    total[:, :half] = (last_a[...].astype(F32) + got_a[...].astype(F32)).astype(total.dtype)
    total[:, half:] = (last_b[...].astype(F32) + got_b[...].astype(F32)).astype(total.dtype)


def finish(sec, wide, narrow, moved, outs, result, grads, rows, gains):
    count = grads.shape[0]
    blank = functools.partial(jnp.zeros, dtype=F32)

    def total(four, lo, hi):
        half = four[0].shape[1]
        pieces = []
        for at in range(2):
            first, last = max(lo - at * half, 0), min(hi - at * half, half)
            if first < last:
                one, two = four[2 * at][:, first:last], four[2 * at + 1][:, first:last]
                pieces.append((at * half + first, one.astype(F32) + two.astype(F32)))
        return pieces

    def lay(four, lo, hi, to):
        for at, value in total(four, lo, hi):
            grads[:, to + at - lo : to + at - lo + value.shape[1]] = value

    def lay_gains(four):
        ((_, block),) = total(four, 4 * D, 4 * D + 128)
        gains[...] = block.T[:2]

    @pl.when(sec[0] == 0)
    def _():
        lay(narrow, 0, 4 * D, 0)
        lay(wide, 0, FF, UP)
        grads[:, DOWN:] = moved[...].astype(F32)
        lay_gains(narrow)

    @pl.when(sec[0] == 1)
    def _():
        lay(narrow, 0, FRESH, 0)
        lay(narrow, 3 * D, 4 * D, FRESH)
        grads[:, FRESH + D :] = blank((count, ALL - FRESH - D))
        lay_gains(narrow)

    @pl.when(sec[0] == 2)
    def _():
        lay(narrow, 0, FF, 0)
        grads[:, FF:] = blank((count, ALL - FF))
        lay_gains(narrow)

    @pl.when(sec[0] == 3)
    def _():
        grads[:, :FF] = moved[...].astype(F32)
        grads[:, FF:] = blank((count, ALL - FF))
        gains[...] = jnp.zeros_like(gains)
        rows[...] = result[...]

    @pl.when(sec[0] != 3)
    def _():
        rows[...] = outs[...]


def shape(rows, cols, dtype=BF):
    return jax.ShapeDtypeStruct((rows, cols), dtype)


def held(rows, cols, dtype=BF):
    return pltpu.VMEM((rows, cols), dtype)


def keep_in_vmem(array):
    return pltpu.with_memory_space_constraint(array, pltpu.VMEM)


def call(kernel, name, ins, states, outs, sems=1, scratch=(), after=(), limit=8, specs=None):
    operands = [a for a, _ in ins] + [keep_in_vmem(s) for s in states]
    aliases = {len(ins) + i: i for i in range(len(states))}
    out_shape = [held(*s.shape, s.dtype) for s in states] + list(outs)
    return pl.pallas_call(
        behind(kernel, len(operands), after),
        name=name,
        out_shape=out_shape,
        in_specs=[s for _, s in ins] + [VM] * len(states) + [ANY] * len(after),
        out_specs=[VM] * len(states) + list(specs or [VM] * len(outs)),
        scratch_shapes=[pltpu.SemaphoreType.DMA((sems,))] + list(scratch),
        input_output_aliases=aliases,
        compiler_params=pltpu.CompilerParams(vmem_limit_bytes=limit << 20),
        cost_estimate=pl.CostEstimate(flops=COST, bytes_accessed=1024, transcendentals=0),
    )(*operands, *after)


def behind(kernel, count, after):
    def ordered(*refs):
        kernel(*refs[:count], *refs[count + len(after) :])

    return ordered


def plain(kernel, name, operands, specs, outs, limit=8, scratch=(), after=()):
    return pl.pallas_call(
        behind(kernel, len(operands), after),
        name=name,
        out_shape=outs,
        in_specs=specs + [ANY] * len(after),
        out_specs=[VM] * len(outs),
        scratch_shapes=list(scratch),
        compiler_params=pltpu.CompilerParams(vmem_limit_bytes=limit << 20),
        cost_estimate=pl.CostEstimate(flops=COST, bytes_accessed=1024, transcendentals=0),
    )(*operands, *after)


def exchange_on(parts, block, bit):
    count, sections = lax.axis_size("dp"), lax.axis_size("section")
    pairs = [(i * sections + p, (i ^ bit) * sections + p) for p in parts for i in range(count)]
    return lax.ppermute(block, ("dp", "section"), pairs)


def shift(block, pairs):
    return lax.ppermute(block, "section", pairs)


def scatter_sum(name, parts, keep, got, sec, spot):
    swap = functools.partial(exchange_on, parts)
    part, half = keep.shape[0] // 4, keep.shape[1] // 2
    pairs = len(got) == 2

    def only(kernel):
        def run(sec_ref, *refs):
            mine = sec_ref[0] == parts[0]
            for p in parts[1:]:
                mine = mine | (sec_ref[0] == p)

            @pl.when(mine)
            def _():
                kernel(*refs)

        return run

    def first(sec_ref, spot_ref, keep_ref, *refs):
        if not pairs:
            only(sum_first)(sec_ref, spot_ref, keep_ref, *refs)
            return
        here, there, *outs = refs

        @pl.when(sec_ref[0] == 0)
        def _():
            sum_first(spot_ref, keep_ref, here, *outs)

        @pl.when((sec_ref[0] == 1) | (sec_ref[0] == 2))
        def _():
            sum_first(spot_ref, keep_ref, there, *outs)

    send_a, send_b, mine_a, mine_b = plain(
        first,
        name + "_first",
        [sec, spot, keep, *got],
        [SM, SM, VM] + [VM] * len(got),
        [shape(2 * part, half)] * 4,
        12,
    )
    got_a, got_b = swap(send_a, 2), swap(send_b, 4)
    send_a, send_b, last_a, last_b = plain(
        only(sum_second),
        name + "_second",
        [sec, spot, mine_a, mine_b, got_a, got_b],
        [SM, SM, VM, VM, VM, VM],
        [shape(part, half)] * 4,
    )
    return (last_a, swap(send_a, 4), last_b, swap(send_b, 2)), (got_a, got_b)


def body(tokens, lengths, section_weights, norm_gains, cotangent):
    slab = pltpu.with_memory_space_constraint(section_weights[0], pltpu.HBM)
    gains = norm_gains[0]
    section = lax.axis_index("section")
    dp = lax.axis_size("dp")
    place = lax.axis_index("dp")
    split = dp == 8
    sec = section.astype(jnp.int32).reshape(1)
    core = (place % 2).astype(jnp.int32).reshape(1)
    spot = jnp.stack([(place // 2) % 2, (place // 4) % 2]).astype(jnp.int32)
    order = ((place % 2) * 2 + (place // 2 + place // 4) % 2).astype(jnp.int32).reshape(1)
    sec, core, spot, order, tokens = lax.optimization_barrier((sec, core, spot, order, tokens))
    total = tokens.shape[0]
    shard = D // dp
    sizes = SPLIT if sum(SPLIT) * ROWS == total else (1,) * (total // ROWS)
    bounds = []
    for size in sizes:
        first = bounds[-1][1] if bounds else 0
        bounds.append((first, first + size * ROWS))

    if split:
        piece = plain(
            take_columns,
            "take_columns",
            [sec, order, slab],
            [SM, SM, HB],
            [shape(D, FF // 4)],
            scratch=[pltpu.SemaphoreType.DMA((1,))],
        )[0]
    else:
        piece = lax.dynamic_slice(section_weights[0], (place * shard, 0), (shard, FF))
    piece = shift(piece, [(3, 2)])

    state = {}
    sent, sent_2, notes, made = [], [], [], []

    def run_first(mb, after=()):
        start, stop = bounds[mb]
        fresh = mb == 0
        kernel = functools.partial(first_forward, start, stop, fresh)
        message = shape(stop - start, D + SV)
        ins = [(sec, SM), (lengths, SM), (gains, VM), (tokens, VM)]
        if fresh:
            names = ["w", "left", "acts", "qkv", "slope", "mid", "right", "outs", "gg"]
            arrays = [
                held(D, ALL),
                held(total, 4 * D),
                held(total, FF),
                held(total, 3 * D),
                held(total, FF),
                held(total, D, F32),
                held(total, 4 * D + FF),
                held(total, D),
                held(8, D, F32),
            ]
            results = call(kernel, "first_forward", ins + [(slab, HB)], [], arrays + [message], 16)
        else:
            names = ["left", "acts", "qkv", "slope", "mid"]
            ins += [(keep_in_vmem(state["w"]), VM)]
            results = call(
                kernel, "first_forward", ins, [state[n] for n in names], [message], after=after
            )
        state.update(zip(names, results))
        sent.append(shift(results[-1], [(0, 1)]))

    def send_acts():
        acts = call(same_acts, "same_acts", [(sec, SM)], [state["acts"]], [], after=[sent[-1]])[0]
        return acts, shift(acts, [(0, 1)])

    def run_second(mb, after=()):
        start, stop = bounds[mb]
        names = ["left", "qkv", "outs"]
        results = call(
            functools.partial(second_forward, start, stop),
            "second_forward",
            [(sec, SM), (lengths, SM), (gains, VM), (keep_in_vmem(state["w"]), VM), (sent[mb], VM)],
            [state[n] for n in names],
            [shape(stop - start, D)],
            after=after,
        )
        state.update(zip(names, results))
        made.append(results[-1])
        sent_2.append(shift(results[-1], [(1, 2)]))

    def run_third(mb, after=()):
        start, stop = bounds[mb]
        names = ["left", "right", "slope"]
        results = call(
            functools.partial(third_forward, start, stop),
            "third_forward",
            [(sec, SM), (gains, VM), (keep_in_vmem(state["w"]), VM), (cotangent, VM), (sent_2[mb], VM)],
            [state[n] for n in names],
            [shape(8, 128, F32)],
            after=after,
        )
        state.update(zip(names, results))
        notes.append(results[-1])

    def halves():
        parts = plain(
            halve_rows,
            "halve_rows",
            [sec, piece],
            [SM, VM],
            [shape(D // 2, FF // 4)] * 2,
            after=[sent[-1], made[-1], sent_2[0]],
        )
        return exchange_on([2], parts[0], 2), exchange_on([2], parts[1], 4)

    def gathered(from_x, from_y):
        mine = plain(
            gather_columns,
            "gather_columns",
            [sec, spot, piece, from_x, from_y],
            [SM, SM] + [VM] * 3,
            [shape(D, HALF)],
            after=[notes[-1]],
        )[0]
        return mine, exchange_on([2], mine, 1)

    if len(bounds) == 4 and split:
        run_first(0)
        run_first(1)
        run_first(2)
        run_second(0)
        run_first(3, after=[sent[1]])
        run_second(1, after=[sent[2]])
        run_second(2)
        sides = halves()
        run_third(0)
        acts, sent_acts = send_acts()
        run_second(3, after=[acts])
        run_third(1)
        run_third(2)
        run_third(3)
        mine, got = gathered(*sides)
    else:
        for run in (run_first, run_second, run_third):
            for mb in range(len(bounds)):
                run(mb)
            if run is run_first:
                _, sent_acts = send_acts()
        if split:
            mine, got = gathered(*halves())
        else:
            whole = lax.all_gather(piece, "dp", axis=0, tiled=True)
            parts = [whole[:, :HALF], whole[:, HALF:]]
            odd = place % 2 == 1
            mine = jnp.where(odd, parts[1], parts[0])
            got = jnp.where(odd, parts[0], parts[1])
    w = keep_in_vmem(state["w"])
    back_2, back_1 = [], []

    state["right"], state["mid"] = call(
        third_back_first,
        "third_back_first",
        [(sec, SM), (core, SM), (w, VM), (keep_in_vmem(mine), VM)]
        + [(keep_in_vmem(state[n]), VM) for n in ("slope", "left")],
        [state["right"], state["mid"]],
        [],
    )

    def run_third_back(mb):
        start, stop = bounds[mb]
        names = ["right", "outs", "gg"]
        results = call(
            functools.partial(third_back, start, stop),
            "third_back",
            [(sec, SM), (core, SM), (gains, VM), (w, VM)]
            + [(keep_in_vmem(a), VM) for a in (got, state["slope"], state["left"], state["mid"])],
            [state[n] for n in names],
            [shape(stop - start, D)],
        )
        state.update(zip(names, results))
        back_2.append(shift(results[-1], [(2, 1)]))

    def run_second_back(mb):
        start, stop = bounds[mb]
        names = ["left", "right", "gg"]
        results = call(
            functools.partial(second_back, start, stop),
            "second_back",
            [(sec, SM), (lengths, SM), (gains, VM), (w, VM)]
            + [(keep_in_vmem(state["qkv"]), VM), (keep_in_vmem(state["outs"]), VM), (back_2[mb], VM)],
            [state[n] for n in names],
            [shape(stop - start, D + SV)],
        )
        state.update(zip(names, results))
        back_1.append(shift(results[-1], [(1, 0)]))

    for run in (run_third_back, run_second_back):
        for mb in range(len(bounds)):
            run(mb)
    left, right, qkv, slope, mid, outs, gg = [
        state[n] for n in ("left", "right", "qkv", "slope", "mid", "outs", "gg")
    ]

    def own_shares(name, roles, extra, left, right, keep=None, after=()):
        width = 4 * D + (256 if extra else 0)
        rows = held(D // 2, width)
        states = [left, right] + ([] if keep is None else [keep])
        return call(
            functools.partial(shares, roles, extra, keep is not None),
            name,
            [(sec, SM), (core, SM), (keep_in_vmem(gg), VM)],
            states,
            [rows] * (2 if keep is None else 1),
            scratch=[pltpu.VMEM((D, total), BF), pltpu.VMEM((D, D), BF)],
            after=after,
        )

    def plain_sums(roles, extra):
        width = 4 * D + (256 if extra else 0)
        full = jnp.zeros((D, width), BF)
        for part, (first, groups) in roles.items():
            blocks = [
                lax.dot_general(
                    left[:, g * D : (g + 1) * D],
                    right[:, first + j * D : first + (j + 1) * D],
                    (((0,), (0,)), ((), ())),
                    preferred_element_type=F32,
                ).astype(BF)
                for j, g in enumerate(groups)
            ]
            if extra:
                blocks += [gg.T.astype(BF), jnp.zeros((D, 248), BF)]
            full = jnp.where(section == part, jnp.concatenate(blocks, axis=1), full)
        full = lax.psum_scatter(full, "dp", scatter_dimension=0, tiled=True)
        blank = jnp.zeros((shard, width // 2), BF)
        return full[:, : width // 2], blank, full[:, width // 2 :], blank

    def run_wide(mb):
        start, stop = bounds[mb]
        return call(
            functools.partial(first_back_wide, start, stop),
            "first_back_wide",
            [(sec, SM), (gains, VM), (w, VM), (keep_in_vmem(slope), VM), (back_1[mb], VM)],
            [right, mid, gg],
            [],
        )

    def run_attend(mb, after=()):
        start, stop = bounds[mb]
        return call(
            functools.partial(first_back_attend, start, stop),
            "first_back_attend",
            [(sec, SM), (lengths, SM), (gains, VM), (tokens, VM), (w, VM)]
            + [(keep_in_vmem(qkv), VM), (keep_in_vmem(mid), VM), (back_1[mb], VM)],
            [right, outs, gg],
            [],
            after=after,
        )

    up_roles = {0: (R2, [2] * 4)}
    down_roles = {1: (R2, [3] * 4), 2: (0, [3] * 4)}
    narrow_roles = {0: (R0, [0] * 3 + [1]), 1: (R0, [0] * 3 + [1]), 2: (R2, [2] * 4)}
    count = len(bounds)
    late = max(count - 2, 0)
    for mb in range(count):
        right, mid, gg = run_wide(mb)
        if mb < late:
            right, outs, gg = run_attend(mb)
    if split:
        left, right, keep, send = own_shares("up_grads", up_roles, False, left, right)
        got_up = exchange_on([0], send, 1)
    for mb in range(late, count):
        right, outs, gg = run_attend(mb)
    right = call(take_acts, "take_acts", [(sec, SM), (sent_acts, VM)], [right], [])[0]
    left, right, result = call(
        last_forward,
        "last_forward",
        [(sec, SM), (core, SM), (mine, VM), (got, VM)],
        [left, right],
        [shape(total, D)],
        limit=12,
    )
    result = shift(result, [(2, 3)])
    if split:
        left, right, keep, send = own_shares("down_grads", down_roles, False, left, right, keep)
        got_down = exchange_on([1, 2], send, 1)
        wide, begun = scatter_sum("wide_sum", [0, 1, 2], keep, [got_up, got_down], sec, spot)
        left, right, keep, send = own_shares("narrow_grads", narrow_roles, True, left, right)
        got_narrow = exchange_on([0, 1, 2], send, 1)
        narrow, _ = scatter_sum("narrow_sum", [0, 1, 2], keep, [got_narrow], sec, spot)
    else:
        wide = plain_sums({**up_roles, **down_roles}, False)
        narrow = plain_sums(narrow_roles, True)
    moved = plain(sum_last, "wide_grads_last", list(wide), [VM] * 4, [shape(shard, FF)])[0]
    moved = shift(moved, [(1, 0), (2, 3)])

    def last(*refs):
        finish(refs[0], refs[1:5], refs[5:9], *refs[9:])

    grads, rows, gain_out = plain(
        last,
        "finish",
        [sec, *wide, *narrow, moved, outs, result],
        [SM] + [VM] * 11,
        [shape(shard, ALL, F32), shape(total, D), shape(2, shard, F32)],
        16,
    )
    return (rows[None], grads[None], gain_out[None])


def solution(mesh):
    placed = (
        P("dp", None),
        P("dp", None),
        P("section", None, None),
        P("section", None, None),
        P("dp", None),
    )
    return jax.shard_map(
        body,
        mesh=mesh,
        in_specs=placed,
        out_specs=(P("section", "dp", None), P("section", "dp", None), P("section", None, "dp")),
        check_vma=False,
    )
```

```python
import functools

import jax
import jax.numpy as jnp
from jax import lax
from jax.experimental import pallas as pl
from jax.experimental.pallas import tpu as pltpu
from jax.sharding import PartitionSpec as P

D = 768
HD = 64
FF = 3072
SV = 384
ROWS = 112
PAIRS = 6
WIDE = 2 * HD
EPS = 1e-05
BF = jnp.bfloat16
F32 = jnp.float32

SPLIT = (1, 1, 1, 1)

L0, L1, L2, L3 = 0, D, 2 * D, 3 * D
R0, R1, R2 = 0, 3 * D, 4 * D
ALL = 4 * D + 2 * FF

QKV, OUT, UP, DOWN = 0, 3 * D, 4 * D, 4 * D + FF
FRESH = 2 * D + D - SV
HALF = FF // 2
TURNED = 4 * D

VM = pl.BlockSpec(memory_space=pltpu.VMEM)
SM = pl.BlockSpec(memory_space=pltpu.SMEM)
HB = pl.BlockSpec(memory_space=pltpu.HBM)
ANY = pl.BlockSpec(memory_space=pl.ANY)


def dot(left, right):
    return jnp.dot(left, right, preferred_element_type=F32)


def dot_nt(left, right):
    return lax.dot_general(left, right, (((1,), (1,)), ((), ())), preferred_element_type=F32)


def normalized(rows):
    centered = rows - jnp.mean(rows, axis=-1, keepdims=True)
    spread = lax.rsqrt(jnp.mean(centered * centered, axis=-1, keepdims=True) + EPS)
    return centered * spread, spread


def norm_back(hat, spread, gain, grad):
    scaled = grad * gain
    inner = jnp.mean(scaled, axis=-1, keepdims=True)
    along = jnp.mean(scaled * hat, axis=-1, keepdims=True)
    return spread * (scaled - inner - hat * along)


def gelu_pair(u):
    c0 = 0.7978845608028654
    c1 = c0 * 0.044715
    square = u * u
    half = 0.5 + 0.5 * jnp.tanh(u * (c0 + c1 * square))
    act = u * half
    return act, half + act * ((1.0 - half) * (2.0 * c0 + (6.0 * c1) * square))


def sequence_start(lengths, bucket, i):
    e0 = lengths[bucket, 0]
    e1 = e0 + lengths[bucket, 1]
    e2 = e1 + lengths[bucket, 2]
    return jnp.where(i >= e2, e2, jnp.where(i >= e1, e1, jnp.where(i >= e0, e0, 0)))


def bias_rows(lengths, bucket):
    i = lax.broadcasted_iota(jnp.int32, (ROWS, ROWS), 0)
    j = lax.broadcasted_iota(jnp.int32, (ROWS, ROWS), 1)
    bias = jnp.where((j <= i) & (j >= sequence_start(lengths, bucket, i)), 0.0, -1e30)
    return jnp.concatenate([bias, bias], axis=0)


def bias_columns(lengths, bucket):
    j = lax.broadcasted_iota(jnp.int32, (ROWS, 2 * ROWS), 0)
    i = lax.broadcasted_iota(jnp.int32, (ROWS, 2 * ROWS), 1)
    i = jnp.where(i >= ROWS, i - ROWS, i)
    return jnp.where((j <= i) & (j >= sequence_start(lengths, bucket, i)), 0.0, -1e30)


def lane_masks(scale):
    low = lax.broadcasted_iota(jnp.int32, (ROWS, WIDE), 1) < HD
    return jnp.where(low, scale, 0.0).astype(BF), jnp.where(low, 0.0, scale).astype(BF)


def two_heads(block, masks):
    return jnp.concatenate([block * masks[0], block * masks[1]], axis=0)


def joined(stacked):
    low = lax.broadcasted_iota(jnp.int32, (ROWS, WIDE), 1) < HD
    return jnp.where(low, stacked[:ROWS], stacked[ROWS:])


def softmax(scores, axis):
    top = jnp.max(scores, axis=axis, keepdims=True)
    powers = jnp.exp(scores - top)
    return powers * (1.0 / jnp.sum(powers, axis=axis, keepdims=True))


def attention(qkv, rows, bias, put):
    masks = lane_masks(HD ** (-0.5))
    at = [WIDE * p for p in range(PAIRS)]
    scores = [
        dot_nt(two_heads(qkv[rows, c : c + WIDE], masks), qkv[rows, D + c : D + c + WIDE]) + bias
        for c in at
    ]
    probs = [softmax(s, -1).astype(BF) for s in scores]
    for c, p in zip(at, probs):
        put(c, joined(dot(p, qkv[rows, 2 * D + c : 2 * D + c + WIDE])))


def attention_back(qkv, rows, grad, bias, put):
    scaled = lane_masks(HD ** (-0.5))
    plain = lane_masks(1.0)
    at = [WIDE * p for p in range(PAIRS)]
    qs = [two_heads(qkv[rows, c : c + WIDE], scaled) for c in at]
    ks = [qkv[rows, D + c : D + c + WIDE] for c in at]
    vs = [qkv[rows, 2 * D + c : 2 * D + c + WIDE] for c in at]
    gs = [two_heads(grad[:, c : c + WIDE], plain) for c in at]
    scores = [dot_nt(k, q) + bias for k, q in zip(ks, qs)]
    grad_probs = [dot_nt(v, g) for v, g in zip(vs, gs)]
    probs = [softmax(s, 0) for s in scores]
    inner = [jnp.sum(d * p, axis=0, keepdims=True) for d, p in zip(grad_probs, probs)]
    grad_scores = [(p * (d - i)).astype(BF) for p, d, i in zip(probs, grad_probs, inner)]
    grad_v = [dot(p.astype(BF), g) for p, g in zip(probs, gs)]
    grad_k = [dot(s, q) for s, q in zip(grad_scores, qs)]
    turned = [s.T for s in grad_scores]
    grad_q = [joined(dot(t, k)) * HD ** (-0.5) for t, k in zip(turned, ks)]
    for c, dq, dk, dv in zip(at, grad_q, grad_k, grad_v):
        put(c, dq, dk, dv)


def buckets_of(start, stop):
    return [(b // ROWS, slice(b, b + ROWS)) for b in range(start, stop, ROWS)]


class Loads:
    def __init__(self, sems):
        self.sems = sems
        self.used = 0

    def start(self, src, dst):
        copy = pltpu.make_async_copy(src, dst, self.sems.at[self.used])
        self.used += 1
        copy.start()
        return copy


def forward_wide(left, store, slope, rows, w, up, down, chunk, waits=None):
    count = FF // chunk

    def lift(c):
        if waits:
            waits[0][c].wait()
        return dot(left[rows, L2 : L2 + D], w[:, up + c * chunk : up + (c + 1) * chunk])

    total = None
    here = lift(0)
    for c in range(count):
        ahead = lift(c + 1) if c + 1 < count else None
        act, gradient = gelu_pair(here)
        act = act.astype(BF)
        store[rows, c * chunk : (c + 1) * chunk] = act
        slope[rows, c * chunk : (c + 1) * chunk] = gradient.astype(BF)
        if down is not None:
            if waits:
                waits[1][c].wait()
            part = dot_nt(act, w[:, down + c * chunk : down + (c + 1) * chunk])
            total = part if total is None else total + part
        here = ahead
    return total


CHUNK = 512
COST = 1000


def first_forward(start, stop, fresh, sec, lengths, gains, tokens, *refs):
    if fresh:
        slab, refs = refs[0], refs[1:]
        w, left, acts, qkv, slope, mid, right, outs, gg, message, sems = refs
        gg[...] = jnp.zeros_like(gg)
    else:
        w, refs = refs[0], refs[1:]
        left, acts, qkv, slope, mid, message, sems = refs[5:]
    rows = slice(start, stop)
    if fresh:

        @pl.when(sec[0] == 1)
        def _():
            load = Loads(sems).start(slab.at[:, pl.ds(0, FRESH + D)], w.at[:, pl.ds(0, FRESH + D)])
            load.wait()
            w[:, TURNED : TURNED + D] = w[:, FRESH : FRESH + D].T
            for c in range(0, FRESH, D):
                wide = min(D, FRESH - c)
                at = TURNED + D + c
                w[:wide, at : at + D] = w[:, c : c + wide].T

        @pl.when(sec[0] == 2)
        def _():
            loads = Loads(sems)
            both = [
                loads.start(slab.at[:, pl.ds(at, HALF)], w.at[:, pl.ds(at, HALF)])
                for at in (0, HALF)
            ]
            for load in both:
                load.wait()

    @pl.when(sec[0] == 0)
    def _():
        loads = Loads(sems)
        first = second = waits = None
        if fresh:

            def get(at, wide):
                return loads.start(slab.at[:, pl.ds(at, wide)], w.at[:, pl.ds(at, wide)])

            first = [get(QKV + c * D, D) for c in range(3)]
            second = get(OUT, D)
            waits = ([], [])
            for c in range(FF // CHUNK):
                waits[0].append(get(UP + c * CHUNK, CHUNK))
                waits[1].append(get(DOWN + c * CHUNK, CHUNK))
        x = tokens[rows, :].astype(F32)
        low = (normalized(x)[0] * gains[0:1, :]).astype(BF)
        left[rows, L0 : L0 + D] = low
        for c in range(3):
            if fresh:
                first[c].wait()
            qkv[rows, c * D : (c + 1) * D] = dot(low, w[:, QKV + c * D : QKV + (c + 1) * D]).astype(BF)
        message[:, D:] = qkv[rows, 2 * D : 2 * D + SV]
        for bucket, here in buckets_of(start, stop):

            def put(c, value):
                left[here, L1 + c : L1 + c + WIDE] = value.astype(BF)

            attention(qkv, here, bias_rows(lengths, bucket), put)
        if fresh:
            second.wait()
        middle = x + dot(left[rows, L1 : L1 + D], w[:, OUT : OUT + D])
        mid[rows, :] = middle
        left[rows, L2 : L2 + D] = (normalized(middle)[0] * gains[1:2, :]).astype(BF)
        total = forward_wide(left, acts, slope, rows, w, UP, DOWN, CHUNK, waits)
        message[:, :D] = (middle + total).astype(BF)


def second_forward(start, stop, sec, lengths, gains, w, arrived, *refs):
    left, qkv, outs, message, sems = refs[3:]
    rows = slice(start, stop)

    @pl.when(sec[0] == 1)
    def _():
        outs[rows, :] = arrived[:, :D]
        x = arrived[:, :D].astype(F32)
        low = (normalized(x)[0] * gains[0:1, :]).astype(BF)
        left[rows, L0 : L0 + D] = low
        mixed = dot(low, w[:, :FRESH]).astype(BF)
        qkv[rows, : 2 * D] = mixed[:, : 2 * D]
        qkv[rows, 2 * D : 2 * D + SV] = arrived[:, D:]
        qkv[rows, 2 * D + SV :] = mixed[:, 2 * D :]
        for bucket, here in buckets_of(start, stop):

            def put(c, value):
                left[here, L1 + c : L1 + c + WIDE] = value.astype(BF)

            attention(qkv, here, bias_rows(lengths, bucket), put)
        message[...] = (x + dot(left[rows, L1 : L1 + D], w[:, FRESH : FRESH + D])).astype(BF)


def third_forward(start, stop, sec, gains, w, cot, arrived, *refs):
    left, right, slope, token, sems = refs[3:]
    rows = slice(start, stop)
    token[...] = jnp.zeros_like(token)

    @pl.when(sec[0] == 2)
    def _():
        left[rows, L1 : L1 + D] = arrived[...]
        left[rows, L3 : L3 + D] = cot[rows, :]
        hat = normalized(arrived[...].astype(F32))[0]
        left[rows, L2 : L2 + D] = (hat * gains[0:1, :]).astype(BF)
        forward_wide(left, right, slope, rows, w, 0, None, CHUNK)


def third_back_quarter(left, right, slope, w, other, at, rows):
    cols = pl.ds(at, FF // 4)
    grad = dot(left[rows, L3 : L3 + D], other[...]).astype(BF).astype(F32)
    lifted = (slope[rows, cols].astype(F32) * grad).astype(BF)
    right[rows, pl.ds(pl.multiple_of(R2 + at, 128), FF // 4)] = lifted
    return dot_nt(lifted, w[:, cols])


def third_back_first(start, stop, sec, spot, core, w, *refs):
    others, refs = refs[:3], refs[3:]
    slope, left, _r, _m, right, mid, sems = refs
    rows = slice(start, stop)

    @pl.when(sec[0] == 2)
    def _():
        at = quarters(core[0], (spot[0] + spot[1]) % 2)
        total = None
        for k, other in enumerate(others):
            part = third_back_quarter(left, right, slope, w, other, at[k], rows)
            total = part if total is None else total + part
        mid[rows, :] = total


def third_back(start, stop, sec, spot, core, gains, w, got, slope, left, mid, *refs):
    right, outs, gg, message, sems = refs[3:]
    rows = slice(start, stop)

    @pl.when(sec[0] == 2)
    def _():
        at = quarters(core[0], (spot[0] + spot[1]) % 2)[3]
        back = mid[rows, :] + third_back_quarter(left, right, slope, w, got, at, rows)
        hat, spread = normalized(left[rows, L1 : L1 + D].astype(F32))
        gg[0:1, :] += jnp.sum(back * hat, axis=0, keepdims=True)
        c = left[rows, L3 : L3 + D].astype(F32)
        resid = (c + norm_back(hat, spread, gains[0:1, :], back)).astype(BF)
        message[...] = resid
        outs[rows, :] = resid


def second_back(start, stop, sec, lengths, gains, w, qkv, outs, arrived, *refs):
    left, right, gg, message, sems = refs[3:]
    rows = slice(start, stop)

    @pl.when(sec[0] == 1)
    def _():
        right[rows, R1 : R1 + D] = arrived[...]
        grad = dot(arrived[...], w[:, TURNED : TURNED + D]).astype(BF)
        for bucket, here in buckets_of(start, stop):
            local = slice(here.start - start, here.stop - start)

            def put(c, dq, dk, dv):
                right[here, R0 + c : R0 + c + WIDE] = dq.astype(BF)
                right[here, R0 + D + c : R0 + D + c + WIDE] = dk.astype(BF)
                if c < SV:
                    message[local, D + c : D + c + WIDE] = dv.astype(BF)
                else:
                    right[here, R0 + 2 * D + c - SV : R0 + 2 * D + c - SV + WIDE] = dv.astype(BF)

            attention_back(qkv, here, grad[local], bias_columns(lengths, bucket), put)
        back = None
        for c in range(0, FRESH, D):
            wide, at = min(D, FRESH - c), TURNED + D + c
            part = dot(right[rows, R0 + c : R0 + c + wide], w[:wide, at : at + D])
            back = part if back is None else back + part
        hat, spread = normalized(outs[rows, :].astype(F32))
        gg[0:1, :] += jnp.sum(back * hat, axis=0, keepdims=True)
        resid = arrived[...].astype(F32) + norm_back(hat, spread, gains[0:1, :], back)
        message[:, :D] = resid.astype(BF)
        left[rows, L3 : L3 + D] = resid.astype(BF)


def first_back_wide(start, stop, sec, gains, w, slope, arrived, *refs):
    right, mid, gg, sems = refs[3:]
    rows = slice(start, stop)

    @pl.when(sec[0] == 0)
    def _():
        grad = arrived[:, :D]
        back = None
        pulled = dot(grad, w[:, DOWN : DOWN + CHUNK])
        for c in range(FF // CHUNK):
            k = c * CHUNK
            ahead = None
            if k + CHUNK < FF:
                ahead = dot(grad, w[:, DOWN + k + CHUNK : DOWN + k + 2 * CHUNK])
            lifted = (slope[rows, k : k + CHUNK].astype(F32) * pulled).astype(BF)
            right[rows, R2 + k : R2 + k + CHUNK] = lifted
            part = dot_nt(lifted, w[:, UP + k : UP + k + CHUNK])
            back = part if back is None else back + part
            pulled = ahead
        hat, spread = normalized(mid[rows, :])
        gg[1:2, :] += jnp.sum(back * hat, axis=0, keepdims=True)
        resid = grad.astype(F32) + norm_back(hat, spread, gains[1:2, :], back)
        right[rows, R1 : R1 + D] = resid.astype(BF)
        mid[rows, :] = resid


def first_back_attend(start, stop, sec, lengths, gains, tokens, w, qkv, mid, arrived, *refs):
    right, outs, gg, token, sems = refs[3:]
    rows = slice(start, stop)
    token[...] = jnp.zeros_like(token)

    @pl.when(sec[0] == 0)
    def _():
        grad = dot_nt(right[rows, R1 : R1 + D], w[:, OUT : OUT + D]).astype(BF)
        for bucket, here in buckets_of(start, stop):
            local = slice(here.start - start, here.stop - start)

            def put(c, dq, dk, dv):
                right[here, R0 + c : R0 + c + WIDE] = dq.astype(BF)
                right[here, R0 + D + c : R0 + D + c + WIDE] = dk.astype(BF)
                if c < SV:
                    dv = dv + arrived[local, D + c : D + c + WIDE].astype(F32)
                right[here, R0 + 2 * D + c : R0 + 2 * D + c + WIDE] = dv.astype(BF)

            attention_back(qkv, here, grad[local], bias_columns(lengths, bucket), put)
        back = dot_nt(right[rows, R0 : R0 + 3 * D], w[:, QKV : QKV + 3 * D])
        hat, spread = normalized(tokens[rows, :].astype(F32))
        gg[0:1, :] += jnp.sum(back * hat, axis=0, keepdims=True)
        outs[rows, :] = (mid[rows, :] + norm_back(hat, spread, gains[0:1, :], back)).astype(BF)


def last_forward(sec, spot, core, *refs):
    others, (_l, _r, left, right, result, sems) = refs[:4], refs[4:]

    @pl.when(sec[0] == 2)
    def _():
        total = left[:, L1 : L1 + D].astype(F32)
        for at, other in zip(quarters(core[0], (spot[0] + spot[1]) % 2), others):
            total = total + dot_nt(right[:, pl.ds(at, FF // 4)], other[...])
        result[...] = total.astype(BF)


def take_acts(sec, arrived, _r, right, sems):
    @pl.when(sec[0] == 1)
    def _():
        right[:, R2:] = arrived[...]


def put_acts(sec, acts, out, sem):
    @pl.when(sec[0] == 0)
    def _():
        Loads(sem).start(acts, out).wait()


def take_columns(sec, order, slab, piece, sems):
    @pl.when(sec[0] == 3)
    def _():
        wide = piece.shape[1]
        at = pl.multiple_of(order[0] * wide, 128)
        Loads(sems).start(slab.at[:, pl.ds(at, wide)], piece).wait()


def halve_rows(sec, piece, upper, lower):
    @pl.when(sec[0] == 2)
    def _():
        upper[...] = piece[: D // 2]
        lower[...] = piece[D // 2 :]


def gather_rows(sec, from_x, from_y, other):
    @pl.when(sec[0] == 2)
    def _():
        other[: D // 2, :] = from_x[...]
        other[D // 2 :, :] = from_y[...]


def quarters(core, odd):
    wide = FF // 4
    return [
        pl.multiple_of(which * HALF + parity * wide, 128)
        for which in (core, 1 - core)
        for parity in (odd, 1 - odd)
    ]


def by_core(core, whole, keep, send):
    wide = whole.shape[0] // 8
    for k in range(4):
        here = slice(k * wide, (k + 1) * wide)
        keep[here, :] = whole[pl.ds(pl.multiple_of((2 * k + core) * wide, wide), wide), :]
        send[here, :] = whole[pl.ds(pl.multiple_of((2 * k + 1 - core) * wide, wide), wide), :]


def shares(roles, extra, again, sec, core, gg, *refs):
    left, right, keep, send, sems, turned, whole = refs[3 if again else 2 :]

    def run(first, groups):
        before = None
        for j, group in enumerate(groups):
            if group != before:
                turned[...] = left[:, group * D : (group + 1) * D].T
            before = group
            whole[...] = dot(turned[...], right[:, first + j * D : first + (j + 1) * D]).astype(BF)
            cols = pl.ds(j * D, D)
            by_core(core[0], whole, keep.at[:, cols], send.at[:, cols])
        if extra:
            block = whole.at[:, pl.ds(0, 256)]
            block[...] = jnp.zeros((D, 256), BF)
            block[:, :8] = gg[...].T.astype(BF)
            cols = pl.ds(len(groups) * D, 256)
            by_core(core[0], block, keep.at[:, cols], send.at[:, cols])

    for part, (first, groups) in roles.items():
        pl.when(sec[0] == part)(functools.partial(run, first, groups))


def sum_first(spot, keep, got, send_a, send_b, mine_a, mine_b):
    part, half = send_a.shape[0] // 2, send_a.shape[1]
    x, y = spot[0], spot[1]

    def both(where, lo):
        rows = pl.ds(pl.multiple_of(where * part, part), part)
        cols = slice(lo, lo + half)
        return (keep[rows, cols].astype(F32) + got[rows, cols].astype(F32)).astype(BF)

    for k in range(2):
        here = slice(k * part, (k + 1) * part)
        send_a[here, :] = both(2 * k + 1 - x, 0)
        send_b[here, :] = both(2 * (1 - y) + k, half)
        mine_a[here, :] = both(2 * k + x, 0)
        mine_b[here, :] = both(2 * y + k, half)


def sum_second(spot, mine_a, mine_b, got_a, got_b, send_a, send_b, last_a, last_b):
    part = send_a.shape[0]
    x, y = spot[0], spot[1]

    def both(mine, got, where):
        rows = pl.ds(pl.multiple_of(where * part, part), part)
        return mine[rows, :].astype(F32) + got[rows, :].astype(F32)

    send_a[...] = both(mine_a, got_a, 1 - y).astype(BF)
    send_b[...] = both(mine_b, got_b, 1 - x).astype(BF)
    last_a[...] = both(mine_a, got_a, y).astype(BF)
    last_b[...] = both(mine_b, got_b, x).astype(BF)


def sum_last(last_a, got_a, last_b, got_b, total):
    half = last_a.shape[1]
    total[:, :half] = (last_a[...].astype(F32) + got_a[...].astype(F32)).astype(total.dtype)
    total[:, half:] = (last_b[...].astype(F32) + got_b[...].astype(F32)).astype(total.dtype)


def finish(sec, wide, narrow, moved, outs, result, grads, rows, gains):
    count = grads.shape[0]
    blank = functools.partial(jnp.zeros, dtype=F32)

    def total(four, lo, hi):
        half = four[0].shape[1]
        pieces = []
        for at in range(2):
            first, last = max(lo - at * half, 0), min(hi - at * half, half)
            if first < last:
                one, two = four[2 * at][:, first:last], four[2 * at + 1][:, first:last]
                pieces.append((at * half + first, one.astype(F32) + two.astype(F32)))
        return pieces

    def lay(four, lo, hi, to):
        for at, value in total(four, lo, hi):
            grads[:, to + at - lo : to + at - lo + value.shape[1]] = value

    def lay_gains(four):
        ((_, block),) = total(four, 4 * D, 4 * D + 128)
        gains[...] = block.T[:2]

    @pl.when(sec[0] == 0)
    def _():
        lay(narrow, 0, 4 * D, 0)
        lay(wide, 0, FF, UP)
        grads[:, DOWN:] = moved[...].astype(F32)
        lay_gains(narrow)

    @pl.when(sec[0] == 1)
    def _():
        lay(narrow, 0, FRESH, 0)
        lay(narrow, 3 * D, 4 * D, FRESH)
        grads[:, FRESH + D :] = blank((count, ALL - FRESH - D))
        lay_gains(narrow)

    @pl.when(sec[0] == 2)
    def _():
        lay(narrow, 0, FF, 0)
        grads[:, FF:] = blank((count, ALL - FF))
        lay_gains(narrow)

    @pl.when(sec[0] == 3)
    def _():
        grads[:, :FF] = moved[...].astype(F32)
        grads[:, FF:] = blank((count, ALL - FF))
        gains[...] = jnp.zeros_like(gains)
        rows[...] = result[...]

    @pl.when(sec[0] != 3)
    def _():
        rows[...] = outs[...]


def shape(rows, cols, dtype=BF):
    return jax.ShapeDtypeStruct((rows, cols), dtype)


def held(rows, cols, dtype=BF):
    return pltpu.VMEM((rows, cols), dtype)


def keep_in_vmem(array):
    return pltpu.with_memory_space_constraint(array, pltpu.VMEM)


def call(kernel, name, ins, states, outs, sems=1, scratch=(), after=(), limit=8, specs=None, cost=COST):
    operands = [a for a, _ in ins] + [keep_in_vmem(s) for s in states]
    aliases = {len(ins) + i: i for i in range(len(states))}
    out_shape = [held(*s.shape, s.dtype) for s in states] + list(outs)
    return pl.pallas_call(
        behind(kernel, len(operands), after),
        name=name,
        out_shape=out_shape,
        in_specs=[s for _, s in ins] + [VM] * len(states) + [ANY] * len(after),
        out_specs=[VM] * len(states) + list(specs or [VM] * len(outs)),
        scratch_shapes=[pltpu.SemaphoreType.DMA((sems,))] + list(scratch),
        input_output_aliases=aliases,
        compiler_params=pltpu.CompilerParams(vmem_limit_bytes=limit << 20),
        cost_estimate=pl.CostEstimate(flops=cost, bytes_accessed=1024, transcendentals=0),
    )(*operands, *after)


def behind(kernel, count, after):
    def ordered(*refs):
        kernel(*refs[:count], *refs[count + len(after) :])

    return ordered


def plain(kernel, name, operands, specs, outs, limit=8, scratch=(), after=(), out_specs=None, cost=COST):
    return pl.pallas_call(
        behind(kernel, len(operands), after),
        name=name,
        out_shape=outs,
        in_specs=specs + [ANY] * len(after),
        out_specs=out_specs or [VM] * len(outs),
        scratch_shapes=list(scratch),
        compiler_params=pltpu.CompilerParams(vmem_limit_bytes=limit << 20),
        cost_estimate=pl.CostEstimate(flops=cost, bytes_accessed=1024, transcendentals=0),
    )(*operands, *after)


def exchange_on(parts, block, bit):
    count, sections = lax.axis_size("dp"), lax.axis_size("section")
    pairs = [(i * sections + p, (i ^ bit) * sections + p) for p in parts for i in range(count)]
    return lax.ppermute(block, ("dp", "section"), pairs)


def shift(block, pairs):
    return lax.ppermute(block, "section", pairs)


def scatter_sum(name, parts, keep, got, sec, spot, after, cost, later=()):
    swap = functools.partial(exchange_on, parts)
    part, half = keep.shape[0] // 4, keep.shape[1] // 2
    pairs = len(got) == 2

    def only(kernel):
        def run(sec_ref, *refs):
            mine = sec_ref[0] == parts[0]
            for p in parts[1:]:
                mine = mine | (sec_ref[0] == p)

            @pl.when(mine)
            def _():
                kernel(*refs)

        return run

    def first(sec_ref, spot_ref, keep_ref, *refs):
        if not pairs:
            only(sum_first)(sec_ref, spot_ref, keep_ref, *refs)
            return
        here, there, *outs = refs

        @pl.when(sec_ref[0] == 0)
        def _():
            sum_first(spot_ref, keep_ref, here, *outs)

        @pl.when((sec_ref[0] == 1) | (sec_ref[0] == 2))
        def _():
            sum_first(spot_ref, keep_ref, there, *outs)

    send_a, send_b, mine_a, mine_b = plain(
        first,
        name + "_first",
        [sec, spot, keep, *got],
        [SM, SM, VM] + [VM] * len(got),
        [shape(2 * part, half)] * 4,
        12,
        after=after,
    )
    got_a, got_b = swap(send_a, 2), swap(send_b, 4)
    began = [mine_a]
    send_a, send_b, last_a, last_b = plain(
        only(sum_second),
        name + "_second",
        [sec, spot, mine_a, mine_b, got_a, got_b],
        [SM, SM, VM, VM, VM, VM],
        [shape(part, half)] * 4,
        after=later,
        cost=cost,
    )
    return (last_a, swap(send_a, 4), last_b, swap(send_b, 2)), began, [last_a]


def body(tokens, lengths, section_weights, norm_gains, cotangent):
    slab = pltpu.with_memory_space_constraint(section_weights[0], pltpu.HBM)
    gains = norm_gains[0]
    section = lax.axis_index("section")
    dp = lax.axis_size("dp")
    place = lax.axis_index("dp")
    split = dp == 8
    sec = section.astype(jnp.int32).reshape(1)
    core = (place % 2).astype(jnp.int32).reshape(1)
    spot = jnp.stack([(place // 2) % 2, (place // 4) % 2]).astype(jnp.int32)
    order = ((place % 2) * 2 + (place // 2 + place // 4) % 2).astype(jnp.int32).reshape(1)
    sec, core, spot, order, tokens = lax.optimization_barrier((sec, core, spot, order, tokens))
    total = tokens.shape[0]
    shard = D // dp
    sizes = SPLIT if sum(SPLIT) * ROWS == total else (1,) * (total // ROWS)
    bounds = []
    for size in sizes:
        first = bounds[-1][1] if bounds else 0
        bounds.append((first, first + size * ROWS))

    if split:
        piece = plain(
            take_columns,
            "take_columns",
            [sec, order, slab],
            [SM, SM, HB],
            [shape(D, FF // 4)],
            scratch=[pltpu.SemaphoreType.DMA((1,))],
        )[0]
    else:
        piece = lax.dynamic_slice(section_weights[0], (place * shard, 0), (shard, FF))
    piece = shift(piece, [(3, 2)])

    state = {}
    sent, sent_2, notes, made, cut = [], [], [], [], []

    def run_first(mb, after=()):
        start, stop = bounds[mb]
        fresh = mb == 0
        kernel = functools.partial(first_forward, start, stop, fresh)
        message = shape(stop - start, D + SV)
        ins = [(sec, SM), (lengths, SM), (gains, VM), (tokens, VM)]
        if fresh:
            names = ["w", "left", "acts", "qkv", "slope", "mid", "right", "outs", "gg"]
            arrays = [
                held(D, ALL),
                held(total, 4 * D),
                held(total, FF),
                held(total, 3 * D),
                held(total, FF),
                held(total, D, F32),
                held(total, 4 * D + FF),
                held(total, D),
                held(8, D, F32),
            ]
            results = call(kernel, "first_forward", ins + [(slab, HB)], [], arrays + [message], 16)
        else:
            names = ["left", "acts", "qkv", "slope", "mid"]
            ins += [(keep_in_vmem(state["w"]), VM)]
            results = call(
                kernel, "first_forward", ins, [state[n] for n in names], [message], after=after
            )
        state.update(zip(names, results))
        sent.append(shift(results[-1], [(0, 1)]))

    def send_acts():
        acts = plain(
            put_acts,
            "put_acts",
            [sec, keep_in_vmem(state["acts"])],
            [SM, VM],
            [pltpu.HBM((total, FF), BF)],
            scratch=[pltpu.SemaphoreType.DMA((1,))],
            after=[sent[-1], *sent_2[:1], *made],
            out_specs=[HB],
        )[0]
        return acts, shift(acts, [(0, 1)])

    def run_second(mb, after=()):
        start, stop = bounds[mb]
        names = ["left", "qkv", "outs"]
        results = call(
            functools.partial(second_forward, start, stop),
            "second_forward",
            [(sec, SM), (lengths, SM), (gains, VM), (keep_in_vmem(state["w"]), VM), (sent[mb], VM)],
            [state[n] for n in names],
            [shape(stop - start, D)],
            after=after,
        )
        state.update(zip(names, results))
        made.append(results[-1])
        sent_2.append(shift(results[-1], [(1, 2)]))

    def run_third(mb, after=()):
        start, stop = bounds[mb]
        names = ["left", "right", "slope"]
        results = call(
            functools.partial(third_forward, start, stop),
            "third_forward",
            [(sec, SM), (gains, VM), (keep_in_vmem(state["w"]), VM), (cotangent, VM), (sent_2[mb], VM)],
            [state[n] for n in names],
            [shape(8, 128, F32)],
            after=after,
        )
        state.update(zip(names, results))
        notes.append(results[-1])

    def halves():
        parts = plain(
            halve_rows,
            "halve_rows",
            [sec, piece],
            [SM, VM],
            [shape(D // 2, FF // 4)] * 2,
            after=[sent[-1], made[-1], sent_2[0]],
        )
        cut.extend(parts)
        return exchange_on([2], parts[0], 2), exchange_on([2], parts[1], 4)

    def gathered(from_x, from_y):
        return plain(
            gather_rows,
            "gather_rows",
            [sec, from_x, from_y],
            [SM, VM, VM],
            [shape(D, FF // 4)],
            after=[notes[-1]],
        )[0]

    if len(bounds) == 4 and split:
        run_first(0)
        run_first(1)
        run_first(2)
        run_second(0)
        run_first(3, after=[sent[1]])
        run_second(1, after=[sent[2]])
        run_second(2)
        swapped = exchange_on([2], piece, 1)
        sides = halves()
        run_third(0)
        acts, sent_acts = send_acts()
        run_second(3, after=[acts])
        run_third(1)
        run_third(2)
        run_third(3)
        other = gathered(*sides)
        parts_3 = [piece, other, swapped, exchange_on([2], other, 1)]
    else:
        for run in (run_first, run_second, run_third):
            for mb in range(len(bounds)):
                run(mb)
            if run is run_first:
                _, sent_acts = send_acts()
        if split:
            swapped = exchange_on([2], piece, 1)
            other = gathered(*halves())
            parts_3 = [piece, other, swapped, exchange_on([2], other, 1)]
        else:
            whole = lax.all_gather(piece, "dp", axis=0, tiled=True)
            wide_3 = FF // 4
            odd = (spot[0] + spot[1]) % 2
            parts_3 = [
                lax.dynamic_slice(whole, (0, which * HALF + parity * wide_3), (D, wide_3))
                for which in (core[0], 1 - core[0])
                for parity in (odd, 1 - odd)
            ]
    w = keep_in_vmem(state["w"])
    back_2, back_1 = [], []

    def run_third_first(first, last):
        state["right"], state["mid"] = call(
            functools.partial(third_back_first, bounds[first][0], bounds[last - 1][1]),
            "third_back_first",
            [(sec, SM), (spot, SM), (core, SM), (w, VM)]
            + [(keep_in_vmem(part), VM) for part in parts_3[:3]]
            + [(keep_in_vmem(state[n]), VM) for n in ("slope", "left")],
            [state["right"], state["mid"]],
            [],
        )

    def run_third_back(mb):
        start, stop = bounds[mb]
        names = ["right", "outs", "gg"]
        results = call(
            functools.partial(third_back, start, stop),
            "third_back",
            [(sec, SM), (spot, SM), (core, SM), (gains, VM), (w, VM)]
            + [(keep_in_vmem(parts_3[3]), VM)]
            + [(keep_in_vmem(state[n]), VM) for n in ("slope", "left", "mid")],
            [state[n] for n in names],
            [shape(stop - start, D)],
        )
        state.update(zip(names, results))
        back_2.append(shift(results[-1], [(2, 1)]))

    def run_second_back(mb):
        start, stop = bounds[mb]
        names = ["left", "right", "gg"]
        results = call(
            functools.partial(second_back, start, stop),
            "second_back",
            [(sec, SM), (lengths, SM), (gains, VM), (w, VM)]
            + [(keep_in_vmem(state["qkv"]), VM), (keep_in_vmem(state["outs"]), VM), (back_2[mb], VM)],
            [state[n] for n in names],
            [shape(stop - start, D + SV)],
        )
        state.update(zip(names, results))
        back_1.append(shift(results[-1], [(1, 0)]))

    for first in range(0, len(bounds), 2):
        last = min(first + 2, len(bounds))
        run_third_first(first, last)
        for mb in range(first, last):
            run_third_back(mb)
    for mb in range(len(bounds)):
        run_second_back(mb)
    left, right, qkv, slope, mid, outs, gg = [
        state[n] for n in ("left", "right", "qkv", "slope", "mid", "outs", "gg")
    ]

    def own_shares(name, roles, extra, left, right, keep=None, after=()):
        width = 4 * D + (256 if extra else 0)
        rows = held(D // 2, width)
        states = [left, right] + ([] if keep is None else [keep])
        return call(
            functools.partial(shares, roles, extra, keep is not None),
            name,
            [(sec, SM), (core, SM), (keep_in_vmem(gg), VM)],
            states,
            [rows] * (2 if keep is None else 1),
            scratch=[pltpu.VMEM((D, total), BF), pltpu.VMEM((D, D), BF)],
            after=after,
        )

    def plain_sums(roles, extra):
        width = 4 * D + (256 if extra else 0)
        full = jnp.zeros((D, width), BF)
        for part, (first, groups) in roles.items():
            blocks = [
                lax.dot_general(
                    left[:, g * D : (g + 1) * D],
                    right[:, first + j * D : first + (j + 1) * D],
                    (((0,), (0,)), ((), ())),
                    preferred_element_type=F32,
                ).astype(BF)
                for j, g in enumerate(groups)
            ]
            if extra:
                blocks += [gg.T.astype(BF), jnp.zeros((D, 248), BF)]
            full = jnp.where(section == part, jnp.concatenate(blocks, axis=1), full)
        full = lax.psum_scatter(full, "dp", scatter_dimension=0, tiled=True)
        blank = jnp.zeros((shard, width // 2), BF)
        return full[:, : width // 2], blank, full[:, width // 2 :], blank

    def run_wide(mb):
        start, stop = bounds[mb]
        return call(
            functools.partial(first_back_wide, start, stop),
            "first_back_wide",
            [(sec, SM), (gains, VM), (w, VM), (keep_in_vmem(slope), VM), (back_1[mb], VM)],
            [right, mid, gg],
            [],
        )

    def run_attend(mb, after=()):
        start, stop = bounds[mb]
        return call(
            functools.partial(first_back_attend, start, stop),
            "first_back_attend",
            [(sec, SM), (lengths, SM), (gains, VM), (tokens, VM), (w, VM)]
            + [(keep_in_vmem(qkv), VM), (keep_in_vmem(mid), VM), (back_1[mb], VM)],
            [right, outs, gg],
            [shape(8, 128, F32)],
            after=after,
        )

    up_roles = {0: (R2, [2] * 4)}
    down_roles = {1: (R2, [3] * 4), 2: (0, [3] * 4)}
    narrow_roles = {0: (R0, [0] * 3 + [1]), 1: (R0, [0] * 3 + [1]), 2: (R2, [2] * 4)}
    count = len(bounds)
    late = max(count - 2, 0)
    for mb in range(count):
        right, mid, gg = run_wide(mb)
        if mb < late:
            right, outs, gg, _ = run_attend(mb)
    def sum_up(four):
        return plain(
            sum_last, "wide_sum_last", list(four), [VM] * 4, [shape(shard, FF)], cost=8000000000
        )[0]

    tokens_of = []
    if split:
        left, right, keep, send = own_shares("up_grads", up_roles, False, left, right)
        got_up = exchange_on([0], send, 1)
    right = call(take_acts, "take_acts", [(sec, SM), (sent_acts, VM)], [right], [])[0]
    if split:
        left, right, keep, send = own_shares("down_grads", down_roles, False, left, right, keep)
        got_down = exchange_on([1, 2], send, 1)
    for mb in range(late, count - 1):
        right, outs, gg, token = run_attend(mb)
        tokens_of.append(token)
    if split:
        wide, begun, seconds = scatter_sum(
            "wide_sum", [0, 1, 2], keep, [got_up, got_down], sec, spot, tokens_of, 30000000000
        )
    right, outs, gg, token = run_attend(count - 1, begun if split else ())
    left, right, result = call(
        last_forward,
        "last_forward",
        [(sec, SM), (spot, SM), (core, SM)] + [(part, VM) for part in parts_3],
        [left, right],
        [shape(total, D)],
        limit=12,
    )
    result = shift(result, [(2, 3)])
    if split:
        moved = sum_up(wide)
        left, right, keep, send = own_shares("narrow_grads", narrow_roles, True, left, right)
        got_narrow = exchange_on([0, 1, 2], send, 1)
        narrow, _, _ = scatter_sum(
            "narrow_sum", [0, 1, 2], keep, [got_narrow], sec, spot, seconds, COST, [moved]
        )
    else:
        wide = plain_sums({**up_roles, **down_roles}, False)
        moved = sum_up(wide)
        narrow = plain_sums(narrow_roles, True)
    moved = shift(moved, [(1, 0), (2, 3)])

    def last(*refs):
        finish(refs[0], refs[1:5], refs[5:9], *refs[9:])

    grads, rows, gain_out = plain(
        last,
        "finish",
        [sec, *wide, *narrow, moved, outs, result],
        [SM] + [VM] * 11,
        [shape(shard, ALL, F32), shape(total, D), shape(2, shard, F32)],
        16,
    )
    return (rows[None], grads[None], gain_out[None])


def solution(mesh):
    placed = (
        P("dp", None),
        P("dp", None),
        P("section", None, None),
        P("section", None, None),
        P("dp", None),
    )
    return jax.shard_map(
        body,
        mesh=mesh,
        in_specs=placed,
        out_specs=(P("section", "dp", None), P("section", "dp", None), P("section", None, "dp")),
        check_vma=False,
    )
```

```python
import functools

import jax
import jax.numpy as jnp
from jax import lax
from jax.experimental import pallas as pl
from jax.experimental.pallas import tpu as pltpu
from jax.sharding import PartitionSpec as P

D = 768
HD = 64
FF = 3072
SV = 384
ROWS = 112
PAIRS = 6
WIDE = 2 * HD
EPS = 1e-05
BF = jnp.bfloat16
F32 = jnp.float32

SPLIT = (1, 1, 1, 1)

L0, L1, L2, L3 = 0, D, 2 * D, 3 * D
R0, R1, R2 = 0, 3 * D, 4 * D
ALL = 4 * D + 2 * FF

QKV, OUT, UP, DOWN = 0, 3 * D, 4 * D, 4 * D + FF
FRESH = 2 * D + D - SV
HALF = FF // 2
TURNED = 4 * D

VM = pl.BlockSpec(memory_space=pltpu.VMEM)
SM = pl.BlockSpec(memory_space=pltpu.SMEM)
HB = pl.BlockSpec(memory_space=pltpu.HBM)
ANY = pl.BlockSpec(memory_space=pl.ANY)


def dot(left, right):
    return jnp.dot(left, right, preferred_element_type=F32)


def dot_nt(left, right):
    return lax.dot_general(left, right, (((1,), (1,)), ((), ())), preferred_element_type=F32)


def normalized(rows):
    centered = rows - jnp.mean(rows, axis=-1, keepdims=True)
    spread = lax.rsqrt(jnp.mean(centered * centered, axis=-1, keepdims=True) + EPS)
    return centered * spread, spread


def norm_back(hat, spread, gain, grad):
    scaled = grad * gain
    inner = jnp.mean(scaled, axis=-1, keepdims=True)
    along = jnp.mean(scaled * hat, axis=-1, keepdims=True)
    return spread * (scaled - inner - hat * along)


def gelu_pair(u):
    c0 = 0.7978845608028654
    c1 = c0 * 0.044715
    square = u * u
    half = 0.5 + 0.5 * jnp.tanh(u * (c0 + c1 * square))
    act = u * half
    return act, half + act * ((1.0 - half) * (2.0 * c0 + (6.0 * c1) * square))


def sequence_start(lengths, bucket, i):
    e0 = lengths[bucket, 0]
    e1 = e0 + lengths[bucket, 1]
    e2 = e1 + lengths[bucket, 2]
    return jnp.where(i >= e2, e2, jnp.where(i >= e1, e1, jnp.where(i >= e0, e0, 0)))


def bias_rows(lengths, bucket):
    i = lax.broadcasted_iota(jnp.int32, (ROWS, ROWS), 0)
    j = lax.broadcasted_iota(jnp.int32, (ROWS, ROWS), 1)
    bias = jnp.where((j <= i) & (j >= sequence_start(lengths, bucket, i)), 0.0, -1e30)
    return jnp.concatenate([bias, bias], axis=0)


def bias_columns(lengths, bucket):
    j = lax.broadcasted_iota(jnp.int32, (ROWS, 2 * ROWS), 0)
    i = lax.broadcasted_iota(jnp.int32, (ROWS, 2 * ROWS), 1)
    i = jnp.where(i >= ROWS, i - ROWS, i)
    return jnp.where((j <= i) & (j >= sequence_start(lengths, bucket, i)), 0.0, -1e30)


def lane_masks(scale):
    low = lax.broadcasted_iota(jnp.int32, (ROWS, WIDE), 1) < HD
    return jnp.where(low, scale, 0.0).astype(BF), jnp.where(low, 0.0, scale).astype(BF)


def two_heads(block, masks):
    return jnp.concatenate([block * masks[0], block * masks[1]], axis=0)


def joined(stacked):
    low = lax.broadcasted_iota(jnp.int32, (ROWS, WIDE), 1) < HD
    return jnp.where(low, stacked[:ROWS], stacked[ROWS:])


def softmax(scores, axis):
    top = jnp.max(scores, axis=axis, keepdims=True)
    powers = jnp.exp(scores - top)
    return powers * (1.0 / jnp.sum(powers, axis=axis, keepdims=True))


def attention(qkv, rows, bias, put):
    masks = lane_masks(HD ** (-0.5))
    at = [WIDE * p for p in range(PAIRS)]
    scores = [
        dot_nt(two_heads(qkv[rows, c : c + WIDE], masks), qkv[rows, D + c : D + c + WIDE]) + bias
        for c in at
    ]
    probs = [softmax(s, -1).astype(BF) for s in scores]
    for c, p in zip(at, probs):
        put(c, joined(dot(p, qkv[rows, 2 * D + c : 2 * D + c + WIDE])))


def attention_back(qkv, rows, grad, bias, put):
    scaled = lane_masks(HD ** (-0.5))
    plain = lane_masks(1.0)
    at = [WIDE * p for p in range(PAIRS)]
    qs = [two_heads(qkv[rows, c : c + WIDE], scaled) for c in at]
    ks = [qkv[rows, D + c : D + c + WIDE] for c in at]
    vs = [qkv[rows, 2 * D + c : 2 * D + c + WIDE] for c in at]
    gs = [two_heads(grad[:, c : c + WIDE], plain) for c in at]
    scores = [dot_nt(k, q) + bias for k, q in zip(ks, qs)]
    grad_probs = [dot_nt(v, g) for v, g in zip(vs, gs)]
    probs = [softmax(s, 0) for s in scores]
    inner = [jnp.sum(d * p, axis=0, keepdims=True) for d, p in zip(grad_probs, probs)]
    grad_scores = [(p * (d - i)).astype(BF) for p, d, i in zip(probs, grad_probs, inner)]
    grad_v = [dot(p.astype(BF), g) for p, g in zip(probs, gs)]
    grad_k = [dot(s, q) for s, q in zip(grad_scores, qs)]
    turned = [s.T for s in grad_scores]
    grad_q = [joined(dot(t, k)) * HD ** (-0.5) for t, k in zip(turned, ks)]
    for c, dq, dk, dv in zip(at, grad_q, grad_k, grad_v):
        put(c, dq, dk, dv)


def buckets_of(start, stop):
    return [(b // ROWS, slice(b, b + ROWS)) for b in range(start, stop, ROWS)]


class Loads:
    def __init__(self, sems):
        self.sems = sems
        self.used = 0

    def start(self, src, dst):
        copy = pltpu.make_async_copy(src, dst, self.sems.at[self.used])
        self.used += 1
        copy.start()
        return copy


def forward_wide(left, store, slope, rows, w, up, down, chunk, waits=None):
    count = FF // chunk

    def lift(c):
        if waits:
            waits[0][c].wait()
        return dot(left[rows, L2 : L2 + D], w[:, up + c * chunk : up + (c + 1) * chunk])

    total = None
    here = lift(0)
    for c in range(count):
        ahead = lift(c + 1) if c + 1 < count else None
        act, gradient = gelu_pair(here)
        act = act.astype(BF)
        store[rows, c * chunk : (c + 1) * chunk] = act
        slope[rows, c * chunk : (c + 1) * chunk] = gradient.astype(BF)
        if down is not None:
            if waits:
                waits[1][c].wait()
            part = dot_nt(act, w[:, down + c * chunk : down + (c + 1) * chunk])
            total = part if total is None else total + part
        here = ahead
    return total


CHUNK = 512
COST = 1000


def first_forward(start, stop, fresh, sec, lengths, gains, tokens, *refs):
    if fresh:
        slab, refs = refs[0], refs[1:]
        w, left, acts, qkv, slope, mid, right, outs, gg, message, sems = refs
        gg[...] = jnp.zeros_like(gg)
    else:
        w, refs = refs[0], refs[1:]
        left, acts, qkv, slope, mid, message, sems = refs[5:]
    rows = slice(start, stop)
    if fresh:

        @pl.when(sec[0] == 1)
        def _():
            load = Loads(sems).start(slab.at[:, pl.ds(0, FRESH + D)], w.at[:, pl.ds(0, FRESH + D)])
            load.wait()
            w[:, TURNED : TURNED + D] = w[:, FRESH : FRESH + D].T
            for c in range(0, FRESH, D):
                wide = min(D, FRESH - c)
                at = TURNED + D + c
                w[:wide, at : at + D] = w[:, c : c + wide].T

        @pl.when(sec[0] == 2)
        def _():
            loads = Loads(sems)
            both = [
                loads.start(slab.at[:, pl.ds(at, HALF)], w.at[:, pl.ds(at, HALF)])
                for at in (0, HALF)
            ]
            for load in both:
                load.wait()

    @pl.when(sec[0] == 0)
    def _():
        loads = Loads(sems)
        first = second = waits = None
        if fresh:

            def get(at, wide):
                return loads.start(slab.at[:, pl.ds(at, wide)], w.at[:, pl.ds(at, wide)])

            first = [get(QKV + c * D, D) for c in range(3)]
            second = get(OUT, D)
            waits = ([], [])
            for c in range(FF // CHUNK):
                waits[0].append(get(UP + c * CHUNK, CHUNK))
                waits[1].append(get(DOWN + c * CHUNK, CHUNK))
        x = tokens[rows, :].astype(F32)
        low = (normalized(x)[0] * gains[0:1, :]).astype(BF)
        left[rows, L0 : L0 + D] = low
        for c in range(3):
            if fresh:
                first[c].wait()
            qkv[rows, c * D : (c + 1) * D] = dot(low, w[:, QKV + c * D : QKV + (c + 1) * D]).astype(BF)
        message[:, D:] = qkv[rows, 2 * D : 2 * D + SV]
        for bucket, here in buckets_of(start, stop):

            def put(c, value):
                left[here, L1 + c : L1 + c + WIDE] = value.astype(BF)

            attention(qkv, here, bias_rows(lengths, bucket), put)
        if fresh:
            second.wait()
        middle = x + dot(left[rows, L1 : L1 + D], w[:, OUT : OUT + D])
        mid[rows, :] = middle
        left[rows, L2 : L2 + D] = (normalized(middle)[0] * gains[1:2, :]).astype(BF)
        total = forward_wide(left, acts, slope, rows, w, UP, DOWN, CHUNK, waits)
        message[:, :D] = (middle + total).astype(BF)


def second_forward(start, stop, sec, lengths, gains, w, arrived, *refs):
    left, qkv, outs, message, sems = refs[3:]
    rows = slice(start, stop)

    @pl.when(sec[0] == 1)
    def _():
        outs[rows, :] = arrived[:, :D]
        x = arrived[:, :D].astype(F32)
        low = (normalized(x)[0] * gains[0:1, :]).astype(BF)
        left[rows, L0 : L0 + D] = low
        mixed = dot(low, w[:, :FRESH]).astype(BF)
        qkv[rows, : 2 * D] = mixed[:, : 2 * D]
        qkv[rows, 2 * D : 2 * D + SV] = arrived[:, D:]
        qkv[rows, 2 * D + SV :] = mixed[:, 2 * D :]
        for bucket, here in buckets_of(start, stop):

            def put(c, value):
                left[here, L1 + c : L1 + c + WIDE] = value.astype(BF)

            attention(qkv, here, bias_rows(lengths, bucket), put)
        message[...] = (x + dot(left[rows, L1 : L1 + D], w[:, FRESH : FRESH + D])).astype(BF)


def third_forward(start, stop, sec, gains, w, cot, arrived, *refs):
    left, right, slope, token, sems = refs[3:]
    rows = slice(start, stop)
    token[...] = jnp.zeros_like(token)

    @pl.when(sec[0] == 2)
    def _():
        left[rows, L1 : L1 + D] = arrived[...]
        left[rows, L3 : L3 + D] = cot[rows, :]
        hat = normalized(arrived[...].astype(F32))[0]
        left[rows, L2 : L2 + D] = (hat * gains[0:1, :]).astype(BF)
        forward_wide(left, right, slope, rows, w, 0, None, CHUNK)


def third_back_quarter(left, right, slope, w, other, at, rows):
    cols = pl.ds(at, FF // 4)
    grad = dot(left[rows, L3 : L3 + D], other[...]).astype(BF).astype(F32)
    lifted = (slope[rows, cols].astype(F32) * grad).astype(BF)
    right[rows, pl.ds(pl.multiple_of(R2 + at, 128), FF // 4)] = lifted
    return dot_nt(lifted, w[:, cols])


def third_back_first(start, stop, sec, spot, core, w, *refs):
    others, refs = refs[:3], refs[3:]
    slope, left, _r, _m, right, mid, sems = refs
    rows = slice(start, stop)

    @pl.when(sec[0] == 2)
    def _():
        at = quarters(core[0], (spot[0] + spot[1]) % 2)
        total = None
        for k, other in enumerate(others):
            part = third_back_quarter(left, right, slope, w, other, at[k], rows)
            total = part if total is None else total + part
        mid[rows, :] = total


def third_back(spans, sec, spot, core, gains, w, got, slope, left, mid, *refs):
    right, outs, gg, *messages, sems = refs[3:]
    rows = slice(spans[0][0], spans[-1][1])

    @pl.when(sec[0] == 2)
    def _():
        at = quarters(core[0], (spot[0] + spot[1]) % 2)[3]
        back = mid[rows, :] + third_back_quarter(left, right, slope, w, got, at, rows)
        hat, spread = normalized(left[rows, L1 : L1 + D].astype(F32))
        gg[0:1, :] += jnp.sum(back * hat, axis=0, keepdims=True)
        c = left[rows, L3 : L3 + D].astype(F32)
        resid = (c + norm_back(hat, spread, gains[0:1, :], back)).astype(BF)
        for (start, stop), message in zip(spans, messages):
            message[...] = resid[start - rows.start : stop - rows.start]
        outs[rows, :] = resid


def second_back(start, stop, sec, lengths, gains, w, outs, arrived, *refs):
    left, right, gg, qkv, message, sems = refs[4:]
    rows = slice(start, stop)

    @pl.when(sec[0] == 1)
    def _():
        right[rows, R1 : R1 + D] = arrived[...]
        grad = dot(arrived[...], w[:, TURNED : TURNED + D]).astype(BF)
        for bucket, here in buckets_of(start, stop):
            local = slice(here.start - start, here.stop - start)

            def put(c, dq, dk, dv):
                right[here, R0 + c : R0 + c + WIDE] = dq.astype(BF)
                right[here, R0 + D + c : R0 + D + c + WIDE] = dk.astype(BF)
                if c < SV:
                    if message.shape[1] > D:
                        message[local, D + c : D + c + WIDE] = dv.astype(BF)
                    else:
                        qkv[here, 2 * D + c : 2 * D + c + WIDE] = dv.astype(BF)
                else:
                    right[here, R0 + 2 * D + c - SV : R0 + 2 * D + c - SV + WIDE] = dv.astype(BF)

            attention_back(qkv, here, grad[local], bias_columns(lengths, bucket), put)
        back = None
        for c in range(0, FRESH, D):
            wide, at = min(D, FRESH - c), TURNED + D + c
            part = dot(right[rows, R0 + c : R0 + c + wide], w[:wide, at : at + D])
            back = part if back is None else back + part
        hat, spread = normalized(outs[rows, :].astype(F32))
        gg[0:1, :] += jnp.sum(back * hat, axis=0, keepdims=True)
        resid = arrived[...].astype(F32) + norm_back(hat, spread, gains[0:1, :], back)
        message[:, :D] = resid.astype(BF)
        left[rows, L3 : L3 + D] = resid.astype(BF)


def first_back_wide(start, stop, sec, gains, w, slope, arrived, *refs):
    right, mid, gg, sems = refs[3:]
    rows = slice(start, stop)

    @pl.when(sec[0] == 0)
    def _():
        grad = arrived[:, :D]
        back = None
        pulled = dot(grad, w[:, DOWN : DOWN + CHUNK])
        for c in range(FF // CHUNK):
            k = c * CHUNK
            ahead = None
            if k + CHUNK < FF:
                ahead = dot(grad, w[:, DOWN + k + CHUNK : DOWN + k + 2 * CHUNK])
            lifted = (slope[rows, k : k + CHUNK].astype(F32) * pulled).astype(BF)
            right[rows, R2 + k : R2 + k + CHUNK] = lifted
            part = dot_nt(lifted, w[:, UP + k : UP + k + CHUNK])
            back = part if back is None else back + part
            pulled = ahead
        hat, spread = normalized(mid[rows, :])
        gg[1:2, :] += jnp.sum(back * hat, axis=0, keepdims=True)
        resid = grad.astype(F32) + norm_back(hat, spread, gains[1:2, :], back)
        right[rows, R1 : R1 + D] = resid.astype(BF)
        mid[rows, :] = resid


def first_back_attend(start, stop, base, off, sec, lengths, gains, tokens, w, qkv, mid, arrived, *refs):
    right, outs, gg, token, sems = refs[3:]
    rows = slice(start, stop)
    token[...] = jnp.zeros_like(token)

    @pl.when(sec[0] == 0)
    def _():
        grad = dot_nt(right[rows, R1 : R1 + D], w[:, OUT : OUT + D]).astype(BF)
        for bucket, here in buckets_of(start, stop):
            local = slice(here.start - start, here.stop - start)

            def put(c, dq, dk, dv):
                right[here, R0 + c : R0 + c + WIDE] = dq.astype(BF)
                right[here, R0 + D + c : R0 + D + c + WIDE] = dk.astype(BF)
                if c < SV:
                    at = slice(here.start - base, here.stop - base)
                    dv = dv + arrived[at, off + c : off + c + WIDE].astype(F32)
                right[here, R0 + 2 * D + c : R0 + 2 * D + c + WIDE] = dv.astype(BF)

            attention_back(qkv, here, grad[local], bias_columns(lengths, bucket), put)
        back = dot_nt(right[rows, R0 : R0 + 3 * D], w[:, QKV : QKV + 3 * D])
        hat, spread = normalized(tokens[rows, :].astype(F32))
        gg[0:1, :] += jnp.sum(back * hat, axis=0, keepdims=True)
        outs[rows, :] = (mid[rows, :] + norm_back(hat, spread, gains[0:1, :], back)).astype(BF)


def last_forward(sec, spot, core, *refs):
    others, (_l, _r, left, right, result, sems) = refs[:4], refs[4:]

    @pl.when(sec[0] == 2)
    def _():
        total = left[:, L1 : L1 + D].astype(F32)
        for at, other in zip(quarters(core[0], (spot[0] + spot[1]) % 2), others):
            total = total + dot_nt(right[:, pl.ds(at, FF // 4)], other[...])
        result[...] = total.astype(BF)


def take_acts(sec, arrived, _r, right, sems):
    @pl.when(sec[0] == 1)
    def _():
        Loads(sems).start(arrived, right.at[:, pl.ds(R2, FF)]).wait()


def put_cached(sec, _q, qkv, out, sems):
    @pl.when(sec[0] == 1)
    def _():
        out[...] = qkv[qkv.shape[0] - out.shape[0] :, 2 * D : 2 * D + SV]


def put_acts(sec, acts, out, sem):
    @pl.when(sec[0] == 0)
    def _():
        Loads(sem).start(acts, out).wait()


def take_columns(sec, order, slab, piece, sems):
    @pl.when(sec[0] == 3)
    def _():
        wide = piece.shape[1]
        at = pl.multiple_of(order[0] * wide, 128)
        Loads(sems).start(slab.at[:, pl.ds(at, wide)], piece).wait()


def halve_rows(sec, piece, upper, lower):
    @pl.when(sec[0] == 2)
    def _():
        upper[...] = piece[: D // 2]
        lower[...] = piece[D // 2 :]


def gather_rows(sec, from_x, from_y, other):
    @pl.when(sec[0] == 2)
    def _():
        other[: D // 2, :] = from_x[...]
        other[D // 2 :, :] = from_y[...]


def quarters(core, odd):
    wide = FF // 4
    return [
        pl.multiple_of(which * HALF + parity * wide, 128)
        for which in (core, 1 - core)
        for parity in (odd, 1 - odd)
    ]


def by_core(core, whole, keep, send):
    wide = whole.shape[0] // 8
    for k in range(4):
        here = slice(k * wide, (k + 1) * wide)
        keep[here, :] = whole[pl.ds(pl.multiple_of((2 * k + core) * wide, wide), wide), :]
        send[here, :] = whole[pl.ds(pl.multiple_of((2 * k + 1 - core) * wide, wide), wide), :]


def shares(roles, extra, again, sec, core, gg, *refs):
    left, right, keep, send, sems, turned, whole = refs[3 if again else 2 :]

    def run(first, groups):
        before = None
        for j, group in enumerate(groups):
            if group != before:
                turned[...] = left[:, group * D : (group + 1) * D].T
            before = group
            whole[...] = dot(turned[...], right[:, first + j * D : first + (j + 1) * D]).astype(BF)
            cols = pl.ds(j * D, D)
            by_core(core[0], whole, keep.at[:, cols], send.at[:, cols])
        if extra:
            block = whole.at[:, pl.ds(0, 256)]
            block[...] = jnp.zeros((D, 256), BF)
            block[:, :8] = gg[...].T.astype(BF)
            cols = pl.ds(len(groups) * D, 256)
            by_core(core[0], block, keep.at[:, cols], send.at[:, cols])

    for part, (first, groups) in roles.items():
        pl.when(sec[0] == part)(functools.partial(run, first, groups))


def sum_first(spot, keep, got, send_a, send_b, mine_a, mine_b):
    part, half = send_a.shape[0] // 2, send_a.shape[1]
    x, y = spot[0], spot[1]

    def both(where, lo):
        rows = pl.ds(pl.multiple_of(where * part, part), part)
        cols = slice(lo, lo + half)
        return (keep[rows, cols].astype(F32) + got[rows, cols].astype(F32)).astype(BF)

    for k in range(2):
        here = slice(k * part, (k + 1) * part)
        send_a[here, :] = both(2 * k + 1 - x, 0)
        send_b[here, :] = both(2 * (1 - y) + k, half)
        mine_a[here, :] = both(2 * k + x, 0)
        mine_b[here, :] = both(2 * y + k, half)


def sum_second(spot, mine_a, mine_b, got_a, got_b, send_a, send_b, last_a, last_b):
    part = send_a.shape[0]
    x, y = spot[0], spot[1]

    def both(mine, got, where):
        rows = pl.ds(pl.multiple_of(where * part, part), part)
        return mine[rows, :].astype(F32) + got[rows, :].astype(F32)

    send_a[...] = both(mine_a, got_a, 1 - y).astype(BF)
    send_b[...] = both(mine_b, got_b, 1 - x).astype(BF)
    last_a[...] = both(mine_a, got_a, y).astype(BF)
    last_b[...] = both(mine_b, got_b, x).astype(BF)


def sum_last(last_a, got_a, last_b, got_b, total):
    half = last_a.shape[1]
    total[:, :half] = (last_a[...].astype(F32) + got_a[...].astype(F32)).astype(total.dtype)
    total[:, half:] = (last_b[...].astype(F32) + got_b[...].astype(F32)).astype(total.dtype)


def finish(sec, wide, narrow, moved, outs, result, grads, rows, gains):
    count = grads.shape[0]
    blank = functools.partial(jnp.zeros, dtype=F32)

    def total(four, lo, hi):
        half = four[0].shape[1]
        pieces = []
        for at in range(2):
            first, last = max(lo - at * half, 0), min(hi - at * half, half)
            if first < last:
                one, two = four[2 * at][:, first:last], four[2 * at + 1][:, first:last]
                pieces.append((at * half + first, one.astype(F32) + two.astype(F32)))
        return pieces

    def lay(four, lo, hi, to):
        for at, value in total(four, lo, hi):
            grads[:, to + at - lo : to + at - lo + value.shape[1]] = value

    def lay_gains(four):
        ((_, block),) = total(four, 4 * D, 4 * D + 128)
        gains[...] = block.T[:2]

    @pl.when(sec[0] == 0)
    def _():
        lay(narrow, 0, 4 * D, 0)
        lay(wide, 0, FF, UP)
        grads[:, DOWN:] = moved[...].astype(F32)
        lay_gains(narrow)

    @pl.when(sec[0] == 1)
    def _():
        lay(narrow, 0, FRESH, 0)
        lay(narrow, 3 * D, 4 * D, FRESH)
        grads[:, FRESH + D :] = blank((count, ALL - FRESH - D))
        lay_gains(narrow)

    @pl.when(sec[0] == 2)
    def _():
        lay(narrow, 0, FF, 0)
        grads[:, FF:] = blank((count, ALL - FF))
        lay_gains(narrow)

    @pl.when(sec[0] == 3)
    def _():
        grads[:, :FF] = moved[...].astype(F32)
        grads[:, FF:] = blank((count, ALL - FF))
        gains[...] = jnp.zeros_like(gains)
        rows[...] = result[...]

    @pl.when(sec[0] != 3)
    def _():
        rows[...] = outs[...]


def shape(rows, cols, dtype=BF):
    return jax.ShapeDtypeStruct((rows, cols), dtype)


def held(rows, cols, dtype=BF):
    return pltpu.VMEM((rows, cols), dtype)


def keep_in_vmem(array):
    return pltpu.with_memory_space_constraint(array, pltpu.VMEM)


def call(kernel, name, ins, states, outs, sems=1, scratch=(), after=(), limit=8, specs=None, cost=COST):
    operands = [a for a, _ in ins] + [keep_in_vmem(s) for s in states]
    aliases = {len(ins) + i: i for i in range(len(states))}
    out_shape = [held(*s.shape, s.dtype) for s in states] + list(outs)
    return pl.pallas_call(
        behind(kernel, len(operands), after),
        name=name,
        out_shape=out_shape,
        in_specs=[s for _, s in ins] + [VM] * len(states) + [ANY] * len(after),
        out_specs=[VM] * len(states) + list(specs or [VM] * len(outs)),
        scratch_shapes=[pltpu.SemaphoreType.DMA((sems,))] + list(scratch),
        input_output_aliases=aliases,
        compiler_params=pltpu.CompilerParams(vmem_limit_bytes=limit << 20),
        cost_estimate=pl.CostEstimate(flops=cost, bytes_accessed=1024, transcendentals=0),
    )(*operands, *after)


def behind(kernel, count, after):
    def ordered(*refs):
        kernel(*refs[:count], *refs[count + len(after) :])

    return ordered


def plain(kernel, name, operands, specs, outs, limit=8, scratch=(), after=(), out_specs=None, cost=COST):
    return pl.pallas_call(
        behind(kernel, len(operands), after),
        name=name,
        out_shape=outs,
        in_specs=specs + [ANY] * len(after),
        out_specs=out_specs or [VM] * len(outs),
        scratch_shapes=list(scratch),
        compiler_params=pltpu.CompilerParams(vmem_limit_bytes=limit << 20),
        cost_estimate=pl.CostEstimate(flops=cost, bytes_accessed=1024, transcendentals=0),
    )(*operands, *after)


def exchange_on(parts, block, bit):
    count, sections = lax.axis_size("dp"), lax.axis_size("section")
    pairs = [(i * sections + p, (i ^ bit) * sections + p) for p in parts for i in range(count)]
    return lax.ppermute(block, ("dp", "section"), pairs)


def shift(block, pairs):
    return lax.ppermute(block, "section", pairs)


def scatter_sum(name, parts, keep, got, sec, spot, after, cost, later=()):
    swap = functools.partial(exchange_on, parts)
    part, half = keep.shape[0] // 4, keep.shape[1] // 2
    pairs = len(got) == 2

    def only(kernel):
        def run(sec_ref, *refs):
            mine = sec_ref[0] == parts[0]
            for p in parts[1:]:
                mine = mine | (sec_ref[0] == p)

            @pl.when(mine)
            def _():
                kernel(*refs)

        return run

    def first(sec_ref, spot_ref, keep_ref, *refs):
        if not pairs:
            only(sum_first)(sec_ref, spot_ref, keep_ref, *refs)
            return
        here, there, *outs = refs

        @pl.when(sec_ref[0] == 0)
        def _():
            sum_first(spot_ref, keep_ref, here, *outs)

        @pl.when((sec_ref[0] == 1) | (sec_ref[0] == 2))
        def _():
            sum_first(spot_ref, keep_ref, there, *outs)

    send_a, send_b, mine_a, mine_b = plain(
        first,
        name + "_first",
        [sec, spot, *map(keep_in_vmem, (keep, *got))],
        [SM, SM, VM] + [VM] * len(got),
        [shape(2 * part, half)] * 4,
        6,
        after=after,
    )
    got_a, got_b = swap(send_a, 2), swap(send_b, 4)
    began = [mine_a]
    send_a, send_b, last_a, last_b = plain(
        only(sum_second),
        name + "_second",
        [sec, spot, mine_a, mine_b, got_a, got_b],
        [SM, SM, VM, VM, VM, VM],
        [shape(part, half)] * 4,
        after=later,
        cost=cost,
    )
    return (last_a, swap(send_a, 4), last_b, swap(send_b, 2)), began, [last_a]


def body(tokens, lengths, section_weights, norm_gains, cotangent):
    slab = pltpu.with_memory_space_constraint(section_weights[0], pltpu.HBM)
    gains = norm_gains[0]
    section = lax.axis_index("section")
    dp = lax.axis_size("dp")
    place = lax.axis_index("dp")
    split = dp == 8
    sec = section.astype(jnp.int32).reshape(1)
    core = (place % 2).astype(jnp.int32).reshape(1)
    spot = jnp.stack([(place // 2) % 2, (place // 4) % 2]).astype(jnp.int32)
    order = ((place % 2) * 2 + (place // 2 + place // 4) % 2).astype(jnp.int32).reshape(1)
    sec, core, spot, order, tokens = lax.optimization_barrier((sec, core, spot, order, tokens))
    total = tokens.shape[0]
    shard = D // dp
    sizes = SPLIT if sum(SPLIT) * ROWS == total else (1,) * (total // ROWS)
    bounds = []
    for size in sizes:
        first = bounds[-1][1] if bounds else 0
        bounds.append((first, first + size * ROWS))

    if split:
        piece = plain(
            take_columns,
            "take_columns",
            [sec, order, slab],
            [SM, SM, HB],
            [shape(D, FF // 4)],
            scratch=[pltpu.SemaphoreType.DMA((1,))],
        )[0]
    else:
        piece = lax.dynamic_slice(section_weights[0], (place * shard, 0), (shard, FF))
    piece = shift(piece, [(3, 2)])

    state = {}
    sent, sent_2, notes, made, cut = [], [], [], [], []

    def run_first(mb, after=()):
        start, stop = bounds[mb]
        fresh = mb == 0
        kernel = functools.partial(first_forward, start, stop, fresh)
        message = shape(stop - start, D + SV)
        ins = [(sec, SM), (lengths, SM), (gains, VM), (tokens, VM)]
        if fresh:
            names = ["w", "left", "acts", "qkv", "slope", "mid", "right", "outs", "gg"]
            arrays = [
                held(D, ALL),
                held(total, 4 * D),
                held(total, FF),
                held(total, 3 * D),
                held(total, FF),
                held(total, D, F32),
                held(total, 4 * D + FF),
                held(total, D),
                held(8, D, F32),
            ]
            results = call(kernel, "first_forward", ins + [(slab, HB)], [], arrays + [message], 16)
        else:
            names = ["left", "acts", "qkv", "slope", "mid"]
            ins += [(keep_in_vmem(state["w"]), VM)]
            results = call(
                kernel, "first_forward", ins, [state[n] for n in names], [message], after=after
            )
        state.update(zip(names, results))
        sent.append(shift(results[-1], [(0, 1)]))

    def send_acts():
        acts = plain(
            put_acts,
            "put_acts",
            [sec, keep_in_vmem(state["acts"])],
            [SM, VM],
            [pltpu.HBM((total, FF), BF)],
            scratch=[pltpu.SemaphoreType.DMA((1,))],
            after=[sent[-1], *sent_2[:1], *made],
            out_specs=[HB],
        )[0]
        return acts, shift(acts, [(0, 1)])

    def run_second(mb, after=()):
        start, stop = bounds[mb]
        names = ["left", "qkv", "outs"]
        results = call(
            functools.partial(second_forward, start, stop),
            "second_forward",
            [(sec, SM), (lengths, SM), (gains, VM), (keep_in_vmem(state["w"]), VM), (sent[mb], VM)],
            [state[n] for n in names],
            [shape(stop - start, D)],
            after=after,
        )
        state.update(zip(names, results))
        made.append(results[-1])
        sent_2.append(shift(results[-1], [(1, 2)]))

    def run_third(mb, after=()):
        start, stop = bounds[mb]
        names = ["left", "right", "slope"]
        results = call(
            functools.partial(third_forward, start, stop),
            "third_forward",
            [(sec, SM), (gains, VM), (keep_in_vmem(state["w"]), VM), (cotangent, VM), (sent_2[mb], VM)],
            [state[n] for n in names],
            [shape(8, 128, F32)],
            after=after,
        )
        state.update(zip(names, results))
        notes.append(results[-1])

    def halves():
        parts = plain(
            halve_rows,
            "halve_rows",
            [sec, piece],
            [SM, VM],
            [shape(D // 2, FF // 4)] * 2,
            after=[sent[-1], made[-1], sent_2[0]],
        )
        cut.extend(parts)
        return exchange_on([2], parts[0], 2), exchange_on([2], parts[1], 4)

    def gathered(from_x, from_y):
        return plain(
            gather_rows,
            "gather_rows",
            [sec, from_x, from_y],
            [SM, VM, VM],
            [shape(D, FF // 4)],
            after=[notes[-1]],
        )[0]

    if len(bounds) == 4 and split:
        run_first(0)
        run_first(1)
        run_first(2)
        run_second(0)
        run_first(3, after=[sent[1]])
        run_second(1, after=[sent[2]])
        run_second(2)
        swapped = exchange_on([2], piece, 1)
        sides = halves()
        run_third(0)
        acts, sent_acts = send_acts()
        run_second(3, after=[acts])
        run_third(1)
        run_third(2)
        run_third(3)
        other = gathered(*sides)
        parts_3 = [piece, other, swapped, exchange_on([2], other, 1)]
    else:
        for run in (run_first, run_second, run_third):
            for mb in range(len(bounds)):
                run(mb)
            if run is run_first:
                _, sent_acts = send_acts()
        if split:
            swapped = exchange_on([2], piece, 1)
            other = gathered(*halves())
            parts_3 = [piece, other, swapped, exchange_on([2], other, 1)]
        else:
            whole = lax.all_gather(piece, "dp", axis=0, tiled=True)
            wide_3 = FF // 4
            odd = (spot[0] + spot[1]) % 2
            parts_3 = [
                lax.dynamic_slice(whole, (0, which * HALF + parity * wide_3), (D, wide_3))
                for which in (core[0], 1 - core[0])
                for parity in (odd, 1 - odd)
            ]
    w = keep_in_vmem(state["w"])
    back_2, back_1 = [], []
    apart = bounds[len(bounds) // 2][0]

    def run_third_first(first, last):
        state["right"], state["mid"] = call(
            functools.partial(third_back_first, bounds[first][0], bounds[last - 1][1]),
            "third_back_first",
            [(sec, SM), (spot, SM), (core, SM), (w, VM)]
            + [(keep_in_vmem(part), VM) for part in parts_3[:3]]
            + [(keep_in_vmem(state[n]), VM) for n in ("slope", "left")],
            [state["right"], state["mid"]],
            [],
        )

    def run_third_back(first, last):
        names = ["right", "outs", "gg"]
        spans = bounds[first:last]
        results = call(
            functools.partial(third_back, spans),
            "third_back",
            [(sec, SM), (spot, SM), (core, SM), (gains, VM), (w, VM)]
            + [(keep_in_vmem(parts_3[3]), VM)]
            + [(keep_in_vmem(state[n]), VM) for n in ("slope", "left", "mid")],
            [state[n] for n in names],
            [shape(stop - start, D) for start, stop in spans],
        )
        state.update(zip(names, results))
        back_2.extend(shift(message, [(2, 1)]) for message in results[3:])

    def run_second_back(mb, after=()):
        start, stop = bounds[mb]
        names = ["left", "right", "gg", "qkv"]
        results = call(
            functools.partial(second_back, start, stop),
            "second_back",
            [(sec, SM), (lengths, SM), (gains, VM), (w, VM)]
            + [(keep_in_vmem(state["outs"]), VM), (back_2[mb], VM)],
            [state[n] for n in names],
            [shape(stop - start, D + SV if start < apart else D)],
            after=after,
        )
        state.update(zip(names, results))
        back_1.append(shift(results[-1], [(1, 0)]))

    for first in range(0, len(bounds), 2):
        last = min(first + 2, len(bounds))
        run_third_first(first, last)
        run_third_back(first, last)
    for mb in range(len(bounds)):
        run_second_back(mb, back_2[mb + 1 : mb + 2] if mb in (1, 2) else ())
    state["qkv"], cached = call(
        put_cached, "put_cached", [(sec, SM)], [state["qkv"]], [shape(total - apart, SV)]
    )
    cached = shift(cached, [(1, 0)])
    left, right, qkv, slope, mid, outs, gg = [
        state[n] for n in ("left", "right", "qkv", "slope", "mid", "outs", "gg")
    ]

    def own_shares(name, roles, extra, left, right, keep=None, after=()):
        width = 4 * D + (256 if extra else 0)
        rows = held(D // 2, width)
        states = [left, right] + ([] if keep is None else [keep])
        return call(
            functools.partial(shares, roles, extra, keep is not None),
            name,
            [(sec, SM), (core, SM), (keep_in_vmem(gg), VM)],
            states,
            [rows] * (2 if keep is None else 1),
            scratch=[pltpu.VMEM((D, total), BF), pltpu.VMEM((D, D), BF)],
            after=after,
        )

    def plain_sums(roles, extra):
        width = 4 * D + (256 if extra else 0)
        full = jnp.zeros((D, width), BF)
        for part, (first, groups) in roles.items():
            blocks = [
                lax.dot_general(
                    left[:, g * D : (g + 1) * D],
                    right[:, first + j * D : first + (j + 1) * D],
                    (((0,), (0,)), ((), ())),
                    preferred_element_type=F32,
                ).astype(BF)
                for j, g in enumerate(groups)
            ]
            if extra:
                blocks += [gg.T.astype(BF), jnp.zeros((D, 248), BF)]
            full = jnp.where(section == part, jnp.concatenate(blocks, axis=1), full)
        full = lax.psum_scatter(full, "dp", scatter_dimension=0, tiled=True)
        blank = jnp.zeros((shard, width // 2), BF)
        return full[:, : width // 2], blank, full[:, width // 2 :], blank

    def run_wide(mb):
        start, stop = bounds[mb]
        return call(
            functools.partial(first_back_wide, start, stop),
            "first_back_wide",
            [(sec, SM), (gains, VM), (w, VM), (keep_in_vmem(slope), VM), (back_1[mb], VM)],
            [right, mid, gg],
            [],
        )

    def run_attend(first, last, after=()):
        start, stop = bounds[first][0], bounds[last - 1][1]
        place_of, heads = ((start, D), back_1[first]) if start < apart else ((apart, 0), cached)
        return call(
            functools.partial(first_back_attend, start, stop, *place_of),
            "first_back_attend",
            [(sec, SM), (lengths, SM), (gains, VM), (tokens, VM), (w, VM)]
            + [(keep_in_vmem(qkv), VM), (keep_in_vmem(mid), VM), (heads, VM)],
            [right, outs, gg],
            [shape(8, 128, F32)],
            after=after,
        )

    up_roles = {0: (R2, [2] * 4)}
    down_roles = {1: (R2, [3] * 4), 2: (0, [3] * 4)}
    narrow_roles = {0: (R0, [0] * 3 + [1]), 1: (R0, [0] * 3 + [1]), 2: (R2, [2] * 4)}
    count = len(bounds)
    late = 1
    for mb in range(count):
        right, mid, gg = run_wide(mb)
        if mb < late:
            right, outs, gg, _ = run_attend(mb, mb + 1)
    def sum_up(four):
        return plain(
            sum_last, "wide_sum_last", list(four), [VM] * 4, [shape(shard, FF)], cost=8000000000
        )[0]

    tokens_of = []
    if split:
        left, right, keep, send = own_shares("up_grads", up_roles, False, left, right)
        got_up = exchange_on([0], send, 1)
    right = call(take_acts, "take_acts", [(sec, SM), (sent_acts, ANY)], [right], [])[0]
    if split:
        left, right, keep, send = own_shares("down_grads", down_roles, False, left, right, keep, [cached])
        got_down = exchange_on([1, 2], send, 1)
    rest = list(range(late, count))
    for mb in rest[:1]:
        right, outs, gg, token = run_attend(mb, mb + 1)
        tokens_of.append(token)
    if split:
        wide, begun, seconds = scatter_sum(
            "wide_sum", [0, 1, 2], keep, [got_up, got_down], sec, spot, tokens_of, 30000000000
        )
    for first, last in [(2, 4)] if count == 4 else [(mb, mb + 1) for mb in rest[1:]]:
        right, outs, gg, token = run_attend(first, last, begun if split else ())
    left, right, result = call(
        last_forward,
        "last_forward",
        [(sec, SM), (spot, SM), (core, SM)] + [(part, VM) for part in parts_3],
        [left, right],
        [shape(total, D)],
        limit=8,
    )
    result = shift(result, [(2, 3)])
    if split:
        moved = sum_up(wide)
        left, right, keep, send = own_shares("narrow_grads", narrow_roles, True, left, right)
        got_narrow = exchange_on([0, 1, 2], send, 1)
        narrow, _, _ = scatter_sum(
            "narrow_sum", [0, 1, 2], keep, [got_narrow], sec, spot, seconds, COST, [moved]
        )
    else:
        wide = plain_sums({**up_roles, **down_roles}, False)
        moved = sum_up(wide)
        narrow = plain_sums(narrow_roles, True)
    moved = shift(moved, [(1, 0), (2, 3)])

    def last(*refs):
        finish(refs[0], refs[1:5], refs[5:9], *refs[9:])

    grads, rows, gain_out = plain(
        last,
        "finish",
        [sec, *wide, *narrow, moved, outs, result],
        [SM] + [VM] * 11,
        [shape(shard, ALL, F32), shape(total, D), shape(2, shard, F32)],
        16,
    )
    return (rows[None], grads[None], gain_out[None])


def solution(mesh):
    placed = (
        P("dp", None),
        P("dp", None),
        P("section", None, None),
        P("section", None, None),
        P("dp", None),
    )
    return jax.shard_map(
        body,
        mesh=mesh,
        in_specs=placed,
        out_specs=(P("section", "dp", None), P("section", "dp", None), P("section", None, "dp")),
        check_vma=False,
    )
```

```python
import functools

import jax
import jax.numpy as jnp
from jax import lax
from jax.experimental import pallas as pl
from jax.experimental.pallas import tpu as pltpu
from jax.sharding import PartitionSpec as P

D = 768
HD = 64
FF = 3072
SV = 384
ROWS = 112
PAIRS = 6
WIDE = 2 * HD
EPS = 1e-05
BF = jnp.bfloat16
F32 = jnp.float32

SPLIT = (1, 1, 1, 1)

L0, L1, L2, L3 = 0, D, 2 * D, 3 * D
R0, R1, R2 = 0, 3 * D, 4 * D
ALL = 4 * D + 2 * FF

QKV, OUT, UP, DOWN = 0, 3 * D, 4 * D, 4 * D + FF
FRESH = 2 * D + D - SV
HALF = FF // 2
TURNED = 4 * D

VM = pl.BlockSpec(memory_space=pltpu.VMEM)
SM = pl.BlockSpec(memory_space=pltpu.SMEM)
HB = pl.BlockSpec(memory_space=pltpu.HBM)
ANY = pl.BlockSpec(memory_space=pl.ANY)


def dot(left, right):
    return jnp.dot(left, right, preferred_element_type=F32)


def dot_nt(left, right):
    return lax.dot_general(left, right, (((1,), (1,)), ((), ())), preferred_element_type=F32)


def normalized(rows):
    centered = rows - jnp.mean(rows, axis=-1, keepdims=True)
    spread = lax.rsqrt(jnp.mean(centered * centered, axis=-1, keepdims=True) + EPS)
    return centered * spread, spread


def norm_back(hat, spread, gain, grad):
    scaled = grad * gain
    inner = jnp.mean(scaled, axis=-1, keepdims=True)
    along = jnp.mean(scaled * hat, axis=-1, keepdims=True)
    return spread * (scaled - inner - hat * along)


def gelu_pair(u):
    c0 = 0.7978845608028654
    c1 = c0 * 0.044715
    square = u * u
    half = 0.5 + 0.5 * jnp.tanh(u * (c0 + c1 * square))
    act = u * half
    return act, half + act * ((1.0 - half) * (2.0 * c0 + (6.0 * c1) * square))


def sequence_start(lengths, bucket, i):
    e0 = lengths[bucket, 0]
    e1 = e0 + lengths[bucket, 1]
    e2 = e1 + lengths[bucket, 2]
    return jnp.where(i >= e2, e2, jnp.where(i >= e1, e1, jnp.where(i >= e0, e0, 0)))


def bias_rows(lengths, bucket):
    i = lax.broadcasted_iota(jnp.int32, (ROWS, ROWS), 0)
    j = lax.broadcasted_iota(jnp.int32, (ROWS, ROWS), 1)
    bias = jnp.where((j <= i) & (j >= sequence_start(lengths, bucket, i)), 0.0, -1e30)
    return jnp.concatenate([bias, bias], axis=0)


def bias_columns(lengths, bucket):
    j = lax.broadcasted_iota(jnp.int32, (ROWS, 2 * ROWS), 0)
    i = lax.broadcasted_iota(jnp.int32, (ROWS, 2 * ROWS), 1)
    i = jnp.where(i >= ROWS, i - ROWS, i)
    return jnp.where((j <= i) & (j >= sequence_start(lengths, bucket, i)), 0.0, -1e30)


def lane_masks(scale):
    low = lax.broadcasted_iota(jnp.int32, (ROWS, WIDE), 1) < HD
    return jnp.where(low, scale, 0.0).astype(BF), jnp.where(low, 0.0, scale).astype(BF)


def two_heads(block, masks):
    return jnp.concatenate([block * masks[0], block * masks[1]], axis=0)


def joined(stacked):
    low = lax.broadcasted_iota(jnp.int32, (ROWS, WIDE), 1) < HD
    return jnp.where(low, stacked[:ROWS], stacked[ROWS:])


def softmax(scores, axis):
    top = jnp.max(scores, axis=axis, keepdims=True)
    powers = jnp.exp(scores - top)
    return powers * (1.0 / jnp.sum(powers, axis=axis, keepdims=True))


def attention(qkv, rows, bias, put):
    masks = lane_masks(HD ** (-0.5))
    at = [WIDE * p for p in range(PAIRS)]
    scores = [
        dot_nt(two_heads(qkv[rows, c : c + WIDE], masks), qkv[rows, D + c : D + c + WIDE]) + bias
        for c in at
    ]
    probs = [softmax(s, -1).astype(BF) for s in scores]
    for c, p in zip(at, probs):
        put(c, joined(dot(p, qkv[rows, 2 * D + c : 2 * D + c + WIDE])))


def attention_back(qkv, rows, grad, bias, put):
    scaled = lane_masks(HD ** (-0.5))
    plain = lane_masks(1.0)
    at = [WIDE * p for p in range(PAIRS)]
    qs = [two_heads(qkv[rows, c : c + WIDE], scaled) for c in at]
    ks = [qkv[rows, D + c : D + c + WIDE] for c in at]
    vs = [qkv[rows, 2 * D + c : 2 * D + c + WIDE] for c in at]
    gs = [two_heads(grad[:, c : c + WIDE], plain) for c in at]
    scores = [dot_nt(k, q) + bias for k, q in zip(ks, qs)]
    grad_probs = [dot_nt(v, g) for v, g in zip(vs, gs)]
    probs = [softmax(s, 0) for s in scores]
    inner = [jnp.sum(d * p, axis=0, keepdims=True) for d, p in zip(grad_probs, probs)]
    grad_scores = [(p * (d - i)).astype(BF) for p, d, i in zip(probs, grad_probs, inner)]
    grad_v = [dot(p.astype(BF), g) for p, g in zip(probs, gs)]
    grad_k = [dot(s, q) for s, q in zip(grad_scores, qs)]
    turned = [s.T for s in grad_scores]
    grad_q = [joined(dot(t, k)) * HD ** (-0.5) for t, k in zip(turned, ks)]
    for c, dq, dk, dv in zip(at, grad_q, grad_k, grad_v):
        put(c, dq, dk, dv)


def buckets_of(start, stop):
    return [(b // ROWS, slice(b, b + ROWS)) for b in range(start, stop, ROWS)]


class Loads:
    def __init__(self, sems):
        self.sems = sems
        self.used = 0

    def start(self, src, dst):
        copy = pltpu.make_async_copy(src, dst, self.sems.at[self.used])
        self.used += 1
        copy.start()
        return copy


def forward_wide(left, store, slope, rows, w, up, down, chunk, waits=None):
    count = FF // chunk

    def lift(c):
        if waits:
            waits[0][c].wait()
        return dot(left[rows, L2 : L2 + D], w[:, up + c * chunk : up + (c + 1) * chunk])

    total = None
    here = lift(0)
    for c in range(count):
        ahead = lift(c + 1) if c + 1 < count else None
        act, gradient = gelu_pair(here)
        act = act.astype(BF)
        store[rows, c * chunk : (c + 1) * chunk] = act
        slope[rows, c * chunk : (c + 1) * chunk] = gradient.astype(BF)
        if down is not None:
            if waits:
                waits[1][c].wait()
            part = dot_nt(act, w[:, down + c * chunk : down + (c + 1) * chunk])
            total = part if total is None else total + part
        here = ahead
    return total


CHUNK = 512
COST = 1000


def first_forward(start, stop, fresh, sec, lengths, gains, tokens, *refs):
    if fresh:
        slab, refs = refs[0], refs[1:]
        w, left, acts, qkv, slope, mid, right, outs, gg, message, sems = refs
        gg[...] = jnp.zeros_like(gg)
    else:
        w, refs = refs[0], refs[1:]
        left, acts, qkv, slope, mid, message, sems = refs[5:]
    rows = slice(start, stop)
    if fresh:

        @pl.when(sec[0] == 1)
        def _():
            load = Loads(sems).start(slab.at[:, pl.ds(0, FRESH + D)], w.at[:, pl.ds(0, FRESH + D)])
            load.wait()
            w[:, TURNED : TURNED + D] = w[:, FRESH : FRESH + D].T
            for c in range(0, FRESH, D):
                wide = min(D, FRESH - c)
                at = TURNED + D + c
                w[:wide, at : at + D] = w[:, c : c + wide].T

        @pl.when(sec[0] == 2)
        def _():
            loads = Loads(sems)
            both = [
                loads.start(slab.at[:, pl.ds(at, HALF)], w.at[:, pl.ds(at, HALF)])
                for at in (0, HALF)
            ]
            for load in both:
                load.wait()

    @pl.when(sec[0] == 0)
    def _():
        loads = Loads(sems)
        first = second = waits = None
        if fresh:

            def get(at, wide):
                return loads.start(slab.at[:, pl.ds(at, wide)], w.at[:, pl.ds(at, wide)])

            first = [get(QKV + c * D, D) for c in range(3)]
            second = get(OUT, D)
            waits = ([], [])
            for c in range(FF // CHUNK):
                waits[0].append(get(UP + c * CHUNK, CHUNK))
                waits[1].append(get(DOWN + c * CHUNK, CHUNK))
        x = tokens[rows, :].astype(F32)
        low = (normalized(x)[0] * gains[0:1, :]).astype(BF)
        left[rows, L0 : L0 + D] = low
        for c in range(3):
            if fresh:
                first[c].wait()
            qkv[rows, c * D : (c + 1) * D] = dot(low, w[:, QKV + c * D : QKV + (c + 1) * D]).astype(BF)
        message[:, D:] = qkv[rows, 2 * D : 2 * D + SV]
        for bucket, here in buckets_of(start, stop):

            def put(c, value):
                left[here, L1 + c : L1 + c + WIDE] = value.astype(BF)

            attention(qkv, here, bias_rows(lengths, bucket), put)
        if fresh:
            second.wait()
        middle = x + dot(left[rows, L1 : L1 + D], w[:, OUT : OUT + D])
        mid[rows, :] = middle
        left[rows, L2 : L2 + D] = (normalized(middle)[0] * gains[1:2, :]).astype(BF)
        total = forward_wide(left, acts, slope, rows, w, UP, DOWN, CHUNK, waits)
        message[:, :D] = (middle + total).astype(BF)


def second_forward(start, stop, sec, lengths, gains, w, arrived, *refs):
    left, qkv, outs, message, sems = refs[3:]
    rows = slice(start, stop)

    @pl.when(sec[0] == 1)
    def _():
        outs[rows, :] = arrived[:, :D]
        x = arrived[:, :D].astype(F32)
        low = (normalized(x)[0] * gains[0:1, :]).astype(BF)
        left[rows, L0 : L0 + D] = low
        mixed = dot(low, w[:, :FRESH]).astype(BF)
        qkv[rows, : 2 * D] = mixed[:, : 2 * D]
        qkv[rows, 2 * D : 2 * D + SV] = arrived[:, D:]
        qkv[rows, 2 * D + SV :] = mixed[:, 2 * D :]
        for bucket, here in buckets_of(start, stop):

            def put(c, value):
                left[here, L1 + c : L1 + c + WIDE] = value.astype(BF)

            attention(qkv, here, bias_rows(lengths, bucket), put)
        message[...] = (x + dot(left[rows, L1 : L1 + D], w[:, FRESH : FRESH + D])).astype(BF)


def third_forward(start, stop, sec, gains, w, cot, arrived, *refs):
    left, right, slope, token, sems = refs[3:]
    rows = slice(start, stop)
    token[...] = jnp.zeros_like(token)

    @pl.when(sec[0] == 2)
    def _():
        left[rows, L1 : L1 + D] = arrived[...]
        left[rows, L3 : L3 + D] = cot[rows, :]
        hat = normalized(arrived[...].astype(F32))[0]
        left[rows, L2 : L2 + D] = (hat * gains[0:1, :]).astype(BF)
        forward_wide(left, right, slope, rows, w, 0, None, CHUNK)


def third_back_quarter(left, right, slope, w, other, at, rows):
    cols = pl.ds(at, FF // 4)
    grad = dot(left[rows, L3 : L3 + D], other[...]).astype(BF).astype(F32)
    lifted = (slope[rows, cols].astype(F32) * grad).astype(BF)
    right[rows, pl.ds(pl.multiple_of(R2 + at, 128), FF // 4)] = lifted
    return dot_nt(lifted, w[:, cols])


def third_back_first(start, stop, sec, spot, core, w, *refs):
    others, refs = refs[:3], refs[3:]
    slope, left, _r, _m, right, mid, sems = refs
    rows = slice(start, stop)

    @pl.when(sec[0] == 2)
    def _():
        at = quarters(core[0], (spot[0] + spot[1]) % 2)
        total = None
        for k, other in enumerate(others):
            part = third_back_quarter(left, right, slope, w, other, at[k], rows)
            total = part if total is None else total + part
        mid[rows, :] = total


def third_back(spans, sec, spot, core, gains, w, got, slope, left, mid, *refs):
    right, outs, gg, *messages, sems = refs[3:]
    rows = slice(spans[0][0], spans[-1][1])

    @pl.when(sec[0] == 2)
    def _():
        at = quarters(core[0], (spot[0] + spot[1]) % 2)[3]
        back = mid[rows, :] + third_back_quarter(left, right, slope, w, got, at, rows)
        hat, spread = normalized(left[rows, L1 : L1 + D].astype(F32))
        gg[0:1, :] += jnp.sum(back * hat, axis=0, keepdims=True)
        c = left[rows, L3 : L3 + D].astype(F32)
        resid = (c + norm_back(hat, spread, gains[0:1, :], back)).astype(BF)
        for (start, stop), message in zip(spans, messages):
            message[...] = resid[start - rows.start : stop - rows.start]
        outs[rows, :] = resid


def second_back(start, stop, sec, lengths, gains, w, outs, arrived, *refs):
    left, right, gg, qkv, message, sems = refs[4:]
    rows = slice(start, stop)

    @pl.when(sec[0] == 1)
    def _():
        right[rows, R1 : R1 + D] = arrived[...]
        grad = dot(arrived[...], w[:, TURNED : TURNED + D]).astype(BF)
        for bucket, here in buckets_of(start, stop):
            local = slice(here.start - start, here.stop - start)

            def put(c, dq, dk, dv):
                right[here, R0 + c : R0 + c + WIDE] = dq.astype(BF)
                right[here, R0 + D + c : R0 + D + c + WIDE] = dk.astype(BF)
                if c < SV:
                    if message.shape[1] > D:
                        message[local, D + c : D + c + WIDE] = dv.astype(BF)
                    else:
                        qkv[here, 2 * D + c : 2 * D + c + WIDE] = dv.astype(BF)
                else:
                    right[here, R0 + 2 * D + c - SV : R0 + 2 * D + c - SV + WIDE] = dv.astype(BF)

            attention_back(qkv, here, grad[local], bias_columns(lengths, bucket), put)
        back = None
        for c in range(0, FRESH, D):
            wide, at = min(D, FRESH - c), TURNED + D + c
            part = dot(right[rows, R0 + c : R0 + c + wide], w[:wide, at : at + D])
            back = part if back is None else back + part
        hat, spread = normalized(outs[rows, :].astype(F32))
        gg[0:1, :] += jnp.sum(back * hat, axis=0, keepdims=True)
        resid = arrived[...].astype(F32) + norm_back(hat, spread, gains[0:1, :], back)
        message[:, :D] = resid.astype(BF)
        left[rows, L3 : L3 + D] = resid.astype(BF)


def first_back_wide(start, stop, sec, gains, w, slope, arrived, *refs):
    right, mid, gg, sems = refs[3:]
    rows = slice(start, stop)

    @pl.when(sec[0] == 0)
    def _():
        grad = arrived[:, :D]
        back = None
        pulled = dot(grad, w[:, DOWN : DOWN + CHUNK])
        for c in range(FF // CHUNK):
            k = c * CHUNK
            ahead = None
            if k + CHUNK < FF:
                ahead = dot(grad, w[:, DOWN + k + CHUNK : DOWN + k + 2 * CHUNK])
            lifted = (slope[rows, k : k + CHUNK].astype(F32) * pulled).astype(BF)
            right[rows, R2 + k : R2 + k + CHUNK] = lifted
            part = dot_nt(lifted, w[:, UP + k : UP + k + CHUNK])
            back = part if back is None else back + part
            pulled = ahead
        hat, spread = normalized(mid[rows, :])
        gg[1:2, :] += jnp.sum(back * hat, axis=0, keepdims=True)
        resid = grad.astype(F32) + norm_back(hat, spread, gains[1:2, :], back)
        right[rows, R1 : R1 + D] = resid.astype(BF)
        mid[rows, :] = resid


def first_back_attend(start, stop, base, off, sec, lengths, gains, tokens, w, qkv, mid, arrived, *refs):
    right, outs, gg, token, sems = refs[3:]
    rows = slice(start, stop)
    token[...] = jnp.zeros_like(token)

    @pl.when(sec[0] == 0)
    def _():
        grad = dot_nt(right[rows, R1 : R1 + D], w[:, OUT : OUT + D]).astype(BF)
        for bucket, here in buckets_of(start, stop):
            local = slice(here.start - start, here.stop - start)

            def put(c, dq, dk, dv):
                right[here, R0 + c : R0 + c + WIDE] = dq.astype(BF)
                right[here, R0 + D + c : R0 + D + c + WIDE] = dk.astype(BF)
                if c < SV:
                    at = slice(here.start - base, here.stop - base)
                    dv = dv + arrived[at, off + c : off + c + WIDE].astype(F32)
                right[here, R0 + 2 * D + c : R0 + 2 * D + c + WIDE] = dv.astype(BF)

            attention_back(qkv, here, grad[local], bias_columns(lengths, bucket), put)
        back = dot_nt(right[rows, R0 : R0 + 3 * D], w[:, QKV : QKV + 3 * D])
        hat, spread = normalized(tokens[rows, :].astype(F32))
        gg[0:1, :] += jnp.sum(back * hat, axis=0, keepdims=True)
        outs[rows, :] = (mid[rows, :] + norm_back(hat, spread, gains[0:1, :], back)).astype(BF)


def last_forward(sec, spot, core, *refs):
    others, (_l, _r, left, right, result, sems) = refs[:4], refs[4:]

    @pl.when(sec[0] == 2)
    def _():
        total = left[:, L1 : L1 + D].astype(F32)
        for at, other in zip(quarters(core[0], (spot[0] + spot[1]) % 2), others):
            total = total + dot_nt(right[:, pl.ds(at, FF // 4)], other[...])
        result[...] = total.astype(BF)


def take_acts(sec, arrived, _r, right, sems):
    @pl.when(sec[0] == 1)
    def _():
        Loads(sems).start(arrived, right.at[:, pl.ds(R2, FF)]).wait()


def put_cached(sec, _q, qkv, out, sems):
    @pl.when(sec[0] == 1)
    def _():
        out[...] = qkv[qkv.shape[0] - out.shape[0] :, 2 * D : 2 * D + SV]


def put_acts(sec, acts, out, sem):
    @pl.when(sec[0] == 0)
    def _():
        Loads(sem).start(acts, out).wait()


def take_columns(sec, order, slab, piece, sems):
    @pl.when(sec[0] == 3)
    def _():
        wide = piece.shape[1]
        at = pl.multiple_of(order[0] * wide, 128)
        Loads(sems).start(slab.at[:, pl.ds(at, wide)], piece).wait()


def halve_rows(sec, piece, upper, lower):
    @pl.when(sec[0] == 2)
    def _():
        upper[...] = piece[: D // 2]
        lower[...] = piece[D // 2 :]


def gather_rows(sec, from_x, from_y, other):
    @pl.when(sec[0] == 2)
    def _():
        other[: D // 2, :] = from_x[...]
        other[D // 2 :, :] = from_y[...]


def quarters(core, odd):
    wide = FF // 4
    return [
        pl.multiple_of(which * HALF + parity * wide, 128)
        for which in (core, 1 - core)
        for parity in (odd, 1 - odd)
    ]


def by_core(core, whole, keep, send):
    wide = whole.shape[0] // 8
    for k in range(4):
        here = slice(k * wide, (k + 1) * wide)
        keep[here, :] = whole[pl.ds(pl.multiple_of((2 * k + core) * wide, wide), wide), :]
        send[here, :] = whole[pl.ds(pl.multiple_of((2 * k + 1 - core) * wide, wide), wide), :]


def shares(roles, extra, again, sec, core, gg, *refs):
    left, right, keep, send, sems, turned, whole = refs[3 if again else 2 :]

    def run(first, groups):
        before = None
        for j, group in enumerate(groups):
            if group != before:
                turned[...] = left[:, group * D : (group + 1) * D].T
            before = group
            whole[...] = dot(turned[...], right[:, first + j * D : first + (j + 1) * D]).astype(BF)
            cols = pl.ds(j * D, D)
            by_core(core[0], whole, keep.at[:, cols], send.at[:, cols])
        if extra:
            block = whole.at[:, pl.ds(0, 256)]
            block[...] = jnp.zeros((D, 256), BF)
            block[:, :8] = gg[...].T.astype(BF)
            cols = pl.ds(len(groups) * D, 256)
            by_core(core[0], block, keep.at[:, cols], send.at[:, cols])

    for part, (first, groups) in roles.items():
        pl.when(sec[0] == part)(functools.partial(run, first, groups))


def sum_first(spot, keep, got, send_a, send_b, mine_a, mine_b):
    part, half = send_a.shape[0] // 2, send_a.shape[1]
    x, y = spot[0], spot[1]

    def both(where, lo):
        rows = pl.ds(pl.multiple_of(where * part, part), part)
        cols = slice(lo, lo + half)
        return (keep[rows, cols].astype(F32) + got[rows, cols].astype(F32)).astype(BF)

    for k in range(2):
        here = slice(k * part, (k + 1) * part)
        send_a[here, :] = both(2 * k + 1 - x, 0)
        send_b[here, :] = both(2 * (1 - y) + k, half)
        mine_a[here, :] = both(2 * k + x, 0)
        mine_b[here, :] = both(2 * y + k, half)


def sum_second(spot, mine_a, mine_b, got_a, got_b, send_a, send_b, last_a, last_b):
    part = send_a.shape[0]
    x, y = spot[0], spot[1]

    def both(mine, got, where):
        rows = pl.ds(pl.multiple_of(where * part, part), part)
        return mine[rows, :].astype(F32) + got[rows, :].astype(F32)

    send_a[...] = both(mine_a, got_a, 1 - y).astype(BF)
    send_b[...] = both(mine_b, got_b, 1 - x).astype(BF)
    last_a[...] = both(mine_a, got_a, y).astype(BF)
    last_b[...] = both(mine_b, got_b, x).astype(BF)


def sum_last(last_a, got_a, last_b, got_b, total):
    half = last_a.shape[1]
    total[:, :half] = (last_a[...].astype(F32) + got_a[...].astype(F32)).astype(total.dtype)
    total[:, half:] = (last_b[...].astype(F32) + got_b[...].astype(F32)).astype(total.dtype)


def pieces_of(four, lo, hi):
    half = four[0].shape[1]
    found = []
    for at in range(2):
        first, last = max(lo - at * half, 0), min(hi - at * half, half)
        if first < last:
            one, two = four[2 * at][:, first:last], four[2 * at + 1][:, first:last]
            found.append((at * half + first, one.astype(F32) + two.astype(F32)))
    return found


def lay(four, lo, hi, block, to):
    for at, value in pieces_of(four, lo, hi):
        block[:, to + at - lo : to + at - lo + value.shape[1]] = value


def finish_wide(sec, wide, moved, outs, result, grads, rows, block, sems):
    count = block.shape[0]

    def write(first):
        cols = pl.ds(first, ALL - first)
        Loads(sems).start(block.at[:, cols], grads.at[:, cols]).wait()

    @pl.when(sec[0] == 0)
    def _():
        lay(wide, 0, FF, block, UP)
        block[:, DOWN:] = moved[...].astype(F32)
        write(UP)

    for part, first in ((1, FRESH + D), (2, FF)):

        @pl.when(sec[0] == part)
        def _(first=first):
            block[:, first:] = jnp.zeros((count, ALL - first), F32)
            write(first)

    @pl.when(sec[0] == 3)
    def _():
        block[:, :FF] = moved[...].astype(F32)
        block[:, FF:] = jnp.zeros((count, ALL - FF), F32)
        write(0)
        rows[...] = result[...]

    @pl.when(sec[0] != 3)
    def _():
        rows[...] = outs[...]


def finish_narrow(sec, narrow, _g, grads, gains, block, sems):
    def write(last):
        cols = pl.ds(0, last)
        Loads(sems).start(block.at[:, cols], grads.at[:, cols]).wait()

    @pl.when(sec[0] == 3)
    def _():
        gains[...] = jnp.zeros_like(gains)

    @pl.when(sec[0] != 3)
    def _():
        ((_, value),) = pieces_of(narrow, 4 * D, 4 * D + 128)
        gains[...] = value.T[:2]

    @pl.when((sec[0] == 0) | (sec[0] == 2))
    def _():
        lay(narrow, 0, 4 * D, block, 0)
        write(4 * D)

    @pl.when(sec[0] == 1)
    def _():
        lay(narrow, 0, FRESH, block, 0)
        lay(narrow, 3 * D, 4 * D, block, FRESH)
        write(FRESH + D)


def shape(rows, cols, dtype=BF):
    return jax.ShapeDtypeStruct((rows, cols), dtype)


def held(rows, cols, dtype=BF):
    return pltpu.VMEM((rows, cols), dtype)


def keep_in_vmem(array):
    return pltpu.with_memory_space_constraint(array, pltpu.VMEM)


def call(kernel, name, ins, states, outs, sems=1, scratch=(), after=(), limit=8, specs=None, cost=COST):
    operands = [a for a, _ in ins] + [keep_in_vmem(s) for s in states]
    aliases = {len(ins) + i: i for i in range(len(states))}
    out_shape = [held(*s.shape, s.dtype) for s in states] + list(outs)
    return pl.pallas_call(
        behind(kernel, len(operands), after),
        name=name,
        out_shape=out_shape,
        in_specs=[s for _, s in ins] + [VM] * len(states) + [ANY] * len(after),
        out_specs=[VM] * len(states) + list(specs or [VM] * len(outs)),
        scratch_shapes=[pltpu.SemaphoreType.DMA((sems,))] + list(scratch),
        input_output_aliases=aliases,
        compiler_params=pltpu.CompilerParams(vmem_limit_bytes=limit << 20),
        cost_estimate=pl.CostEstimate(flops=cost, bytes_accessed=1024, transcendentals=0),
    )(*operands, *after)


def behind(kernel, count, after):
    def ordered(*refs):
        kernel(*refs[:count], *refs[count + len(after) :])

    return ordered


def plain(kernel, name, operands, specs, outs, limit=8, scratch=(), after=(), out_specs=None, cost=COST, aliases=None):
    return pl.pallas_call(
        behind(kernel, len(operands), after),
        name=name,
        out_shape=outs,
        in_specs=specs + [ANY] * len(after),
        out_specs=out_specs or [VM] * len(outs),
        scratch_shapes=list(scratch),
        input_output_aliases=aliases or {},
        compiler_params=pltpu.CompilerParams(vmem_limit_bytes=limit << 20),
        cost_estimate=pl.CostEstimate(flops=cost, bytes_accessed=1024, transcendentals=0),
    )(*operands, *after)


def exchange_on(parts, block, bit):
    count, sections = lax.axis_size("dp"), lax.axis_size("section")
    pairs = [(i * sections + p, (i ^ bit) * sections + p) for p in parts for i in range(count)]
    return lax.ppermute(block, ("dp", "section"), pairs)


def shift(block, pairs):
    return lax.ppermute(block, "section", pairs)


def scatter_sum(name, parts, keep, got, sec, spot, after, cost, later=()):
    swap = functools.partial(exchange_on, parts)
    part, half = keep.shape[0] // 4, keep.shape[1] // 2
    pairs = len(got) == 2

    def only(kernel):
        def run(sec_ref, *refs):
            mine = sec_ref[0] == parts[0]
            for p in parts[1:]:
                mine = mine | (sec_ref[0] == p)

            @pl.when(mine)
            def _():
                kernel(*refs)

        return run

    def first(sec_ref, spot_ref, keep_ref, *refs):
        if not pairs:
            only(sum_first)(sec_ref, spot_ref, keep_ref, *refs)
            return
        here, there, *outs = refs

        @pl.when(sec_ref[0] == 0)
        def _():
            sum_first(spot_ref, keep_ref, here, *outs)

        @pl.when((sec_ref[0] == 1) | (sec_ref[0] == 2))
        def _():
            sum_first(spot_ref, keep_ref, there, *outs)

    send_a, send_b, mine_a, mine_b = plain(
        first,
        name + "_first",
        [sec, spot, *map(keep_in_vmem, (keep, *got))],
        [SM, SM, VM] + [VM] * len(got),
        [shape(2 * part, half)] * 4,
        6,
        after=after,
    )
    got_a, got_b = swap(send_a, 2), swap(send_b, 4)
    began = [mine_a]
    send_a, send_b, last_a, last_b = plain(
        only(sum_second),
        name + "_second",
        [sec, spot, mine_a, mine_b, got_a, got_b],
        [SM, SM, VM, VM, VM, VM],
        [shape(part, half)] * 4,
        after=later,
        cost=cost,
    )
    return (last_a, swap(send_a, 4), last_b, swap(send_b, 2)), began, [last_a]


def body(tokens, lengths, section_weights, norm_gains, cotangent):
    slab = pltpu.with_memory_space_constraint(section_weights[0], pltpu.HBM)
    gains = norm_gains[0]
    section = lax.axis_index("section")
    dp = lax.axis_size("dp")
    place = lax.axis_index("dp")
    split = dp == 8
    sec = section.astype(jnp.int32).reshape(1)
    core = (place % 2).astype(jnp.int32).reshape(1)
    spot = jnp.stack([(place // 2) % 2, (place // 4) % 2]).astype(jnp.int32)
    order = ((place % 2) * 2 + (place // 2 + place // 4) % 2).astype(jnp.int32).reshape(1)
    sec, core, spot, order, tokens = lax.optimization_barrier((sec, core, spot, order, tokens))
    total = tokens.shape[0]
    shard = D // dp
    sizes = SPLIT if sum(SPLIT) * ROWS == total else (1,) * (total // ROWS)
    bounds = []
    for size in sizes:
        first = bounds[-1][1] if bounds else 0
        bounds.append((first, first + size * ROWS))

    if split:
        piece = plain(
            take_columns,
            "take_columns",
            [sec, order, slab],
            [SM, SM, HB],
            [shape(D, FF // 4)],
            scratch=[pltpu.SemaphoreType.DMA((1,))],
        )[0]
    else:
        piece = lax.dynamic_slice(section_weights[0], (place * shard, 0), (shard, FF))
    piece = shift(piece, [(3, 2)])

    state = {}
    sent, sent_2, notes, made, cut = [], [], [], [], []

    def run_first(mb, after=()):
        start, stop = bounds[mb]
        fresh = mb == 0
        kernel = functools.partial(first_forward, start, stop, fresh)
        message = shape(stop - start, D + SV)
        ins = [(sec, SM), (lengths, SM), (gains, VM), (tokens, VM)]
        if fresh:
            names = ["w", "left", "acts", "qkv", "slope", "mid", "right", "outs", "gg"]
            arrays = [
                held(D, ALL),
                held(total, 4 * D),
                held(total, FF),
                held(total, 3 * D),
                held(total, FF),
                held(total, D, F32),
                held(total, 4 * D + FF),
                held(total, D),
                held(8, D, F32),
            ]
            results = call(kernel, "first_forward", ins + [(slab, HB)], [], arrays + [message], 16)
        else:
            names = ["left", "acts", "qkv", "slope", "mid"]
            ins += [(keep_in_vmem(state["w"]), VM)]
            results = call(
                kernel, "first_forward", ins, [state[n] for n in names], [message], after=after
            )
        state.update(zip(names, results))
        sent.append(shift(results[-1], [(0, 1)]))

    def send_acts():
        acts = plain(
            put_acts,
            "put_acts",
            [sec, keep_in_vmem(state["acts"])],
            [SM, VM],
            [pltpu.HBM((total, FF), BF)],
            scratch=[pltpu.SemaphoreType.DMA((1,))],
            after=[sent[-1], *sent_2[:1], *made],
            out_specs=[HB],
        )[0]
        return acts, shift(acts, [(0, 1)])

    def run_second(mb, after=()):
        start, stop = bounds[mb]
        names = ["left", "qkv", "outs"]
        results = call(
            functools.partial(second_forward, start, stop),
            "second_forward",
            [(sec, SM), (lengths, SM), (gains, VM), (keep_in_vmem(state["w"]), VM), (sent[mb], VM)],
            [state[n] for n in names],
            [shape(stop - start, D)],
            after=after,
        )
        state.update(zip(names, results))
        made.append(results[-1])
        sent_2.append(shift(results[-1], [(1, 2)]))

    def run_third(mb, after=()):
        start, stop = bounds[mb]
        names = ["left", "right", "slope"]
        results = call(
            functools.partial(third_forward, start, stop),
            "third_forward",
            [(sec, SM), (gains, VM), (keep_in_vmem(state["w"]), VM), (cotangent, VM), (sent_2[mb], VM)],
            [state[n] for n in names],
            [shape(8, 128, F32)],
            after=after,
        )
        state.update(zip(names, results))
        notes.append(results[-1])

    def halves():
        parts = plain(
            halve_rows,
            "halve_rows",
            [sec, piece],
            [SM, VM],
            [shape(D // 2, FF // 4)] * 2,
            after=[sent[-1], made[-1], sent_2[0]],
        )
        cut.extend(parts)
        return exchange_on([2], parts[0], 2), exchange_on([2], parts[1], 4)

    def gathered(from_x, from_y):
        return plain(
            gather_rows,
            "gather_rows",
            [sec, from_x, from_y],
            [SM, VM, VM],
            [shape(D, FF // 4)],
            after=[notes[-1]],
        )[0]

    if len(bounds) == 4 and split:
        run_first(0)
        run_first(1)
        run_first(2)
        run_second(0)
        run_first(3, after=[sent[1]])
        run_second(1, after=[sent[2]])
        run_second(2)
        swapped = exchange_on([2], piece, 1)
        sides = halves()
        run_third(0)
        acts, sent_acts = send_acts()
        run_second(3, after=[acts])
        run_third(1)
        run_third(2)
        run_third(3)
        other = gathered(*sides)
        parts_3 = [piece, other, swapped, exchange_on([2], other, 1)]
    else:
        for run in (run_first, run_second, run_third):
            for mb in range(len(bounds)):
                run(mb)
            if run is run_first:
                _, sent_acts = send_acts()
        if split:
            swapped = exchange_on([2], piece, 1)
            other = gathered(*halves())
            parts_3 = [piece, other, swapped, exchange_on([2], other, 1)]
        else:
            whole = lax.all_gather(piece, "dp", axis=0, tiled=True)
            wide_3 = FF // 4
            odd = (spot[0] + spot[1]) % 2
            parts_3 = [
                lax.dynamic_slice(whole, (0, which * HALF + parity * wide_3), (D, wide_3))
                for which in (core[0], 1 - core[0])
                for parity in (odd, 1 - odd)
            ]
    w = keep_in_vmem(state["w"])
    back_2, back_1 = [], []
    apart = bounds[len(bounds) // 2][0]

    def run_third_first(first, last):
        state["right"], state["mid"] = call(
            functools.partial(third_back_first, bounds[first][0], bounds[last - 1][1]),
            "third_back_first",
            [(sec, SM), (spot, SM), (core, SM), (w, VM)]
            + [(keep_in_vmem(part), VM) for part in parts_3[:3]]
            + [(keep_in_vmem(state[n]), VM) for n in ("slope", "left")],
            [state["right"], state["mid"]],
            [],
        )

    def run_third_back(first, last):
        names = ["right", "outs", "gg"]
        spans = bounds[first:last]
        results = call(
            functools.partial(third_back, spans),
            "third_back",
            [(sec, SM), (spot, SM), (core, SM), (gains, VM), (w, VM)]
            + [(keep_in_vmem(parts_3[3]), VM)]
            + [(keep_in_vmem(state[n]), VM) for n in ("slope", "left", "mid")],
            [state[n] for n in names],
            [shape(stop - start, D) for start, stop in spans],
        )
        state.update(zip(names, results))
        back_2.extend(shift(message, [(2, 1)]) for message in results[3:])

    def run_second_back(mb, after=()):
        start, stop = bounds[mb]
        names = ["left", "right", "gg", "qkv"]
        results = call(
            functools.partial(second_back, start, stop),
            "second_back",
            [(sec, SM), (lengths, SM), (gains, VM), (w, VM)]
            + [(keep_in_vmem(state["outs"]), VM), (back_2[mb], VM)],
            [state[n] for n in names],
            [shape(stop - start, D + SV if start < apart else D)],
            after=after,
        )
        state.update(zip(names, results))
        back_1.append(shift(results[-1], [(1, 0)]))

    for first in range(0, len(bounds), 2):
        last = min(first + 2, len(bounds))
        run_third_first(first, last)
        run_third_back(first, last)
    for mb in range(len(bounds)):
        run_second_back(mb, back_2[mb + 1 : mb + 2] if mb in (1, 2) else ())
    state["qkv"], cached = call(
        put_cached, "put_cached", [(sec, SM)], [state["qkv"]], [shape(total - apart, SV)]
    )
    cached = shift(cached, [(1, 0)])
    left, right, qkv, slope, mid, outs, gg = [
        state[n] for n in ("left", "right", "qkv", "slope", "mid", "outs", "gg")
    ]

    def own_shares(name, roles, extra, left, right, keep=None, after=()):
        width = 4 * D + (256 if extra else 0)
        rows = held(D // 2, width)
        states = [left, right] + ([] if keep is None else [keep])
        return call(
            functools.partial(shares, roles, extra, keep is not None),
            name,
            [(sec, SM), (core, SM), (keep_in_vmem(gg), VM)],
            states,
            [rows] * (2 if keep is None else 1),
            scratch=[pltpu.VMEM((D, total), BF), pltpu.VMEM((D, D), BF)],
            after=after,
        )

    def plain_sums(roles, extra):
        width = 4 * D + (256 if extra else 0)
        full = jnp.zeros((D, width), BF)
        for part, (first, groups) in roles.items():
            blocks = [
                lax.dot_general(
                    left[:, g * D : (g + 1) * D],
                    right[:, first + j * D : first + (j + 1) * D],
                    (((0,), (0,)), ((), ())),
                    preferred_element_type=F32,
                ).astype(BF)
                for j, g in enumerate(groups)
            ]
            if extra:
                blocks += [gg.T.astype(BF), jnp.zeros((D, 248), BF)]
            full = jnp.where(section == part, jnp.concatenate(blocks, axis=1), full)
        full = lax.psum_scatter(full, "dp", scatter_dimension=0, tiled=True)
        blank = jnp.zeros((shard, width // 2), BF)
        return full[:, : width // 2], blank, full[:, width // 2 :], blank

    def run_wide(mb):
        start, stop = bounds[mb]
        return call(
            functools.partial(first_back_wide, start, stop),
            "first_back_wide",
            [(sec, SM), (gains, VM), (w, VM), (keep_in_vmem(slope), VM), (back_1[mb], VM)],
            [right, mid, gg],
            [],
        )

    def run_attend(first, last, after=()):
        start, stop = bounds[first][0], bounds[last - 1][1]
        place_of, heads = ((start, D), back_1[first]) if start < apart else ((apart, 0), cached)
        return call(
            functools.partial(first_back_attend, start, stop, *place_of),
            "first_back_attend",
            [(sec, SM), (lengths, SM), (gains, VM), (tokens, VM), (w, VM)]
            + [(keep_in_vmem(qkv), VM), (keep_in_vmem(mid), VM), (heads, VM)],
            [right, outs, gg],
            [shape(8, 128, F32)],
            after=after,
        )

    up_roles = {0: (R2, [2] * 4)}
    down_roles = {1: (R2, [3] * 4), 2: (0, [3] * 4)}
    narrow_roles = {0: (R0, [0] * 3 + [1]), 1: (R0, [0] * 3 + [1]), 2: (R2, [2] * 4)}
    count = len(bounds)
    late = 1
    for mb in range(count):
        right, mid, gg = run_wide(mb)
        if mb < late:
            right, outs, gg, _ = run_attend(mb, mb + 1)
    def sum_up(four):
        return plain(
            sum_last, "wide_sum_last", list(four), [VM] * 4, [shape(shard, FF)], cost=8000000000
        )[0]

    tokens_of = []
    if split:
        left, right, keep, send = own_shares("up_grads", up_roles, False, left, right)
        got_up = exchange_on([0], send, 1)
    right = call(take_acts, "take_acts", [(sec, SM), (sent_acts, ANY)], [right], [])[0]
    if split:
        left, right, keep, send = own_shares("down_grads", down_roles, False, left, right, keep, [cached])
        got_down = exchange_on([1, 2], send, 1)
    rest = list(range(late, count))
    for mb in rest[:1]:
        right, outs, gg, token = run_attend(mb, mb + 1)
        tokens_of.append(token)
    if split:
        wide, begun, seconds = scatter_sum(
            "wide_sum", [0, 1, 2], keep, [got_up, got_down], sec, spot, tokens_of, 30000000000
        )
    for first, last in [(2, 4)] if count == 4 else [(mb, mb + 1) for mb in rest[1:]]:
        right, outs, gg, token = run_attend(first, last, begun if split else ())
    left, right, result = call(
        last_forward,
        "last_forward",
        [(sec, SM), (spot, SM), (core, SM)] + [(part, VM) for part in parts_3],
        [left, right],
        [shape(total, D)],
        limit=8,
    )
    result = shift(result, [(2, 3)])
    if split:
        moved = sum_up(wide)
        left, right, keep, send = own_shares("narrow_grads", narrow_roles, True, left, right)
        got_narrow = exchange_on([0, 1, 2], send, 1)
        narrow, _, _ = scatter_sum(
            "narrow_sum", [0, 1, 2], keep, [got_narrow], sec, spot, seconds, COST, [moved]
        )
    else:
        wide = plain_sums({**up_roles, **down_roles}, False)
        moved = sum_up(wide)
        narrow = plain_sums(narrow_roles, True)
    moved = shift(moved, [(1, 0), (2, 3)])

    sems = pltpu.SemaphoreType.DMA((1,))
    grads, rows = plain(
        lambda *refs: finish_wide(refs[0], refs[1:5], *refs[5:]),
        "finish_wide",
        [sec, *wide, moved, outs, result],
        [SM] + [VM] * 7,
        [pltpu.HBM((shard, ALL), F32), shape(total, D)],
        12,
        [pltpu.VMEM((shard, ALL), F32), sems],
        out_specs=[HB, VM],
    )
    grads, gain_out = plain(
        lambda *refs: finish_narrow(refs[0], refs[1:5], *refs[5:]),
        "finish_narrow",
        [sec, *narrow, grads],
        [SM] + [VM] * 4 + [HB],
        [pltpu.HBM((shard, ALL), F32), shape(2, shard, F32)],
        8,
        [pltpu.VMEM((shard, 4 * D), F32), sems],
        out_specs=[HB, VM],
        aliases={5: 0},
    )
    return (rows[None], grads[None], gain_out[None])


def solution(mesh):
    placed = (
        P("dp", None),
        P("dp", None),
        P("section", None, None),
        P("section", None, None),
        P("dp", None),
    )
    return jax.shard_map(
        body,
        mesh=mesh,
        in_specs=placed,
        out_specs=(P("section", "dp", None), P("section", "dp", None), P("section", None, "dp")),
        check_vma=False,
    )
```

```python
import functools

import jax
import jax.numpy as jnp
from jax import lax
from jax.experimental import pallas as pl
from jax.experimental.pallas import tpu as pltpu
from jax.sharding import PartitionSpec as P

D = 768
HD = 64
FF = 3072
SV = 384
ROWS = 112
PAIRS = 6
WIDE = 2 * HD
EPS = 1e-05
BF = jnp.bfloat16
F32 = jnp.float32

SPLIT = (1, 1, 1, 1)

L0, L1, L2, L3 = 0, D, 2 * D, 3 * D
R0, R1, R2 = 0, 3 * D, 4 * D
ALL = 4 * D + 2 * FF

QKV, OUT, UP, DOWN = 0, 3 * D, 4 * D, 4 * D + FF
FRESH = 2 * D + D - SV
HALF = FF // 2
TURNED = 4 * D

VM = pl.BlockSpec(memory_space=pltpu.VMEM)
SM = pl.BlockSpec(memory_space=pltpu.SMEM)
HB = pl.BlockSpec(memory_space=pltpu.HBM)
ANY = pl.BlockSpec(memory_space=pl.ANY)


def dot(left, right):
    return jnp.dot(left, right, preferred_element_type=F32)


def dot_nt(left, right):
    return lax.dot_general(left, right, (((1,), (1,)), ((), ())), preferred_element_type=F32)


def normalized(rows):
    centered = rows - jnp.mean(rows, axis=-1, keepdims=True)
    spread = lax.rsqrt(jnp.mean(centered * centered, axis=-1, keepdims=True) + EPS)
    return centered * spread, spread


def norm_back(hat, spread, gain, grad):
    scaled = grad * gain
    inner = jnp.mean(scaled, axis=-1, keepdims=True)
    along = jnp.mean(scaled * hat, axis=-1, keepdims=True)
    return spread * (scaled - inner - hat * along)


def gelu_pair(u):
    c0 = 0.7978845608028654
    c1 = c0 * 0.044715
    square = u * u
    half = 0.5 + 0.5 * jnp.tanh(u * (c0 + c1 * square))
    act = u * half
    return act, half + act * ((1.0 - half) * (2.0 * c0 + (6.0 * c1) * square))


def sequence_start(lengths, bucket, i):
    e0 = lengths[bucket, 0]
    e1 = e0 + lengths[bucket, 1]
    e2 = e1 + lengths[bucket, 2]
    return jnp.where(i >= e2, e2, jnp.where(i >= e1, e1, jnp.where(i >= e0, e0, 0)))


def bias_rows(lengths, bucket):
    i = lax.broadcasted_iota(jnp.int32, (ROWS, ROWS), 0)
    j = lax.broadcasted_iota(jnp.int32, (ROWS, ROWS), 1)
    bias = jnp.where((j <= i) & (j >= sequence_start(lengths, bucket, i)), 0.0, -1e30)
    return jnp.concatenate([bias, bias], axis=0)


def bias_columns(lengths, bucket):
    j = lax.broadcasted_iota(jnp.int32, (ROWS, 2 * ROWS), 0)
    i = lax.broadcasted_iota(jnp.int32, (ROWS, 2 * ROWS), 1)
    i = jnp.where(i >= ROWS, i - ROWS, i)
    return jnp.where((j <= i) & (j >= sequence_start(lengths, bucket, i)), 0.0, -1e30)


def lane_masks(scale):
    low = lax.broadcasted_iota(jnp.int32, (ROWS, WIDE), 1) < HD
    return jnp.where(low, scale, 0.0).astype(BF), jnp.where(low, 0.0, scale).astype(BF)


def two_heads(block, masks):
    return jnp.concatenate([block * masks[0], block * masks[1]], axis=0)


def joined(stacked):
    low = lax.broadcasted_iota(jnp.int32, (ROWS, WIDE), 1) < HD
    return jnp.where(low, stacked[:ROWS], stacked[ROWS:])


def softmax(scores, axis):
    top = jnp.max(scores, axis=axis, keepdims=True)
    powers = jnp.exp(scores - top)
    return powers * (1.0 / jnp.sum(powers, axis=axis, keepdims=True))


def attention(qkv, rows, bias, put):
    masks = lane_masks(HD ** (-0.5))
    at = [WIDE * p for p in range(PAIRS)]
    scores = [
        dot_nt(two_heads(qkv[rows, c : c + WIDE], masks), qkv[rows, D + c : D + c + WIDE]) + bias
        for c in at
    ]
    probs = [softmax(s, -1).astype(BF) for s in scores]
    for c, p in zip(at, probs):
        put(c, joined(dot(p, qkv[rows, 2 * D + c : 2 * D + c + WIDE])))


def attention_back(qkv, rows, grad, bias, put):
    scaled = lane_masks(HD ** (-0.5))
    plain = lane_masks(1.0)
    at = [WIDE * p for p in range(PAIRS)]
    qs = [two_heads(qkv[rows, c : c + WIDE], scaled) for c in at]
    ks = [qkv[rows, D + c : D + c + WIDE] for c in at]
    vs = [qkv[rows, 2 * D + c : 2 * D + c + WIDE] for c in at]
    gs = [two_heads(grad[:, c : c + WIDE], plain) for c in at]
    scores = [dot_nt(k, q) + bias for k, q in zip(ks, qs)]
    grad_probs = [dot_nt(v, g) for v, g in zip(vs, gs)]
    probs = [softmax(s, 0) for s in scores]
    inner = [jnp.sum(d * p, axis=0, keepdims=True) for d, p in zip(grad_probs, probs)]
    grad_scores = [(p * (d - i)).astype(BF) for p, d, i in zip(probs, grad_probs, inner)]
    grad_v = [dot(p.astype(BF), g) for p, g in zip(probs, gs)]
    grad_k = [dot(s, q) for s, q in zip(grad_scores, qs)]
    turned = [s.T for s in grad_scores]
    grad_q = [joined(dot(t, k)) * HD ** (-0.5) for t, k in zip(turned, ks)]
    for c, dq, dk, dv in zip(at, grad_q, grad_k, grad_v):
        put(c, dq, dk, dv)


def buckets_of(start, stop):
    return [(b // ROWS, slice(b, b + ROWS)) for b in range(start, stop, ROWS)]


class Loads:
    def __init__(self, sems):
        self.sems = sems
        self.used = 0

    def start(self, src, dst):
        copy = pltpu.make_async_copy(src, dst, self.sems.at[self.used])
        self.used += 1
        copy.start()
        return copy


def forward_wide(left, store, slope, rows, w, up, down, chunk, waits=None):
    count = FF // chunk

    def lift(c):
        if waits:
            waits[0][c].wait()
        return dot(left[rows, L2 : L2 + D], w[:, up + c * chunk : up + (c + 1) * chunk])

    total = None
    here = lift(0)
    for c in range(count):
        ahead = lift(c + 1) if c + 1 < count else None
        act, gradient = gelu_pair(here)
        act = act.astype(BF)
        store[rows, c * chunk : (c + 1) * chunk] = act
        slope[rows, c * chunk : (c + 1) * chunk] = gradient.astype(BF)
        if down is not None:
            if waits:
                waits[1][c].wait()
            part = dot_nt(act, w[:, down + c * chunk : down + (c + 1) * chunk])
            total = part if total is None else total + part
        here = ahead
    return total


CHUNK = 512
COST = 1000


def first_forward(start, stop, fresh, sec, lengths, gains, tokens, *refs):
    if fresh:
        slab, refs = refs[0], refs[1:]
        w, left, acts, qkv, slope, mid, right, outs, gg, message, sems = refs
        gg[...] = jnp.zeros_like(gg)
    else:
        w, refs = refs[0], refs[1:]
        left, acts, qkv, slope, mid, message, sems = refs[5:]
    rows = slice(start, stop)
    if fresh:

        @pl.when(sec[0] == 1)
        def _():
            load = Loads(sems).start(slab.at[:, pl.ds(0, FRESH + D)], w.at[:, pl.ds(0, FRESH + D)])
            load.wait()
            w[:, TURNED : TURNED + D] = w[:, FRESH : FRESH + D].T
            for c in range(0, FRESH, D):
                wide = min(D, FRESH - c)
                at = TURNED + D + c
                w[:wide, at : at + D] = w[:, c : c + wide].T

        @pl.when(sec[0] == 2)
        def _():
            loads = Loads(sems)
            both = [
                loads.start(slab.at[:, pl.ds(at, HALF)], w.at[:, pl.ds(at, HALF)])
                for at in (0, HALF)
            ]
            for load in both:
                load.wait()

    @pl.when(sec[0] == 0)
    def _():
        loads = Loads(sems)
        first = second = waits = None
        if fresh:

            def get(at, wide):
                return loads.start(slab.at[:, pl.ds(at, wide)], w.at[:, pl.ds(at, wide)])

            first = [get(QKV + c * D, D) for c in range(3)]
            second = get(OUT, D)
            waits = ([], [])
            for c in range(FF // CHUNK):
                waits[0].append(get(UP + c * CHUNK, CHUNK))
                waits[1].append(get(DOWN + c * CHUNK, CHUNK))
        x = tokens[rows, :].astype(F32)
        low = (normalized(x)[0] * gains[0:1, :]).astype(BF)
        left[rows, L0 : L0 + D] = low
        for c in range(3):
            if fresh:
                first[c].wait()
            qkv[rows, c * D : (c + 1) * D] = dot(low, w[:, QKV + c * D : QKV + (c + 1) * D]).astype(BF)
        message[:, D:] = qkv[rows, 2 * D : 2 * D + SV]
        for bucket, here in buckets_of(start, stop):

            def put(c, value):
                left[here, L1 + c : L1 + c + WIDE] = value.astype(BF)

            attention(qkv, here, bias_rows(lengths, bucket), put)
        if fresh:
            second.wait()
        middle = x + dot(left[rows, L1 : L1 + D], w[:, OUT : OUT + D])
        mid[rows, :] = middle
        left[rows, L2 : L2 + D] = (normalized(middle)[0] * gains[1:2, :]).astype(BF)
        total = forward_wide(left, acts, slope, rows, w, UP, DOWN, CHUNK, waits)
        message[:, :D] = (middle + total).astype(BF)


def second_forward(start, stop, sec, lengths, gains, w, arrived, *refs):
    left, qkv, outs, message, sems = refs[3:]
    rows = slice(start, stop)

    @pl.when(sec[0] == 1)
    def _():
        outs[rows, :] = arrived[:, :D]
        x = arrived[:, :D].astype(F32)
        low = (normalized(x)[0] * gains[0:1, :]).astype(BF)
        left[rows, L0 : L0 + D] = low
        mixed = dot(low, w[:, :FRESH]).astype(BF)
        qkv[rows, : 2 * D] = mixed[:, : 2 * D]
        qkv[rows, 2 * D : 2 * D + SV] = arrived[:, D:]
        qkv[rows, 2 * D + SV :] = mixed[:, 2 * D :]
        for bucket, here in buckets_of(start, stop):

            def put(c, value):
                left[here, L1 + c : L1 + c + WIDE] = value.astype(BF)

            attention(qkv, here, bias_rows(lengths, bucket), put)
        message[...] = (x + dot(left[rows, L1 : L1 + D], w[:, FRESH : FRESH + D])).astype(BF)


def third_forward(start, stop, sec, gains, w, cot, arrived, *refs):
    left, right, slope, token, sems = refs[3:]
    rows = slice(start, stop)
    token[...] = jnp.zeros_like(token)

    @pl.when(sec[0] == 2)
    def _():
        left[rows, L1 : L1 + D] = arrived[...]
        left[rows, L3 : L3 + D] = cot[rows, :]
        hat = normalized(arrived[...].astype(F32))[0]
        left[rows, L2 : L2 + D] = (hat * gains[0:1, :]).astype(BF)
        forward_wide(left, right, slope, rows, w, 0, None, CHUNK)


def third_back_quarter(left, right, slope, w, other, at, rows):
    cols = pl.ds(at, FF // 4)
    grad = dot(left[rows, L3 : L3 + D], other[...]).astype(BF).astype(F32)
    lifted = (slope[rows, cols].astype(F32) * grad).astype(BF)
    right[rows, pl.ds(pl.multiple_of(R2 + at, 128), FF // 4)] = lifted
    return dot_nt(lifted, w[:, cols])


def third_back_first(start, stop, sec, spot, core, w, *refs):
    others, refs = refs[:3], refs[3:]
    slope, left, _r, _m, right, mid, sems = refs
    rows = slice(start, stop)

    @pl.when(sec[0] == 2)
    def _():
        at = quarters(core[0], (spot[0] + spot[1]) % 2)
        total = None
        for k, other in enumerate(others):
            part = third_back_quarter(left, right, slope, w, other, at[k], rows)
            total = part if total is None else total + part
        mid[rows, :] = total


def third_back(spans, sec, spot, core, gains, w, got, slope, left, mid, *refs):
    right, outs, gg, *messages, sems = refs[3:]
    rows = slice(spans[0][0], spans[-1][1])

    @pl.when(sec[0] == 2)
    def _():
        at = quarters(core[0], (spot[0] + spot[1]) % 2)[3]
        back = mid[rows, :] + third_back_quarter(left, right, slope, w, got, at, rows)
        hat, spread = normalized(left[rows, L1 : L1 + D].astype(F32))
        gg[0:1, :] += jnp.sum(back * hat, axis=0, keepdims=True)
        c = left[rows, L3 : L3 + D].astype(F32)
        resid = (c + norm_back(hat, spread, gains[0:1, :], back)).astype(BF)
        for (start, stop), message in zip(spans, messages):
            message[...] = resid[start - rows.start : stop - rows.start]
        outs[rows, :] = resid


def second_back(start, stop, sec, lengths, gains, w, outs, arrived, *refs):
    left, right, gg, qkv, message, sems = refs[4:]
    rows = slice(start, stop)

    @pl.when(sec[0] == 1)
    def _():
        right[rows, R1 : R1 + D] = arrived[...]
        grad = dot(arrived[...], w[:, TURNED : TURNED + D]).astype(BF)
        for bucket, here in buckets_of(start, stop):
            local = slice(here.start - start, here.stop - start)

            def put(c, dq, dk, dv):
                right[here, R0 + c : R0 + c + WIDE] = dq.astype(BF)
                right[here, R0 + D + c : R0 + D + c + WIDE] = dk.astype(BF)
                if c < SV:
                    if message.shape[1] > D:
                        message[local, D + c : D + c + WIDE] = dv.astype(BF)
                    else:
                        qkv[here, 2 * D + c : 2 * D + c + WIDE] = dv.astype(BF)
                else:
                    right[here, R0 + 2 * D + c - SV : R0 + 2 * D + c - SV + WIDE] = dv.astype(BF)

            attention_back(qkv, here, grad[local], bias_columns(lengths, bucket), put)
        back = None
        for c in range(0, FRESH, D):
            wide, at = min(D, FRESH - c), TURNED + D + c
            part = dot(right[rows, R0 + c : R0 + c + wide], w[:wide, at : at + D])
            back = part if back is None else back + part
        hat, spread = normalized(outs[rows, :].astype(F32))
        gg[0:1, :] += jnp.sum(back * hat, axis=0, keepdims=True)
        resid = arrived[...].astype(F32) + norm_back(hat, spread, gains[0:1, :], back)
        message[:, :D] = resid.astype(BF)
        left[rows, L3 : L3 + D] = resid.astype(BF)


def first_back_wide(start, stop, sec, gains, w, slope, arrived, *refs):
    right, mid, gg, sems = refs[3:]
    rows = slice(start, stop)

    @pl.when(sec[0] == 0)
    def _():
        grad = arrived[:, :D]
        back = None
        pulled = dot(grad, w[:, DOWN : DOWN + CHUNK])
        for c in range(FF // CHUNK):
            k = c * CHUNK
            ahead = None
            if k + CHUNK < FF:
                ahead = dot(grad, w[:, DOWN + k + CHUNK : DOWN + k + 2 * CHUNK])
            lifted = (slope[rows, k : k + CHUNK].astype(F32) * pulled).astype(BF)
            right[rows, R2 + k : R2 + k + CHUNK] = lifted
            part = dot_nt(lifted, w[:, UP + k : UP + k + CHUNK])
            back = part if back is None else back + part
            pulled = ahead
        hat, spread = normalized(mid[rows, :])
        gg[1:2, :] += jnp.sum(back * hat, axis=0, keepdims=True)
        resid = grad.astype(F32) + norm_back(hat, spread, gains[1:2, :], back)
        right[rows, R1 : R1 + D] = resid.astype(BF)
        mid[rows, :] = resid


def first_back_attend(start, stop, base, off, sec, lengths, gains, tokens, w, qkv, mid, arrived, *refs):
    right, outs, gg, token, sems = refs[3:]
    rows = slice(start, stop)
    token[...] = jnp.zeros_like(token)

    @pl.when(sec[0] == 0)
    def _():
        grad = dot_nt(right[rows, R1 : R1 + D], w[:, OUT : OUT + D]).astype(BF)
        for bucket, here in buckets_of(start, stop):
            local = slice(here.start - start, here.stop - start)

            def put(c, dq, dk, dv):
                right[here, R0 + c : R0 + c + WIDE] = dq.astype(BF)
                right[here, R0 + D + c : R0 + D + c + WIDE] = dk.astype(BF)
                if c < SV:
                    at = slice(here.start - base, here.stop - base)
                    dv = dv + arrived[at, off + c : off + c + WIDE].astype(F32)
                right[here, R0 + 2 * D + c : R0 + 2 * D + c + WIDE] = dv.astype(BF)

            attention_back(qkv, here, grad[local], bias_columns(lengths, bucket), put)
        back = dot_nt(right[rows, R0 : R0 + 3 * D], w[:, QKV : QKV + 3 * D])
        hat, spread = normalized(tokens[rows, :].astype(F32))
        gg[0:1, :] += jnp.sum(back * hat, axis=0, keepdims=True)
        outs[rows, :] = (mid[rows, :] + norm_back(hat, spread, gains[0:1, :], back)).astype(BF)


def last_forward(sec, spot, core, *refs):
    others, (_l, _r, left, right, result, sems) = refs[:4], refs[4:]

    @pl.when(sec[0] == 2)
    def _():
        total = left[:, L1 : L1 + D].astype(F32)
        for at, other in zip(quarters(core[0], (spot[0] + spot[1]) % 2), others):
            total = total + dot_nt(right[:, pl.ds(at, FF // 4)], other[...])
        result[...] = total.astype(BF)


def take_acts(sec, arrived, _r, right, sems):
    @pl.when(sec[0] == 1)
    def _():
        Loads(sems).start(arrived, right.at[:, pl.ds(R2, FF)]).wait()


def put_cached(sec, _q, qkv, out, sems):
    @pl.when(sec[0] == 1)
    def _():
        out[...] = qkv[qkv.shape[0] - out.shape[0] :, 2 * D : 2 * D + SV]


def put_acts(sec, acts, out, token, sem):
    token[...] = jnp.zeros_like(token)

    @pl.when(sec[0] == 0)
    def _():
        Loads(sem).start(acts, out).wait()


def take_columns(sec, order, slab, piece, sems):
    @pl.when(sec[0] == 3)
    def _():
        wide = piece.shape[1]
        at = pl.multiple_of(order[0] * wide, 128)
        Loads(sems).start(slab.at[:, pl.ds(at, wide)], piece).wait()


def halve_rows(sec, piece, upper, lower):
    @pl.when(sec[0] == 2)
    def _():
        upper[...] = piece[: D // 2]
        lower[...] = piece[D // 2 :]


def gather_rows(sec, from_x, from_y, other):
    @pl.when(sec[0] == 2)
    def _():
        other[: D // 2, :] = from_x[...]
        other[D // 2 :, :] = from_y[...]


def quarters(core, odd):
    wide = FF // 4
    return [
        pl.multiple_of(which * HALF + parity * wide, 128)
        for which in (core, 1 - core)
        for parity in (odd, 1 - odd)
    ]


def by_core(core, whole, keep, send):
    wide = whole.shape[0] // 8
    for k in range(4):
        here = slice(k * wide, (k + 1) * wide)
        keep[here, :] = whole[pl.ds(pl.multiple_of((2 * k + core) * wide, wide), wide), :]
        send[here, :] = whole[pl.ds(pl.multiple_of((2 * k + 1 - core) * wide, wide), wide), :]


def shares(roles, extra, again, sec, core, gg, *refs):
    left, right, keep, send, sems, turned, whole = refs[3 if again else 2 :]

    def run(first, groups):
        before = None
        for j, group in enumerate(groups):
            if group != before:
                turned[...] = left[:, group * D : (group + 1) * D].T
            before = group
            whole[...] = dot(turned[...], right[:, first + j * D : first + (j + 1) * D]).astype(BF)
            cols = pl.ds(j * D, D)
            by_core(core[0], whole, keep.at[:, cols], send.at[:, cols])
        if extra:
            block = whole.at[:, pl.ds(0, 256)]
            block[...] = jnp.zeros((D, 256), BF)
            block[:, :8] = gg[...].T.astype(BF)
            cols = pl.ds(len(groups) * D, 256)
            by_core(core[0], block, keep.at[:, cols], send.at[:, cols])

    for part, (first, groups) in roles.items():
        pl.when(sec[0] == part)(functools.partial(run, first, groups))


def sum_first(spot, keep, got, send_a, send_b, mine_a, mine_b):
    part, half = send_a.shape[0] // 2, send_a.shape[1]
    x, y = spot[0], spot[1]

    def both(where, lo):
        rows = pl.ds(pl.multiple_of(where * part, part), part)
        cols = slice(lo, lo + half)
        return (keep[rows, cols].astype(F32) + got[rows, cols].astype(F32)).astype(BF)

    for k in range(2):
        here = slice(k * part, (k + 1) * part)
        send_a[here, :] = both(2 * k + 1 - x, 0)
        send_b[here, :] = both(2 * (1 - y) + k, half)
        mine_a[here, :] = both(2 * k + x, 0)
        mine_b[here, :] = both(2 * y + k, half)


def sum_second(spot, mine_a, mine_b, got_a, got_b, send_a, send_b, last_a, last_b):
    part = send_a.shape[0]
    x, y = spot[0], spot[1]

    def both(mine, got, where):
        rows = pl.ds(pl.multiple_of(where * part, part), part)
        return mine[rows, :].astype(F32) + got[rows, :].astype(F32)

    send_a[...] = both(mine_a, got_a, 1 - y).astype(BF)
    send_b[...] = both(mine_b, got_b, 1 - x).astype(BF)
    last_a[...] = both(mine_a, got_a, y).astype(BF)
    last_b[...] = both(mine_b, got_b, x).astype(BF)


def sum_last(last_a, got_a, last_b, got_b, total):
    half = last_a.shape[1]
    total[:, :half] = (last_a[...].astype(F32) + got_a[...].astype(F32)).astype(total.dtype)
    total[:, half:] = (last_b[...].astype(F32) + got_b[...].astype(F32)).astype(total.dtype)


def pieces_of(four, lo, hi):
    half = four[0].shape[1]
    found = []
    for at in range(2):
        first, last = max(lo - at * half, 0), min(hi - at * half, half)
        if first < last:
            one, two = four[2 * at][:, first:last], four[2 * at + 1][:, first:last]
            found.append((at * half + first, one.astype(F32) + two.astype(F32)))
    return found


def lay(four, lo, hi, block, to):
    for at, value in pieces_of(four, lo, hi):
        block[:, to + at - lo : to + at - lo + value.shape[1]] = value


def finish_wide(sec, wide, moved, outs, result, grads, rows, block, sems):
    count = block.shape[0]

    def write(first):
        cols = pl.ds(first, ALL - first)
        Loads(sems).start(block.at[:, cols], grads.at[:, cols]).wait()

    @pl.when(sec[0] == 0)
    def _():
        lay(wide, 0, FF, block, UP)
        block[:, DOWN:] = moved[...].astype(F32)
        write(UP)

    for part, first in ((1, FRESH + D), (2, FF)):

        @pl.when(sec[0] == part)
        def _(first=first):
            block[:, first:] = jnp.zeros((count, ALL - first), F32)
            write(first)

    @pl.when(sec[0] == 3)
    def _():
        block[:, :FF] = moved[...].astype(F32)
        block[:, FF:] = jnp.zeros((count, ALL - FF), F32)
        write(0)
        rows[...] = result[...]

    @pl.when(sec[0] != 3)
    def _():
        rows[...] = outs[...]


def finish_narrow(sec, narrow, _g, grads, gains, block, sems):
    def write(last):
        cols = pl.ds(0, last)
        Loads(sems).start(block.at[:, cols], grads.at[:, cols]).wait()

    @pl.when(sec[0] == 3)
    def _():
        gains[...] = jnp.zeros_like(gains)

    @pl.when(sec[0] != 3)
    def _():
        ((_, value),) = pieces_of(narrow, 4 * D, 4 * D + 128)
        gains[...] = value.T[:2]

    @pl.when((sec[0] == 0) | (sec[0] == 2))
    def _():
        lay(narrow, 0, 4 * D, block, 0)
        write(4 * D)

    @pl.when(sec[0] == 1)
    def _():
        lay(narrow, 0, FRESH, block, 0)
        lay(narrow, 3 * D, 4 * D, block, FRESH)
        write(FRESH + D)


def shape(rows, cols, dtype=BF):
    return jax.ShapeDtypeStruct((rows, cols), dtype)


def held(rows, cols, dtype=BF):
    return pltpu.VMEM((rows, cols), dtype)


def keep_in_vmem(array):
    return pltpu.with_memory_space_constraint(array, pltpu.VMEM)


def call(kernel, name, ins, states, outs, sems=1, scratch=(), after=(), limit=8, specs=None, cost=COST):
    operands = [a for a, _ in ins] + [keep_in_vmem(s) for s in states]
    aliases = {len(ins) + i: i for i in range(len(states))}
    out_shape = [held(*s.shape, s.dtype) for s in states] + list(outs)
    return pl.pallas_call(
        behind(kernel, len(operands), after),
        name=name,
        out_shape=out_shape,
        in_specs=[s for _, s in ins] + [VM] * len(states) + [ANY] * len(after),
        out_specs=[VM] * len(states) + list(specs or [VM] * len(outs)),
        scratch_shapes=[pltpu.SemaphoreType.DMA((sems,))] + list(scratch),
        input_output_aliases=aliases,
        compiler_params=pltpu.CompilerParams(vmem_limit_bytes=limit << 20),
        cost_estimate=pl.CostEstimate(flops=cost, bytes_accessed=1024, transcendentals=0),
    )(*operands, *after)


def behind(kernel, count, after):
    def ordered(*refs):
        kernel(*refs[:count], *refs[count + len(after) :])

    return ordered


def plain(kernel, name, operands, specs, outs, limit=8, scratch=(), after=(), out_specs=None, cost=COST, aliases=None):
    return pl.pallas_call(
        behind(kernel, len(operands), after),
        name=name,
        out_shape=outs,
        in_specs=specs + [ANY] * len(after),
        out_specs=out_specs or [VM] * len(outs),
        scratch_shapes=list(scratch),
        input_output_aliases=aliases or {},
        compiler_params=pltpu.CompilerParams(vmem_limit_bytes=limit << 20),
        cost_estimate=pl.CostEstimate(flops=cost, bytes_accessed=1024, transcendentals=0),
    )(*operands, *after)


def exchange_on(parts, block, bit):
    count, sections = lax.axis_size("dp"), lax.axis_size("section")
    pairs = [(i * sections + p, (i ^ bit) * sections + p) for p in parts for i in range(count)]
    return lax.ppermute(block, ("dp", "section"), pairs)


def shift(block, pairs):
    return lax.ppermute(block, "section", pairs)


def scatter_sum(name, parts, keep, got, sec, spot, after, cost, later=()):
    swap = functools.partial(exchange_on, parts)
    part, half = keep.shape[0] // 4, keep.shape[1] // 2
    pairs = len(got) == 2

    def only(kernel):
        def run(sec_ref, *refs):
            mine = sec_ref[0] == parts[0]
            for p in parts[1:]:
                mine = mine | (sec_ref[0] == p)

            @pl.when(mine)
            def _():
                kernel(*refs)

        return run

    def first(sec_ref, spot_ref, keep_ref, *refs):
        if not pairs:
            only(sum_first)(sec_ref, spot_ref, keep_ref, *refs)
            return
        here, there, *outs = refs

        @pl.when(sec_ref[0] == 0)
        def _():
            sum_first(spot_ref, keep_ref, here, *outs)

        @pl.when((sec_ref[0] == 1) | (sec_ref[0] == 2))
        def _():
            sum_first(spot_ref, keep_ref, there, *outs)

    send_a, send_b, mine_a, mine_b = plain(
        first,
        name + "_first",
        [sec, spot, *map(keep_in_vmem, (keep, *got))],
        [SM, SM, VM] + [VM] * len(got),
        [shape(2 * part, half)] * 4,
        6,
        after=after,
    )
    got_a, got_b = swap(send_a, 2), swap(send_b, 4)
    began = [mine_a]
    send_a, send_b, last_a, last_b = plain(
        only(sum_second),
        name + "_second",
        [sec, spot, mine_a, mine_b, got_a, got_b],
        [SM, SM, VM, VM, VM, VM],
        [shape(part, half)] * 4,
        after=later,
        cost=cost,
    )
    return (last_a, swap(send_a, 4), last_b, swap(send_b, 2)), began, [last_a]


def body(tokens, lengths, section_weights, norm_gains, cotangent):
    slab = pltpu.with_memory_space_constraint(section_weights[0], pltpu.HBM)
    gains = norm_gains[0]
    section = lax.axis_index("section")
    dp = lax.axis_size("dp")
    place = lax.axis_index("dp")
    split = dp == 8
    sec = section.astype(jnp.int32).reshape(1)
    core = (place % 2).astype(jnp.int32).reshape(1)
    spot = jnp.stack([(place // 2) % 2, (place // 4) % 2]).astype(jnp.int32)
    order = ((place % 2) * 2 + (place // 2 + place // 4) % 2).astype(jnp.int32).reshape(1)
    sec, core, spot, order, tokens = lax.optimization_barrier((sec, core, spot, order, tokens))
    total = tokens.shape[0]
    shard = D // dp
    sizes = SPLIT if sum(SPLIT) * ROWS == total else (1,) * (total // ROWS)
    bounds = []
    for size in sizes:
        first = bounds[-1][1] if bounds else 0
        bounds.append((first, first + size * ROWS))

    if split:
        piece = plain(
            take_columns,
            "take_columns",
            [sec, order, slab],
            [SM, SM, HB],
            [shape(D, FF // 4)],
            scratch=[pltpu.SemaphoreType.DMA((1,))],
        )[0]
    else:
        piece = lax.dynamic_slice(section_weights[0], (place * shard, 0), (shard, FF))
    piece = shift(piece, [(3, 2)])

    state = {}
    sent, sent_2, notes, made, cut = [], [], [], [], []

    def run_first(mb, after=()):
        start, stop = bounds[mb]
        fresh = mb == 0
        kernel = functools.partial(first_forward, start, stop, fresh)
        message = shape(stop - start, D + SV)
        ins = [(sec, SM), (lengths, SM), (gains, VM), (tokens, VM)]
        if fresh:
            names = ["w", "left", "acts", "qkv", "slope", "mid", "right", "outs", "gg"]
            arrays = [
                held(D, ALL),
                held(total, 4 * D),
                held(total, FF),
                held(total, 3 * D),
                held(total, FF),
                held(total, D, F32),
                held(total, 4 * D + FF),
                held(total, D),
                held(8, D, F32),
            ]
            results = call(kernel, "first_forward", ins + [(slab, HB)], [], arrays + [message], 16)
        else:
            names = ["left", "acts", "qkv", "slope", "mid"]
            ins += [(keep_in_vmem(state["w"]), VM)]
            results = call(
                kernel, "first_forward", ins, [state[n] for n in names], [message], after=after
            )
        state.update(zip(names, results))
        sent.append(shift(results[-1], [(0, 1)]))

    def send_acts():
        acts, token = plain(
            put_acts,
            "put_acts",
            [sec, keep_in_vmem(state["acts"])],
            [SM, VM],
            [pltpu.HBM((total, FF), BF), shape(8, 128, F32)],
            scratch=[pltpu.SemaphoreType.DMA((1,))],
            after=[sent[-1], *sent_2[:1], *made],
            out_specs=[HB, VM],
        )
        return token, shift(acts, [(0, 1)])

    def run_second(mb, after=()):
        start, stop = bounds[mb]
        names = ["left", "qkv", "outs"]
        results = call(
            functools.partial(second_forward, start, stop),
            "second_forward",
            [(sec, SM), (lengths, SM), (gains, VM), (keep_in_vmem(state["w"]), VM), (sent[mb], VM)],
            [state[n] for n in names],
            [shape(stop - start, D)],
            after=after,
        )
        state.update(zip(names, results))
        made.append(results[-1])
        sent_2.append(shift(results[-1], [(1, 2)]))

    def run_third(mb, after=()):
        start, stop = bounds[mb]
        names = ["left", "right", "slope"]
        results = call(
            functools.partial(third_forward, start, stop),
            "third_forward",
            [(sec, SM), (gains, VM), (keep_in_vmem(state["w"]), VM), (cotangent, VM), (sent_2[mb], VM)],
            [state[n] for n in names],
            [shape(8, 128, F32)],
            after=after,
        )
        state.update(zip(names, results))
        notes.append(results[-1])

    def halves():
        parts = plain(
            halve_rows,
            "halve_rows",
            [sec, piece],
            [SM, VM],
            [shape(D // 2, FF // 4)] * 2,
            after=[sent[-1], made[-1], sent_2[0]],
        )
        cut.extend(parts)
        return exchange_on([2], parts[0], 2), exchange_on([2], parts[1], 4)

    def gathered(from_x, from_y):
        return plain(
            gather_rows,
            "gather_rows",
            [sec, from_x, from_y],
            [SM, VM, VM],
            [shape(D, FF // 4)],
            after=[notes[-1]],
        )[0]

    if len(bounds) == 4 and split:
        run_first(0)
        run_first(1)
        run_first(2)
        run_second(0)
        run_first(3, after=[sent[1]])
        run_second(1, after=[sent[2]])
        run_second(2)
        swapped = exchange_on([2], piece, 1)
        sides = halves()
        run_third(0)
        acts_gone, sent_acts = send_acts()
        run_second(3, after=[acts_gone])
        run_third(1)
        run_third(2)
        run_third(3)
        other = gathered(*sides)
        parts_3 = [piece, other, swapped, exchange_on([2], other, 1)]
    else:
        for run in (run_first, run_second, run_third):
            for mb in range(len(bounds)):
                run(mb)
            if run is run_first:
                _, sent_acts = send_acts()
        if split:
            swapped = exchange_on([2], piece, 1)
            other = gathered(*halves())
            parts_3 = [piece, other, swapped, exchange_on([2], other, 1)]
        else:
            whole = lax.all_gather(piece, "dp", axis=0, tiled=True)
            wide_3 = FF // 4
            odd = (spot[0] + spot[1]) % 2
            parts_3 = [
                lax.dynamic_slice(whole, (0, which * HALF + parity * wide_3), (D, wide_3))
                for which in (core[0], 1 - core[0])
                for parity in (odd, 1 - odd)
            ]
    w = keep_in_vmem(state["w"])
    back_2, back_1 = [], []
    apart = bounds[len(bounds) // 2][0]

    def run_third_first(first, last):
        state["right"], state["mid"] = call(
            functools.partial(third_back_first, bounds[first][0], bounds[last - 1][1]),
            "third_back_first",
            [(sec, SM), (spot, SM), (core, SM), (w, VM)]
            + [(keep_in_vmem(part), VM) for part in parts_3[:3]]
            + [(keep_in_vmem(state[n]), VM) for n in ("slope", "left")],
            [state["right"], state["mid"]],
            [],
        )

    def run_third_back(first, last):
        names = ["right", "outs", "gg"]
        spans = bounds[first:last]
        results = call(
            functools.partial(third_back, spans),
            "third_back",
            [(sec, SM), (spot, SM), (core, SM), (gains, VM), (w, VM)]
            + [(keep_in_vmem(parts_3[3]), VM)]
            + [(keep_in_vmem(state[n]), VM) for n in ("slope", "left", "mid")],
            [state[n] for n in names],
            [shape(stop - start, D) for start, stop in spans],
        )
        state.update(zip(names, results))
        back_2.extend(shift(message, [(2, 1)]) for message in results[3:])

    def run_second_back(mb, after=()):
        start, stop = bounds[mb]
        names = ["left", "right", "gg", "qkv"]
        results = call(
            functools.partial(second_back, start, stop),
            "second_back",
            [(sec, SM), (lengths, SM), (gains, VM), (w, VM)]
            + [(keep_in_vmem(state["outs"]), VM), (back_2[mb], VM)],
            [state[n] for n in names],
            [shape(stop - start, D + SV if start < apart else D)],
            after=after,
        )
        state.update(zip(names, results))
        back_1.append(shift(results[-1], [(1, 0)]))

    for first in range(0, len(bounds), 2):
        last = min(first + 2, len(bounds))
        run_third_first(first, last)
        run_third_back(first, last)
    for mb in range(len(bounds)):
        run_second_back(mb, back_2[mb + 1 : mb + 2] if mb in (1, 2) else ())
    state["qkv"], cached = call(
        put_cached, "put_cached", [(sec, SM)], [state["qkv"]], [shape(total - apart, SV)]
    )
    cached = shift(cached, [(1, 0)])
    left, right, qkv, slope, mid, outs, gg = [
        state[n] for n in ("left", "right", "qkv", "slope", "mid", "outs", "gg")
    ]

    def own_shares(name, roles, extra, left, right, keep=None, after=()):
        width = 4 * D + (256 if extra else 0)
        rows = held(D // 2, width)
        states = [left, right] + ([] if keep is None else [keep])
        return call(
            functools.partial(shares, roles, extra, keep is not None),
            name,
            [(sec, SM), (core, SM), (keep_in_vmem(gg), VM)],
            states,
            [rows] * (2 if keep is None else 1),
            scratch=[pltpu.VMEM((D, total), BF), pltpu.VMEM((D, D), BF)],
            after=after,
        )

    def plain_sums(roles, extra):
        width = 4 * D + (256 if extra else 0)
        full = jnp.zeros((D, width), BF)
        for part, (first, groups) in roles.items():
            blocks = [
                lax.dot_general(
                    left[:, g * D : (g + 1) * D],
                    right[:, first + j * D : first + (j + 1) * D],
                    (((0,), (0,)), ((), ())),
                    preferred_element_type=F32,
                ).astype(BF)
                for j, g in enumerate(groups)
            ]
            if extra:
                blocks += [gg.T.astype(BF), jnp.zeros((D, 248), BF)]
            full = jnp.where(section == part, jnp.concatenate(blocks, axis=1), full)
        full = lax.psum_scatter(full, "dp", scatter_dimension=0, tiled=True)
        blank = jnp.zeros((shard, width // 2), BF)
        return full[:, : width // 2], blank, full[:, width // 2 :], blank

    def run_wide(mb):
        start, stop = bounds[mb]
        return call(
            functools.partial(first_back_wide, start, stop),
            "first_back_wide",
            [(sec, SM), (gains, VM), (w, VM), (keep_in_vmem(slope), VM), (back_1[mb], VM)],
            [right, mid, gg],
            [],
        )

    def run_attend(first, last, after=()):
        start, stop = bounds[first][0], bounds[last - 1][1]
        place_of, heads = ((start, D), back_1[first]) if start < apart else ((apart, 0), cached)
        return call(
            functools.partial(first_back_attend, start, stop, *place_of),
            "first_back_attend",
            [(sec, SM), (lengths, SM), (gains, VM), (tokens, VM), (w, VM)]
            + [(keep_in_vmem(qkv), VM), (keep_in_vmem(mid), VM), (heads, VM)],
            [right, outs, gg],
            [shape(8, 128, F32)],
            after=after,
        )

    up_roles = {0: (R2, [2] * 4)}
    down_roles = {1: (R2, [3] * 4), 2: (0, [3] * 4)}
    narrow_roles = {0: (R0, [0] * 3 + [1]), 1: (R0, [0] * 3 + [1]), 2: (R2, [2] * 4)}
    count = len(bounds)
    late = 1
    for mb in range(count):
        right, mid, gg = run_wide(mb)
        if mb < late:
            right, outs, gg, _ = run_attend(mb, mb + 1)
    def sum_up(four):
        return plain(
            sum_last, "wide_sum_last", list(four), [VM] * 4, [shape(shard, FF)], cost=8000000000
        )[0]

    tokens_of = []
    if split:
        left, right, keep, send = own_shares("up_grads", up_roles, False, left, right)
        got_up = exchange_on([0], send, 1)
    right = call(take_acts, "take_acts", [(sec, SM), (sent_acts, ANY)], [right], [])[0]
    if split:
        left, right, keep, send = own_shares("down_grads", down_roles, False, left, right, keep, [cached])
        got_down = exchange_on([1, 2], send, 1)
    rest = list(range(late, count))
    for mb in rest[:1]:
        right, outs, gg, token = run_attend(mb, mb + 1)
        tokens_of.append(token)
    if split:
        wide, begun, seconds = scatter_sum(
            "wide_sum", [0, 1, 2], keep, [got_up, got_down], sec, spot, tokens_of, 30000000000
        )
    for first, last in [(2, 4)] if count == 4 else [(mb, mb + 1) for mb in rest[1:]]:
        right, outs, gg, token = run_attend(first, last, begun if split else ())
    left, right, result = call(
        last_forward,
        "last_forward",
        [(sec, SM), (spot, SM), (core, SM)] + [(part, VM) for part in parts_3],
        [left, right],
        [shape(total, D)],
        limit=8,
    )
    result = shift(result, [(2, 3)])
    if split:
        moved = sum_up(wide)
        left, right, keep, send = own_shares("narrow_grads", narrow_roles, True, left, right)
        got_narrow = exchange_on([0, 1, 2], send, 1)
        narrow, _, _ = scatter_sum(
            "narrow_sum", [0, 1, 2], keep, [got_narrow], sec, spot, seconds, COST, [moved]
        )
    else:
        wide = plain_sums({**up_roles, **down_roles}, False)
        moved = sum_up(wide)
        narrow = plain_sums(narrow_roles, True)
    moved = shift(moved, [(1, 0), (2, 3)])

    sems = pltpu.SemaphoreType.DMA((1,))
    grads, rows = plain(
        lambda *refs: finish_wide(refs[0], refs[1:5], *refs[5:]),
        "finish_wide",
        [sec, *wide, moved, outs, result],
        [SM] + [VM] * 7,
        [pltpu.HBM((shard, ALL), F32), shape(total, D)],
        12,
        [pltpu.VMEM((shard, ALL), F32), sems],
        out_specs=[HB, VM],
    )
    grads, gain_out = plain(
        lambda *refs: finish_narrow(refs[0], refs[1:5], *refs[5:]),
        "finish_narrow",
        [sec, *narrow, grads],
        [SM] + [VM] * 4 + [HB],
        [pltpu.HBM((shard, ALL), F32), shape(2, shard, F32)],
        8,
        [pltpu.VMEM((shard, 4 * D), F32), sems],
        out_specs=[HB, VM],
        aliases={5: 0},
    )
    return (rows[None], grads[None], gain_out[None])


def solution(mesh):
    placed = (
        P("dp", None),
        P("dp", None),
        P("section", None, None),
        P("section", None, None),
        P("dp", None),
    )
    return jax.shard_map(
        body,
        mesh=mesh,
        in_specs=placed,
        out_specs=(P("section", "dp", None), P("section", "dp", None), P("section", None, "dp")),
        check_vma=False,
    )
```

```python
import functools

import jax
import jax.numpy as jnp
from jax import lax
from jax.experimental import pallas as pl
from jax.experimental.pallas import tpu as pltpu
from jax.sharding import PartitionSpec as P

D = 768
HD = 64
FF = 3072
SV = 384
ROWS = 112
PAIRS = 6
WIDE = 2 * HD
EPS = 1e-05
BF = jnp.bfloat16
F32 = jnp.float32

SPLIT = (1, 1, 1, 1)

L0, L1, L2, L3 = 0, D, 2 * D, 3 * D
R0, R1, R2 = 0, 3 * D, 4 * D
ALL = 4 * D + 2 * FF

QKV, OUT, UP, DOWN = 0, 3 * D, 4 * D, 4 * D + FF
FRESH = 2 * D + D - SV
HALF = FF // 2
TURNED = 4 * D

VM = pl.BlockSpec(memory_space=pltpu.VMEM)
SM = pl.BlockSpec(memory_space=pltpu.SMEM)
HB = pl.BlockSpec(memory_space=pltpu.HBM)
ANY = pl.BlockSpec(memory_space=pl.ANY)


def dot(left, right):
    return jnp.dot(left, right, preferred_element_type=F32)


def dot_nt(left, right):
    return lax.dot_general(left, right, (((1,), (1,)), ((), ())), preferred_element_type=F32)


def normalized(rows):
    centered = rows - jnp.mean(rows, axis=-1, keepdims=True)
    spread = lax.rsqrt(jnp.mean(centered * centered, axis=-1, keepdims=True) + EPS)
    return centered * spread, spread


def norm_back(hat, spread, gain, grad):
    scaled = grad * gain
    inner = jnp.mean(scaled, axis=-1, keepdims=True)
    along = jnp.mean(scaled * hat, axis=-1, keepdims=True)
    return spread * (scaled - inner - hat * along)


def gelu_pair(u):
    c0 = 0.7978845608028654
    c1 = c0 * 0.044715
    square = u * u
    half = 0.5 + 0.5 * jnp.tanh(u * (c0 + c1 * square))
    act = u * half
    return act, half + act * ((1.0 - half) * (2.0 * c0 + (6.0 * c1) * square))


def sequence_start(lengths, bucket, i):
    e0 = lengths[bucket, 0]
    e1 = e0 + lengths[bucket, 1]
    e2 = e1 + lengths[bucket, 2]
    return jnp.where(i >= e2, e2, jnp.where(i >= e1, e1, jnp.where(i >= e0, e0, 0)))


def bias_rows(lengths, bucket):
    i = lax.broadcasted_iota(jnp.int32, (ROWS, ROWS), 0)
    j = lax.broadcasted_iota(jnp.int32, (ROWS, ROWS), 1)
    bias = jnp.where((j <= i) & (j >= sequence_start(lengths, bucket, i)), 0.0, -1e30)
    return jnp.concatenate([bias, bias], axis=0)


def bias_columns(lengths, bucket):
    j = lax.broadcasted_iota(jnp.int32, (ROWS, 2 * ROWS), 0)
    i = lax.broadcasted_iota(jnp.int32, (ROWS, 2 * ROWS), 1)
    i = jnp.where(i >= ROWS, i - ROWS, i)
    return jnp.where((j <= i) & (j >= sequence_start(lengths, bucket, i)), 0.0, -1e30)


def lane_masks(scale):
    low = lax.broadcasted_iota(jnp.int32, (ROWS, WIDE), 1) < HD
    return jnp.where(low, scale, 0.0).astype(BF), jnp.where(low, 0.0, scale).astype(BF)


def two_heads(block, masks):
    return jnp.concatenate([block * masks[0], block * masks[1]], axis=0)


def joined(stacked):
    low = lax.broadcasted_iota(jnp.int32, (ROWS, WIDE), 1) < HD
    return jnp.where(low, stacked[:ROWS], stacked[ROWS:])


def softmax(scores, axis):
    top = jnp.max(scores, axis=axis, keepdims=True)
    powers = jnp.exp(scores - top)
    return powers * (1.0 / jnp.sum(powers, axis=axis, keepdims=True))


def attention(qkv, rows, bias, put):
    masks = lane_masks(HD ** (-0.5))
    at = [WIDE * p for p in range(PAIRS)]
    scores = [
        dot_nt(two_heads(qkv[rows, c : c + WIDE], masks), qkv[rows, D + c : D + c + WIDE]) + bias
        for c in at
    ]
    probs = [softmax(s, -1).astype(BF) for s in scores]
    for c, p in zip(at, probs):
        put(c, joined(dot(p, qkv[rows, 2 * D + c : 2 * D + c + WIDE])))


def attention_back(qkv, rows, grad, bias, put):
    scaled = lane_masks(HD ** (-0.5))
    plain = lane_masks(1.0)
    at = [WIDE * p for p in range(PAIRS)]
    qs = [two_heads(qkv[rows, c : c + WIDE], scaled) for c in at]
    ks = [qkv[rows, D + c : D + c + WIDE] for c in at]
    vs = [qkv[rows, 2 * D + c : 2 * D + c + WIDE] for c in at]
    gs = [two_heads(grad[:, c : c + WIDE], plain) for c in at]
    scores = [dot_nt(k, q) + bias for k, q in zip(ks, qs)]
    grad_probs = [dot_nt(v, g) for v, g in zip(vs, gs)]
    probs = [softmax(s, 0) for s in scores]
    inner = [jnp.sum(d * p, axis=0, keepdims=True) for d, p in zip(grad_probs, probs)]
    grad_scores = [(p * (d - i)).astype(BF) for p, d, i in zip(probs, grad_probs, inner)]
    grad_v = [dot(p.astype(BF), g) for p, g in zip(probs, gs)]
    grad_k = [dot(s, q) for s, q in zip(grad_scores, qs)]
    turned = [s.T for s in grad_scores]
    grad_q = [joined(dot(t, k)) * HD ** (-0.5) for t, k in zip(turned, ks)]
    for c, dq, dk, dv in zip(at, grad_q, grad_k, grad_v):
        put(c, dq, dk, dv)


def buckets_of(start, stop):
    return [(b // ROWS, slice(b, b + ROWS)) for b in range(start, stop, ROWS)]


class Loads:
    def __init__(self, sems):
        self.sems = sems
        self.used = 0

    def start(self, src, dst):
        copy = pltpu.make_async_copy(src, dst, self.sems.at[self.used])
        self.used += 1
        copy.start()
        return copy


def forward_wide(left, store, slope, rows, w, up, down, chunk, waits=None):
    count = FF // chunk

    def lift(c):
        if waits:
            waits[0][c].wait()
        return dot(left[rows, L2 : L2 + D], w[:, up + c * chunk : up + (c + 1) * chunk])

    total = None
    here = lift(0)
    for c in range(count):
        ahead = lift(c + 1) if c + 1 < count else None
        act, gradient = gelu_pair(here)
        act = act.astype(BF)
        store[rows, c * chunk : (c + 1) * chunk] = act
        slope[rows, c * chunk : (c + 1) * chunk] = gradient.astype(BF)
        if down is not None:
            if waits:
                waits[1][c].wait()
            part = dot_nt(act, w[:, down + c * chunk : down + (c + 1) * chunk])
            total = part if total is None else total + part
        here = ahead
    return total


CHUNK = 512
COST = 1000


def first_forward(start, stop, fresh, sec, lengths, gains, tokens, *refs):
    if fresh:
        slab, refs = refs[0], refs[1:]
        w, left, acts, qkv, slope, mid, right, outs, gg, message, sems = refs
        gg[...] = jnp.zeros_like(gg)
    else:
        w, refs = refs[0], refs[1:]
        left, acts, qkv, slope, mid, message, sems = refs[5:]
    rows = slice(start, stop)
    if fresh:

        @pl.when(sec[0] == 1)
        def _():
            load = Loads(sems).start(slab.at[:, pl.ds(0, FRESH + D)], w.at[:, pl.ds(0, FRESH + D)])
            load.wait()
            w[:, TURNED : TURNED + D] = w[:, FRESH : FRESH + D].T
            for c in range(0, FRESH, D):
                wide = min(D, FRESH - c)
                at = TURNED + D + c
                w[:wide, at : at + D] = w[:, c : c + wide].T

        @pl.when(sec[0] == 2)
        def _():
            loads = Loads(sems)
            both = [
                loads.start(slab.at[:, pl.ds(at, HALF)], w.at[:, pl.ds(at, HALF)])
                for at in (0, HALF)
            ]
            for load in both:
                load.wait()

    @pl.when(sec[0] == 0)
    def _():
        loads = Loads(sems)
        first = second = waits = None
        if fresh:

            def get(at, wide):
                return loads.start(slab.at[:, pl.ds(at, wide)], w.at[:, pl.ds(at, wide)])

            first = [get(QKV + c * D, D) for c in range(3)]
            second = get(OUT, D)
            waits = ([], [])
            for c in range(FF // CHUNK):
                waits[0].append(get(UP + c * CHUNK, CHUNK))
                waits[1].append(get(DOWN + c * CHUNK, CHUNK))
        x = tokens[rows, :].astype(F32)
        low = (normalized(x)[0] * gains[0:1, :]).astype(BF)
        left[rows, L0 : L0 + D] = low
        for c in range(3):
            if fresh:
                first[c].wait()
            qkv[rows, c * D : (c + 1) * D] = dot(low, w[:, QKV + c * D : QKV + (c + 1) * D]).astype(BF)
        message[:, D:] = qkv[rows, 2 * D : 2 * D + SV]
        for bucket, here in buckets_of(start, stop):

            def put(c, value):
                left[here, L1 + c : L1 + c + WIDE] = value.astype(BF)

            attention(qkv, here, bias_rows(lengths, bucket), put)
        if fresh:
            second.wait()
        middle = x + dot(left[rows, L1 : L1 + D], w[:, OUT : OUT + D])
        mid[rows, :] = middle
        left[rows, L2 : L2 + D] = (normalized(middle)[0] * gains[1:2, :]).astype(BF)
        total = forward_wide(left, acts, slope, rows, w, UP, DOWN, CHUNK, waits)
        message[:, :D] = (middle + total).astype(BF)


def second_forward(start, stop, sec, lengths, gains, w, arrived, *refs):
    left, qkv, outs, message, sems = refs[3:]
    rows = slice(start, stop)

    @pl.when(sec[0] == 1)
    def _():
        outs[rows, :] = arrived[:, :D]
        x = arrived[:, :D].astype(F32)
        low = (normalized(x)[0] * gains[0:1, :]).astype(BF)
        left[rows, L0 : L0 + D] = low
        mixed = dot(low, w[:, :FRESH]).astype(BF)
        qkv[rows, : 2 * D] = mixed[:, : 2 * D]
        qkv[rows, 2 * D : 2 * D + SV] = arrived[:, D:]
        qkv[rows, 2 * D + SV :] = mixed[:, 2 * D :]
        for bucket, here in buckets_of(start, stop):

            def put(c, value):
                left[here, L1 + c : L1 + c + WIDE] = value.astype(BF)

            attention(qkv, here, bias_rows(lengths, bucket), put)
        message[...] = (x + dot(left[rows, L1 : L1 + D], w[:, FRESH : FRESH + D])).astype(BF)


def third_forward(start, stop, sec, gains, w, cot, arrived, *refs):
    left, right, slope, token, sems = refs[3:]
    rows = slice(start, stop)
    token[...] = jnp.zeros_like(token)

    @pl.when(sec[0] == 2)
    def _():
        left[rows, L1 : L1 + D] = arrived[...]
        left[rows, L3 : L3 + D] = cot[rows, :]
        hat = normalized(arrived[...].astype(F32))[0]
        left[rows, L2 : L2 + D] = (hat * gains[0:1, :]).astype(BF)
        forward_wide(left, right, slope, rows, w, 0, None, CHUNK)


def third_back_quarter(left, right, slope, w, other, at, rows):
    cols = pl.ds(at, FF // 4)
    grad = dot(left[rows, L3 : L3 + D], other[...]).astype(BF).astype(F32)
    lifted = (slope[rows, cols].astype(F32) * grad).astype(BF)
    right[rows, pl.ds(pl.multiple_of(R2 + at, 128), FF // 4)] = lifted
    return dot_nt(lifted, w[:, cols])


def third_back_first(start, stop, sec, spot, core, w, *refs):
    others, refs = refs[:3], refs[3:]
    slope, left, _r, _m, right, mid, sems = refs
    rows = slice(start, stop)

    @pl.when(sec[0] == 2)
    def _():
        at = quarters(core[0], (spot[0] + spot[1]) % 2)
        total = None
        for k, other in enumerate(others):
            part = third_back_quarter(left, right, slope, w, other, at[k], rows)
            total = part if total is None else total + part
        mid[rows, :] = total


def third_back(spans, sec, spot, core, gains, w, got, slope, left, mid, *refs):
    right, outs, gg, *messages, sems = refs[3:]
    rows = slice(spans[0][0], spans[-1][1])

    @pl.when(sec[0] == 2)
    def _():
        at = quarters(core[0], (spot[0] + spot[1]) % 2)[3]
        back = mid[rows, :] + third_back_quarter(left, right, slope, w, got, at, rows)
        hat, spread = normalized(left[rows, L1 : L1 + D].astype(F32))
        gg[0:1, :] += jnp.sum(back * hat, axis=0, keepdims=True)
        c = left[rows, L3 : L3 + D].astype(F32)
        resid = (c + norm_back(hat, spread, gains[0:1, :], back)).astype(BF)
        for (start, stop), message in zip(spans, messages):
            message[...] = resid[start - rows.start : stop - rows.start]
        outs[rows, :] = resid


def second_back(start, stop, sec, lengths, gains, w, outs, arrived, *refs):
    left, right, gg, qkv, message, sems = refs[4:]
    rows = slice(start, stop)

    @pl.when(sec[0] == 1)
    def _():
        right[rows, R1 : R1 + D] = arrived[...]
        grad = dot(arrived[...], w[:, TURNED : TURNED + D]).astype(BF)
        for bucket, here in buckets_of(start, stop):
            local = slice(here.start - start, here.stop - start)

            def put(c, dq, dk, dv):
                right[here, R0 + c : R0 + c + WIDE] = dq.astype(BF)
                right[here, R0 + D + c : R0 + D + c + WIDE] = dk.astype(BF)
                if c < SV:
                    if message.shape[1] > D:
                        message[local, D + c : D + c + WIDE] = dv.astype(BF)
                    else:
                        qkv[here, 2 * D + c : 2 * D + c + WIDE] = dv.astype(BF)
                else:
                    right[here, R0 + 2 * D + c - SV : R0 + 2 * D + c - SV + WIDE] = dv.astype(BF)

            attention_back(qkv, here, grad[local], bias_columns(lengths, bucket), put)
        back = None
        for c in range(0, FRESH, D):
            wide, at = min(D, FRESH - c), TURNED + D + c
            part = dot(right[rows, R0 + c : R0 + c + wide], w[:wide, at : at + D])
            back = part if back is None else back + part
        hat, spread = normalized(outs[rows, :].astype(F32))
        gg[0:1, :] += jnp.sum(back * hat, axis=0, keepdims=True)
        resid = arrived[...].astype(F32) + norm_back(hat, spread, gains[0:1, :], back)
        message[:, :D] = resid.astype(BF)
        left[rows, L3 : L3 + D] = resid.astype(BF)


def first_back_wide(start, stop, sec, gains, w, slope, arrived, *refs):
    right, mid, gg, sems = refs[3:]
    rows = slice(start, stop)

    @pl.when(sec[0] == 0)
    def _():
        grad = arrived[:, :D]
        back = None
        pulled = dot(grad, w[:, DOWN : DOWN + CHUNK])
        for c in range(FF // CHUNK):
            k = c * CHUNK
            ahead = None
            if k + CHUNK < FF:
                ahead = dot(grad, w[:, DOWN + k + CHUNK : DOWN + k + 2 * CHUNK])
            lifted = (slope[rows, k : k + CHUNK].astype(F32) * pulled).astype(BF)
            right[rows, R2 + k : R2 + k + CHUNK] = lifted
            part = dot_nt(lifted, w[:, UP + k : UP + k + CHUNK])
            back = part if back is None else back + part
            pulled = ahead
        hat, spread = normalized(mid[rows, :])
        gg[1:2, :] += jnp.sum(back * hat, axis=0, keepdims=True)
        resid = grad.astype(F32) + norm_back(hat, spread, gains[1:2, :], back)
        right[rows, R1 : R1 + D] = resid.astype(BF)
        mid[rows, :] = resid


def first_back_attend(start, stop, base, off, sec, lengths, gains, tokens, w, qkv, mid, arrived, *refs):
    right, outs, gg, token, sems = refs[3:]
    rows = slice(start, stop)
    token[...] = jnp.zeros_like(token)

    @pl.when(sec[0] == 0)
    def _():
        grad = dot_nt(right[rows, R1 : R1 + D], w[:, OUT : OUT + D]).astype(BF)
        for bucket, here in buckets_of(start, stop):
            local = slice(here.start - start, here.stop - start)

            def put(c, dq, dk, dv):
                right[here, R0 + c : R0 + c + WIDE] = dq.astype(BF)
                right[here, R0 + D + c : R0 + D + c + WIDE] = dk.astype(BF)
                if c < SV:
                    at = slice(here.start - base, here.stop - base)
                    dv = dv + arrived[at, off + c : off + c + WIDE].astype(F32)
                right[here, R0 + 2 * D + c : R0 + 2 * D + c + WIDE] = dv.astype(BF)

            attention_back(qkv, here, grad[local], bias_columns(lengths, bucket), put)
        back = dot_nt(right[rows, R0 : R0 + 3 * D], w[:, QKV : QKV + 3 * D])
        hat, spread = normalized(tokens[rows, :].astype(F32))
        gg[0:1, :] += jnp.sum(back * hat, axis=0, keepdims=True)
        outs[rows, :] = (mid[rows, :] + norm_back(hat, spread, gains[0:1, :], back)).astype(BF)


def last_forward(sec, spot, core, *refs):
    others, (_l, _r, left, right, result, sems) = refs[:4], refs[4:]

    @pl.when(sec[0] == 2)
    def _():
        total = left[:, L1 : L1 + D].astype(F32)
        for at, other in zip(quarters(core[0], (spot[0] + spot[1]) % 2), others):
            total = total + dot_nt(right[:, pl.ds(at, FF // 4)], other[...])
        result[...] = total.astype(BF)


def take_acts(sec, arrived, _r, right, sems):
    @pl.when(sec[0] == 1)
    def _():
        Loads(sems).start(arrived, right.at[:, pl.ds(R2, FF)]).wait()


def put_cached(sec, _q, qkv, out, sems):
    @pl.when(sec[0] == 1)
    def _():
        out[...] = qkv[qkv.shape[0] - out.shape[0] :, 2 * D : 2 * D + SV]


def put_acts(sec, acts, out, token, sem):
    token[...] = jnp.zeros_like(token)

    @pl.when(sec[0] == 0)
    def _():
        Loads(sem).start(acts, out).wait()


def take_columns(sec, order, slab, piece, sems):
    @pl.when(sec[0] == 3)
    def _():
        wide = piece.shape[1]
        at = pl.multiple_of(order[0] * wide, 128)
        Loads(sems).start(slab.at[:, pl.ds(at, wide)], piece).wait()


def halve_rows(sec, piece, upper, lower):
    @pl.when(sec[0] == 2)
    def _():
        upper[...] = piece[: D // 2]
        lower[...] = piece[D // 2 :]


def gather_rows(sec, from_x, from_y, other):
    @pl.when(sec[0] == 2)
    def _():
        other[: D // 2, :] = from_x[...]
        other[D // 2 :, :] = from_y[...]


def quarters(core, odd):
    wide = FF // 4
    return [
        pl.multiple_of(which * HALF + parity * wide, 128)
        for which in (core, 1 - core)
        for parity in (odd, 1 - odd)
    ]


def by_core(core, whole, keep, send):
    wide = whole.shape[0] // 8
    for k in range(4):
        here = slice(k * wide, (k + 1) * wide)
        keep[here, :] = whole[pl.ds(pl.multiple_of((2 * k + core) * wide, wide), wide), :]
        send[here, :] = whole[pl.ds(pl.multiple_of((2 * k + 1 - core) * wide, wide), wide), :]


def shares(roles, extra, again, sec, core, gg, *refs):
    left, right, keep, send, sems, turned, whole = refs[3 if again else 2 :]

    def run(first, groups):
        before = None
        for j, group in enumerate(groups):
            if group != before:
                turned[...] = left[:, group * D : (group + 1) * D].T
            before = group
            whole[...] = dot(turned[...], right[:, first + j * D : first + (j + 1) * D]).astype(BF)
            cols = pl.ds(j * D, D)
            by_core(core[0], whole, keep.at[:, cols], send.at[:, cols])
        if extra:
            block = whole.at[:, pl.ds(0, 128)]
            block[...] = jnp.zeros((D, 128), BF)
            block[:, :8] = gg[...].T.astype(BF)
            cols = pl.ds(len(groups) * D, 128)
            by_core(core[0], block, keep.at[:, cols], send.at[:, cols])

    for part, (first, groups) in roles.items():
        pl.when(sec[0] == part)(functools.partial(run, first, groups))


def sum_first(spot, keep, got, send_a, send_b, mine_a, mine_b):
    part, half, rest = send_a.shape[0] // 2, send_a.shape[1], send_b.shape[1]
    x, y = spot[0], spot[1]

    def both(where, lo, wide):
        rows = pl.ds(pl.multiple_of(where * part, part), part)
        cols = slice(lo, lo + wide)
        return (keep[rows, cols].astype(F32) + got[rows, cols].astype(F32)).astype(BF)

    for k in range(2):
        here = slice(k * part, (k + 1) * part)
        send_a[here, :] = both(2 * k + 1 - x, 0, half)
        send_b[here, :] = both(2 * (1 - y) + k, half, rest)
        mine_a[here, :] = both(2 * k + x, 0, half)
        mine_b[here, :] = both(2 * y + k, half, rest)


def sum_second(spot, mine_a, mine_b, got_a, got_b, send_a, send_b, last_a, last_b):
    part = send_a.shape[0]
    x, y = spot[0], spot[1]

    def both(mine, got, where):
        rows = pl.ds(pl.multiple_of(where * part, part), part)
        return mine[rows, :].astype(F32) + got[rows, :].astype(F32)

    send_a[...] = both(mine_a, got_a, 1 - y).astype(BF)
    send_b[...] = both(mine_b, got_b, 1 - x).astype(BF)
    last_a[...] = both(mine_a, got_a, y).astype(BF)
    last_b[...] = both(mine_b, got_b, x).astype(BF)


def sum_last(last_a, got_a, last_b, got_b, total):
    half = last_a.shape[1]
    total[:, :half] = (last_a[...].astype(F32) + got_a[...].astype(F32)).astype(total.dtype)
    total[:, half:] = (last_b[...].astype(F32) + got_b[...].astype(F32)).astype(total.dtype)


def pieces_of(four, lo, hi):
    half = four[0].shape[1]
    found = []
    for at in range(2):
        first, last = max(lo - at * half, 0), min(hi - at * half, four[2 * at].shape[1])
        if first < last:
            one, two = four[2 * at][:, first:last], four[2 * at + 1][:, first:last]
            found.append((at * half + first, one.astype(F32) + two.astype(F32)))
    return found


def lay(four, lo, hi, block, to):
    for at, value in pieces_of(four, lo, hi):
        block[:, to + at - lo : to + at - lo + value.shape[1]] = value


def finish_wide(sec, wide, moved, outs, result, grads, rows, block, sems):
    count = block.shape[0]

    def write(first):
        cols = pl.ds(first, ALL - first)
        Loads(sems).start(block.at[:, cols], grads.at[:, cols]).wait()

    @pl.when(sec[0] == 0)
    def _():
        lay(wide, 0, FF, block, UP)
        block[:, DOWN:] = moved[...].astype(F32)
        write(UP)

    for part, first in ((1, FRESH + D), (2, FF)):

        @pl.when(sec[0] == part)
        def _(first=first):
            block[:, first:] = jnp.zeros((count, ALL - first), F32)
            write(first)

    @pl.when(sec[0] == 3)
    def _():
        block[:, :FF] = moved[...].astype(F32)
        block[:, FF:] = jnp.zeros((count, ALL - FF), F32)
        write(0)
        rows[...] = result[...]

    @pl.when(sec[0] != 3)
    def _():
        rows[...] = outs[...]


def finish_narrow(sec, narrow, _g, grads, gains, block, sems):
    def write(last):
        cols = pl.ds(0, last)
        Loads(sems).start(block.at[:, cols], grads.at[:, cols]).wait()

    @pl.when(sec[0] == 3)
    def _():
        gains[...] = jnp.zeros_like(gains)

    @pl.when(sec[0] != 3)
    def _():
        ((_, value),) = pieces_of(narrow, 4 * D, 4 * D + 128)
        gains[...] = value.T[:2]

    @pl.when((sec[0] == 0) | (sec[0] == 2))
    def _():
        lay(narrow, 0, 4 * D, block, 0)
        write(4 * D)

    @pl.when(sec[0] == 1)
    def _():
        lay(narrow, 0, FRESH, block, 0)
        lay(narrow, 3 * D, 4 * D, block, FRESH)
        write(FRESH + D)


def shape(rows, cols, dtype=BF):
    return jax.ShapeDtypeStruct((rows, cols), dtype)


def held(rows, cols, dtype=BF):
    return pltpu.VMEM((rows, cols), dtype)


def keep_in_vmem(array):
    return pltpu.with_memory_space_constraint(array, pltpu.VMEM)


def call(kernel, name, ins, states, outs, sems=1, scratch=(), after=(), limit=8, specs=None, cost=COST):
    operands = [a for a, _ in ins] + [keep_in_vmem(s) for s in states]
    aliases = {len(ins) + i: i for i in range(len(states))}
    out_shape = [held(*s.shape, s.dtype) for s in states] + list(outs)
    return pl.pallas_call(
        behind(kernel, len(operands), after),
        name=name,
        out_shape=out_shape,
        in_specs=[s for _, s in ins] + [VM] * len(states) + [ANY] * len(after),
        out_specs=[VM] * len(states) + list(specs or [VM] * len(outs)),
        scratch_shapes=[pltpu.SemaphoreType.DMA((sems,))] + list(scratch),
        input_output_aliases=aliases,
        compiler_params=pltpu.CompilerParams(vmem_limit_bytes=limit << 20),
        cost_estimate=pl.CostEstimate(flops=cost, bytes_accessed=1024, transcendentals=0),
    )(*operands, *after)


def behind(kernel, count, after):
    def ordered(*refs):
        kernel(*refs[:count], *refs[count + len(after) :])

    return ordered


def plain(kernel, name, operands, specs, outs, limit=8, scratch=(), after=(), out_specs=None, cost=COST, aliases=None):
    return pl.pallas_call(
        behind(kernel, len(operands), after),
        name=name,
        out_shape=outs,
        in_specs=specs + [ANY] * len(after),
        out_specs=out_specs or [VM] * len(outs),
        scratch_shapes=list(scratch),
        input_output_aliases=aliases or {},
        compiler_params=pltpu.CompilerParams(vmem_limit_bytes=limit << 20),
        cost_estimate=pl.CostEstimate(flops=cost, bytes_accessed=1024, transcendentals=0),
    )(*operands, *after)


def exchange_on(parts, block, bit):
    count, sections = lax.axis_size("dp"), lax.axis_size("section")
    pairs = [(i * sections + p, (i ^ bit) * sections + p) for p in parts for i in range(count)]
    return lax.ppermute(block, ("dp", "section"), pairs)


def shift(block, pairs):
    return lax.ppermute(block, "section", pairs)


def scatter_sum(name, parts, keep, got, sec, spot, after, cost, later=()):
    swap = functools.partial(exchange_on, parts)
    part = keep.shape[0] // 4
    halves = (2 * D, keep.shape[1] - 2 * D)
    pairs = len(got) == 2

    def only(kernel):
        def run(sec_ref, *refs):
            mine = sec_ref[0] == parts[0]
            for p in parts[1:]:
                mine = mine | (sec_ref[0] == p)

            @pl.when(mine)
            def _():
                kernel(*refs)

        return run

    def first(sec_ref, spot_ref, keep_ref, *refs):
        if not pairs:
            only(sum_first)(sec_ref, spot_ref, keep_ref, *refs)
            return
        here, there, *outs = refs

        @pl.when(sec_ref[0] == 0)
        def _():
            sum_first(spot_ref, keep_ref, here, *outs)

        @pl.when((sec_ref[0] == 1) | (sec_ref[0] == 2))
        def _():
            sum_first(spot_ref, keep_ref, there, *outs)

    send_a, send_b, mine_a, mine_b = plain(
        first,
        name + "_first",
        [sec, spot, *map(keep_in_vmem, (keep, *got))],
        [SM, SM, VM] + [VM] * len(got),
        [shape(2 * part, half) for half in halves] * 2,
        6,
        after=after,
    )
    got_a, got_b = swap(send_a, 2), swap(send_b, 4)
    began = [mine_a]
    send_a, send_b, last_a, last_b = plain(
        only(sum_second),
        name + "_second",
        [sec, spot, mine_a, mine_b, got_a, got_b],
        [SM, SM, VM, VM, VM, VM],
        [shape(part, half) for half in halves] * 2,
        after=later,
        cost=cost,
    )
    return (last_a, swap(send_a, 4), last_b, swap(send_b, 2)), began, [last_a]


def body(tokens, lengths, section_weights, norm_gains, cotangent):
    slab = pltpu.with_memory_space_constraint(section_weights[0], pltpu.HBM)
    gains = norm_gains[0]
    section = lax.axis_index("section")
    dp = lax.axis_size("dp")
    place = lax.axis_index("dp")
    split = dp == 8
    sec = section.astype(jnp.int32).reshape(1)
    core = (place % 2).astype(jnp.int32).reshape(1)
    spot = jnp.stack([(place // 2) % 2, (place // 4) % 2]).astype(jnp.int32)
    order = ((place % 2) * 2 + (place // 2 + place // 4) % 2).astype(jnp.int32).reshape(1)
    sec, core, spot, order, tokens = lax.optimization_barrier((sec, core, spot, order, tokens))
    total = tokens.shape[0]
    shard = D // dp
    sizes = SPLIT if sum(SPLIT) * ROWS == total else (1,) * (total // ROWS)
    bounds = []
    for size in sizes:
        first = bounds[-1][1] if bounds else 0
        bounds.append((first, first + size * ROWS))

    if split:
        piece = plain(
            take_columns,
            "take_columns",
            [sec, order, slab],
            [SM, SM, HB],
            [shape(D, FF // 4)],
            scratch=[pltpu.SemaphoreType.DMA((1,))],
        )[0]
    else:
        piece = lax.dynamic_slice(section_weights[0], (place * shard, 0), (shard, FF))
    piece = shift(piece, [(3, 2)])

    state = {}
    sent, sent_2, notes, made, cut = [], [], [], [], []

    def run_first(mb, after=()):
        start, stop = bounds[mb]
        fresh = mb == 0
        kernel = functools.partial(first_forward, start, stop, fresh)
        message = shape(stop - start, D + SV)
        ins = [(sec, SM), (lengths, SM), (gains, VM), (tokens, VM)]
        if fresh:
            names = ["w", "left", "acts", "qkv", "slope", "mid", "right", "outs", "gg"]
            arrays = [
                held(D, ALL),
                held(total, 4 * D),
                held(total, FF),
                held(total, 3 * D),
                held(total, FF),
                held(total, D, F32),
                held(total, 4 * D + FF),
                held(total, D),
                held(8, D, F32),
            ]
            results = call(kernel, "first_forward", ins + [(slab, HB)], [], arrays + [message], 16)
        else:
            names = ["left", "acts", "qkv", "slope", "mid"]
            ins += [(keep_in_vmem(state["w"]), VM)]
            results = call(
                kernel, "first_forward", ins, [state[n] for n in names], [message], after=after
            )
        state.update(zip(names, results))
        sent.append(shift(results[-1], [(0, 1)]))

    def send_acts():
        acts, token = plain(
            put_acts,
            "put_acts",
            [sec, keep_in_vmem(state["acts"])],
            [SM, VM],
            [pltpu.HBM((total, FF), BF), shape(8, 128, F32)],
            scratch=[pltpu.SemaphoreType.DMA((1,))],
            after=[sent[-1], *sent_2[:1], *made],
            out_specs=[HB, VM],
        )
        return token, shift(acts, [(0, 1)])

    def run_second(mb, after=()):
        start, stop = bounds[mb]
        names = ["left", "qkv", "outs"]
        results = call(
            functools.partial(second_forward, start, stop),
            "second_forward",
            [(sec, SM), (lengths, SM), (gains, VM), (keep_in_vmem(state["w"]), VM), (sent[mb], VM)],
            [state[n] for n in names],
            [shape(stop - start, D)],
            after=after,
        )
        state.update(zip(names, results))
        made.append(results[-1])
        sent_2.append(shift(results[-1], [(1, 2)]))

    def run_third(mb, after=()):
        start, stop = bounds[mb]
        names = ["left", "right", "slope"]
        results = call(
            functools.partial(third_forward, start, stop),
            "third_forward",
            [(sec, SM), (gains, VM), (keep_in_vmem(state["w"]), VM), (cotangent, VM), (sent_2[mb], VM)],
            [state[n] for n in names],
            [shape(8, 128, F32)],
            after=after,
        )
        state.update(zip(names, results))
        notes.append(results[-1])

    def halves():
        parts = plain(
            halve_rows,
            "halve_rows",
            [sec, piece],
            [SM, VM],
            [shape(D // 2, FF // 4)] * 2,
            after=[sent[-1], made[-1], sent_2[0]],
        )
        cut.extend(parts)
        return exchange_on([2], parts[0], 2), exchange_on([2], parts[1], 4)

    def gathered(from_x, from_y):
        return plain(
            gather_rows,
            "gather_rows",
            [sec, from_x, from_y],
            [SM, VM, VM],
            [shape(D, FF // 4)],
            after=[notes[-1]],
        )[0]

    if len(bounds) == 4 and split:
        run_first(0)
        run_first(1)
        run_first(2)
        run_second(0)
        run_first(3, after=[sent[1]])
        run_second(1, after=[sent[2]])
        run_second(2)
        swapped = exchange_on([2], piece, 1)
        sides = halves()
        run_third(0)
        acts_gone, sent_acts = send_acts()
        run_second(3, after=[acts_gone])
        run_third(1)
        run_third(2)
        run_third(3)
        other = gathered(*sides)
        parts_3 = [piece, other, swapped, exchange_on([2], other, 1)]
    else:
        for run in (run_first, run_second, run_third):
            for mb in range(len(bounds)):
                run(mb)
            if run is run_first:
                _, sent_acts = send_acts()
        if split:
            swapped = exchange_on([2], piece, 1)
            other = gathered(*halves())
            parts_3 = [piece, other, swapped, exchange_on([2], other, 1)]
        else:
            whole = lax.all_gather(piece, "dp", axis=0, tiled=True)
            wide_3 = FF // 4
            odd = (spot[0] + spot[1]) % 2
            parts_3 = [
                lax.dynamic_slice(whole, (0, which * HALF + parity * wide_3), (D, wide_3))
                for which in (core[0], 1 - core[0])
                for parity in (odd, 1 - odd)
            ]
    w = keep_in_vmem(state["w"])
    back_2, back_1 = [], []
    apart = bounds[len(bounds) // 2][0]

    def run_third_first(first, last):
        state["right"], state["mid"] = call(
            functools.partial(third_back_first, bounds[first][0], bounds[last - 1][1]),
            "third_back_first",
            [(sec, SM), (spot, SM), (core, SM), (w, VM)]
            + [(keep_in_vmem(part), VM) for part in parts_3[:3]]
            + [(keep_in_vmem(state[n]), VM) for n in ("slope", "left")],
            [state["right"], state["mid"]],
            [],
        )

    def run_third_back(first, last):
        names = ["right", "outs", "gg"]
        spans = bounds[first:last]
        results = call(
            functools.partial(third_back, spans),
            "third_back",
            [(sec, SM), (spot, SM), (core, SM), (gains, VM), (w, VM)]
            + [(keep_in_vmem(parts_3[3]), VM)]
            + [(keep_in_vmem(state[n]), VM) for n in ("slope", "left", "mid")],
            [state[n] for n in names],
            [shape(stop - start, D) for start, stop in spans],
        )
        state.update(zip(names, results))
        back_2.extend(shift(message, [(2, 1)]) for message in results[3:])

    def run_second_back(mb, after=()):
        start, stop = bounds[mb]
        names = ["left", "right", "gg", "qkv"]
        results = call(
            functools.partial(second_back, start, stop),
            "second_back",
            [(sec, SM), (lengths, SM), (gains, VM), (w, VM)]
            + [(keep_in_vmem(state["outs"]), VM), (back_2[mb], VM)],
            [state[n] for n in names],
            [shape(stop - start, D + SV if start < apart else D)],
            after=after,
        )
        state.update(zip(names, results))
        back_1.append(shift(results[-1], [(1, 0)]))

    for first in range(0, len(bounds), 2):
        last = min(first + 2, len(bounds))
        run_third_first(first, last)
        run_third_back(first, last)
    for mb in range(len(bounds)):
        run_second_back(mb, back_2[mb + 1 : mb + 2] if mb in (1, 2) else ())
    state["qkv"], cached = call(
        put_cached, "put_cached", [(sec, SM)], [state["qkv"]], [shape(total - apart, SV)]
    )
    cached = shift(cached, [(1, 0)])
    left, right, qkv, slope, mid, outs, gg = [
        state[n] for n in ("left", "right", "qkv", "slope", "mid", "outs", "gg")
    ]

    def own_shares(name, roles, extra, left, right, keep=None, after=()):
        width = 4 * D + (128 if extra else 0)
        rows = held(D // 2, width)
        states = [left, right] + ([] if keep is None else [keep])
        return call(
            functools.partial(shares, roles, extra, keep is not None),
            name,
            [(sec, SM), (core, SM), (keep_in_vmem(gg), VM)],
            states,
            [rows] * (2 if keep is None else 1),
            scratch=[pltpu.VMEM((D, total), BF), pltpu.VMEM((D, D), BF)],
            after=after,
        )

    def plain_sums(roles, extra):
        width = 4 * D + (128 if extra else 0)
        full = jnp.zeros((D, width), BF)
        for part, (first, groups) in roles.items():
            blocks = [
                lax.dot_general(
                    left[:, g * D : (g + 1) * D],
                    right[:, first + j * D : first + (j + 1) * D],
                    (((0,), (0,)), ((), ())),
                    preferred_element_type=F32,
                ).astype(BF)
                for j, g in enumerate(groups)
            ]
            if extra:
                blocks += [gg.T.astype(BF), jnp.zeros((D, 120), BF)]
            full = jnp.where(section == part, jnp.concatenate(blocks, axis=1), full)
        full = lax.psum_scatter(full, "dp", scatter_dimension=0, tiled=True)
        halves = full[:, : 2 * D], full[:, 2 * D :]
        return tuple(a for half in halves for a in (half, jnp.zeros_like(half)))

    def run_wide(mb):
        start, stop = bounds[mb]
        return call(
            functools.partial(first_back_wide, start, stop),
            "first_back_wide",
            [(sec, SM), (gains, VM), (w, VM), (keep_in_vmem(slope), VM), (back_1[mb], VM)],
            [right, mid, gg],
            [],
        )

    def run_attend(first, last, after=()):
        start, stop = bounds[first][0], bounds[last - 1][1]
        place_of, heads = ((start, D), back_1[first]) if start < apart else ((apart, 0), cached)
        return call(
            functools.partial(first_back_attend, start, stop, *place_of),
            "first_back_attend",
            [(sec, SM), (lengths, SM), (gains, VM), (tokens, VM), (w, VM)]
            + [(keep_in_vmem(qkv), VM), (keep_in_vmem(mid), VM), (heads, VM)],
            [right, outs, gg],
            [shape(8, 128, F32)],
            after=after,
        )

    up_roles = {0: (R2, [2] * 4)}
    down_roles = {1: (R2, [3] * 4), 2: (0, [3] * 4)}
    narrow_roles = {0: (R0, [0] * 3 + [1]), 1: (R0, [0] * 3 + [1]), 2: (R2, [2] * 4)}
    count = len(bounds)
    late = 1
    for mb in range(count):
        right, mid, gg = run_wide(mb)
        if mb < late:
            right, outs, gg, _ = run_attend(mb, mb + 1)
    def sum_up(four):
        return plain(
            sum_last, "wide_sum_last", list(four), [VM] * 4, [shape(shard, FF)], cost=8000000000
        )[0]

    tokens_of = []
    if split:
        left, right, keep, send = own_shares("up_grads", up_roles, False, left, right)
        got_up = exchange_on([0], send, 1)
    right = call(take_acts, "take_acts", [(sec, SM), (sent_acts, ANY)], [right], [])[0]
    if split:
        left, right, keep, send = own_shares("down_grads", down_roles, False, left, right, keep, [cached])
        got_down = exchange_on([1, 2], send, 1)
    rest = list(range(late, count))
    for mb in rest[:1]:
        right, outs, gg, token = run_attend(mb, mb + 1)
        tokens_of.append(token)
    if split:
        wide, begun, seconds = scatter_sum(
            "wide_sum", [0, 1, 2], keep, [got_up, got_down], sec, spot, tokens_of, 30000000000
        )
    for first, last in [(2, 4)] if count == 4 else [(mb, mb + 1) for mb in rest[1:]]:
        right, outs, gg, token = run_attend(first, last, begun if split else ())
    left, right, result = call(
        last_forward,
        "last_forward",
        [(sec, SM), (spot, SM), (core, SM)] + [(part, VM) for part in parts_3],
        [left, right],
        [shape(total, D)],
        limit=8,
    )
    result = shift(result, [(2, 3)])
    if split:
        moved = sum_up(wide)
        left, right, keep, send = own_shares("narrow_grads", narrow_roles, True, left, right)
        got_narrow = exchange_on([0, 1, 2], send, 1)
        narrow, _, _ = scatter_sum(
            "narrow_sum", [0, 1, 2], keep, [got_narrow], sec, spot, seconds, COST, [moved]
        )
    else:
        wide = plain_sums({**up_roles, **down_roles}, False)
        moved = sum_up(wide)
        narrow = plain_sums(narrow_roles, True)
    moved = shift(moved, [(1, 0), (2, 3)])

    sems = pltpu.SemaphoreType.DMA((1,))
    grads, rows = plain(
        lambda *refs: finish_wide(refs[0], refs[1:5], *refs[5:]),
        "finish_wide",
        [sec, *wide, moved, outs, result],
        [SM] + [VM] * 7,
        [pltpu.HBM((shard, ALL), F32), shape(total, D)],
        12,
        [pltpu.VMEM((shard, ALL), F32), sems],
        out_specs=[HB, VM],
    )
    grads, gain_out = plain(
        lambda *refs: finish_narrow(refs[0], refs[1:5], *refs[5:]),
        "finish_narrow",
        [sec, *narrow, grads],
        [SM] + [VM] * 4 + [HB],
        [pltpu.HBM((shard, ALL), F32), shape(2, shard, F32)],
        8,
        [pltpu.VMEM((shard, 4 * D), F32), sems],
        out_specs=[HB, VM],
        aliases={5: 0},
    )
    return (rows[None], grads[None], gain_out[None])


def solution(mesh):
    placed = (
        P("dp", None),
        P("dp", None),
        P("section", None, None),
        P("section", None, None),
        P("dp", None),
    )
    return jax.shard_map(
        body,
        mesh=mesh,
        in_specs=placed,
        out_specs=(P("section", "dp", None), P("section", "dp", None), P("section", None, "dp")),
        check_vma=False,
    )
```
